256 devices in a mesh: op: 64 (over y, z, core), wf: 4 (over x).
Axes of the slice: x: 4, y: 4, z: 8, core: 2. Of those that a mesh axis runs over, the one named last changes fastest.
Arguments:
- guess: float32 [16, 128, 128], P('wf'), may hold values from -6 to 6
- left_ops: bfloat16 [1024, 16, 128, 128], P('op', 'wf'), may hold values from -1 to 1
- right_ops: bfloat16 [1024, 16, 128, 128], P('op', 'wf'), may hold values from -1 to 1
- op_shift: int32 [1024], P('op'), may hold values from -2 to 2
- op_mask: int32 [1024, 16], P('op', 'wf'), may hold values 0 or 1
- left_dims: int32 [16], replicated, may hold values from 1 to 128, 1984 in all
- right_dims: int32 [16], replicated, may hold values from 1 to 128, 1984 in all
Outputs:
- ritz_vector: float32 [16, 128, 128], P('wf')
- energies: float32 [2], replicated
The draws below stay inside these ranges and needn't reach their ends.
Inputs may be any that keep to these rules, and one draw needn't show every extreme that they name: `left_dims`: left sector dimensions sum to 1984 and the largest is exactly 128. `right_dims`: right sector dimensions sum to 1984 and the largest is exactly 128.
All inputs are finite; a program needn't handle non-finite values. No bound on the sum of `op_mask` on one device may be relied on, other than what follows from the above.
Results may differ from the reference program's by a relative error of at most 0.004.
Values may be sent and summed in bfloat16 or wider, within the bound.
No kernel may reach another device: no remote copies, remote signals or barrier semaphores. Data moves between devices by JAX's collectives and lax.ppermute only.
A program may use at most 64 MiB of HBM per device.

```python
import math
import jax
import jax.numpy as jnp
import numpy as np
from jax import lax

BOND = 2048
SECTORS = 16
BLOCK = 128
OPERATORS = 1024
ITERS = 2


def shared_shift(key):
    shift_key = jax.random.fold_in(key, 7)
    return jax.random.randint(shift_key, (OPERATORS,), -2, 3, dtype=jnp.int32)


def draw_op_shift(key, part):
    return shared_shift(key)


def draw_left_ops(key, part):
    shift = shared_shift(key)
    key = jax.random.fold_in(key, 21)
    noise_key, profile_key, gain_key = jax.random.split(key, 3)
    spread = BLOCK ** (-0.5)
    shape = (OPERATORS, SECTORS, BLOCK, BLOCK)
    noise = jnp.clip(jax.random.normal(noise_key, shape, jnp.float32), -3.0, 3.0) * spread
    profile = jnp.exp(jax.random.uniform(profile_key, (SECTORS, BLOCK), jnp.float32, math.log(0.6), math.log(2.0)))
    gains = jax.random.uniform(gain_key, (OPERATORS,), jnp.float32, 0.5, 1.5)
    on_diag = jnp.where(shift == 0, 0.4, 0.0).astype(jnp.float32) * gains
    diagonal = on_diag[:, None, None] * profile[None, :, :]
    identity = jnp.eye(BLOCK, dtype=jnp.float32)
    full = noise + diagonal[:, :, :, None] * identity[None, None, :, :]
    return jnp.clip(full, -1.0, 1.0).astype(jnp.bfloat16)


def draw_right_ops(key, part):
    shift = shared_shift(key)
    key = jax.random.fold_in(key, 22)
    noise_key, profile_key, gain_key = jax.random.split(key, 3)
    spread = (2.0 * BLOCK * OPERATORS) ** (-0.5)
    shape = (OPERATORS, SECTORS, BLOCK, BLOCK)
    noise = jnp.clip(jax.random.normal(noise_key, shape, jnp.float32), -3.0, 3.0) * spread
    profile = jnp.exp(jax.random.uniform(profile_key, (SECTORS, BLOCK), jnp.float32, math.log(0.6), math.log(2.0)))
    gains = jax.random.uniform(gain_key, (OPERATORS,), jnp.float32, 0.5, 1.5)
    on_diag = jnp.where(shift == 0, 10.0 / OPERATORS, 0.0).astype(jnp.float32) * gains
    diagonal = on_diag[:, None, None] * profile[None, :, :]
    identity = jnp.eye(BLOCK, dtype=jnp.float32)
    full = noise + diagonal[:, :, :, None] * identity[None, None, :, :]
    return jnp.clip(full, -1.0, 1.0).astype(jnp.bfloat16)


def touch_ends(values, own_key, smallest, largest):
    index_at = [jax.random.randint(jax.random.fold_in(own_key, axis), (), 0, length) for axis, length in enumerate(values.shape)]
    main_axis = values.shape.index(max(values.shape))
    next_to = index_at[:main_axis] + [(index_at[main_axis] + 1) % values.shape[main_axis]] + index_at[main_axis + 1:]
    return values.at[tuple(index_at)].set(smallest).at[tuple(next_to)].set(largest)


def steps_of(stream_key, extent, cuts, low, high):
    def one(position, blocks):
        heights = jax.random.uniform(jax.random.fold_in(jax.random.fold_in(stream_key, 6), position), (blocks,), jnp.float32, low / len(cuts), high / len(cuts))
        return jnp.repeat(jnp.exp(heights), extent[position] // blocks).reshape((-1,) + (1,) * (len(extent) - position - 1))

    loudness = one(*cuts[0])
    for cut in cuts[1:]:
        loudness = loudness * one(*cut)
    return loudness


def length_profile(count, total, reach, skew):
    loads = [(1 << 20) // math.isqrt(standing ** skew) + 1 for standing in range(2, count + 1)]
    surplus, holding = total - reach - (count - 1), [1] * (count - 1)
    while surplus > 0:
        candidates = [i for i in range(count - 1) if holding[i] < reach]
        whole, budget = sum([loads[i] for i in candidates]), surplus
        for i in candidates:
            extra = min(reach - holding[i], max(1, budget * loads[i] // whole), surplus)
            holding[i] = holding[i] + extra
            surplus = surplus - extra
    return np.array([reach] + holding)


def uneven(own_key, count, total, most, lean):
    if count == 2:
        one = jax.random.randint(own_key, (), max(1, total - most), min(most, total - 1) + 1)
        return jnp.stack([one, total - one])
    tallies = jnp.asarray(length_profile(count, total, most, lean), jnp.int32)
    couples = (count - 1) // 2
    donor, receiver = tallies[1:1 + 2 * couples:2], tallies[2:2 + 2 * couples:2]
    slack = jnp.minimum(donor - 1, most - receiver)
    shifted = jax.random.randint(jax.random.fold_in(own_key, 1), (couples,), 0, 1 << 20) % (slack + 1)
    tallies = tallies.at[1:1 + 2 * couples:2].set(donor - shifted).at[2:2 + 2 * couples:2].set(receiver + shifted)
    return tallies[jax.random.permutation(jax.random.fold_in(own_key, 2), count)]


def scatter_about(own_key, dims, scale, most, shards=(), held_as=jnp.bfloat16):
    array = scale * jax.random.normal(own_key, dims, jnp.float32)
    if shards:
        array = array * steps_of(own_key, dims, shards, -0.22, 0.18)
    return jnp.clip(array, -most, most).astype(held_as)


def setup_inputs(seed: int = 0) -> dict:
    key_list = jax.random.split(jax.random.key(seed), 8)
    return {
        "guess": scatter_about(key_list[0], (SECTORS, BLOCK, BLOCK), 1.0, 6.0, ((0, 4),), jnp.float32),
        "left_ops": draw_left_ops(jax.random.fold_in(key_list[7], 71), 0),
        "right_ops": draw_right_ops(jax.random.fold_in(key_list[7], 71), 0),
        "op_shift": draw_op_shift(jax.random.fold_in(key_list[7], 71), 0),
        "op_mask": touch_ends((jax.random.randint(key_list[4], (OPERATORS, SECTORS), 0, 4) < 3).astype(jnp.int32), jax.random.fold_in(key_list[4], 1), 0, 1),
        "left_dims": uneven(key_list[5], SECTORS, BOND - BOND // 32, BLOCK, 1).astype(jnp.int32),
        "right_dims": uneven(key_list[6], SECTORS, BOND - BOND // 32, BLOCK, 1).astype(jnp.int32),
    }


EPS = 1e-06
HIGH = lax.Precision.HIGHEST

def sector_mask(left_dims, right_dims):
    states = jnp.arange(BLOCK, dtype=jnp.int32)
    left_live = states[None, :] < left_dims[:, None]
    right_live = states[None, :] < right_dims[::-1][:, None]
    return (left_live[:, :, None] & right_live[:, None, :]).astype(jnp.float32)

def apply_hamiltonian(vector, left_ops, right_ops, op_shift, op_mask, live_mask):
    vec_half = vector.astype(jnp.bfloat16)
    padded = jnp.pad(vec_half, ((2, 2), (0, 0), (0, 0)))
    vec_wide = vec_half.astype(jnp.float32)

    def one_operator(accumulated, operator_slice):
        left_block, right_block, shift_value, block_live = operator_slice
        left_wide = left_block.astype(jnp.float32)
        right_wide = right_block.astype(jnp.float32)
        weight_live = block_live.astype(jnp.float32)[:, None, None]
        middle = jnp.einsum('sab,sbc->sac', left_wide, vec_wide, precision=HIGH).astype(jnp.bfloat16)
        middle = lax.optimization_barrier(middle).astype(jnp.float32)
        forward = jnp.einsum('sac,sdc->sad', middle, right_wide, precision=HIGH) * weight_live
        start = (shift_value + 2).astype(jnp.int32)
        source = lax.dynamic_slice_in_dim(padded, start, SECTORS, 0).astype(jnp.float32)
        back_middle = jnp.einsum('sba,sbc->sac', left_wide, source, precision=HIGH).astype(jnp.bfloat16)
        back_middle = lax.optimization_barrier(back_middle).astype(jnp.float32)
        adjoint = jnp.einsum('sac,scd->sad', back_middle, right_wide, precision=HIGH) * weight_live
        accumulated = accumulated.at[2:2 + SECTORS].add(adjoint)
        current = lax.dynamic_slice_in_dim(accumulated, start, SECTORS, 0)
        accumulated = lax.dynamic_update_slice_in_dim(accumulated, current + forward, start, 0)
        return (accumulated, None)
    zeros_init = jnp.zeros((SECTORS + 4, BLOCK, BLOCK), jnp.float32)
    summed, _ = lax.scan(one_operator, zeros_init, (left_ops, right_ops, op_shift, op_mask))
    return summed[2:2 + SECTORS] * live_mask

def reference(guess, left_ops, right_ops, op_shift, op_mask, left_dims, right_dims):
    live_mask = sector_mask(left_dims, right_dims)
    entries = float(SECTORS * BLOCK * BLOCK)

    def inner(first_vec, second_vec):
        return jnp.sum(first_vec * second_vec) / entries

    def hamiltonian(vector):
        return apply_hamiltonian(vector, left_ops, right_ops, op_shift, op_mask, live_mask)
    start_vec = guess * live_mask
    vector = start_vec / jnp.sqrt(inner(start_vec, start_vec) + EPS)
    image = hamiltonian(vector)
    lowest_list = []
    for turn_index in range(ITERS):
        ritz_value = inner(vector, image)
        residual = image - ritz_value * vector
        res_norm = inner(residual, residual)
        direction = residual / jnp.sqrt(res_norm + EPS)
        turned = hamiltonian(direction)
        curvature = inner(direction, turned)
        lowest = 0.5 * (ritz_value + curvature) - jnp.sqrt(0.25 * (ritz_value - curvature) * (ritz_value - curvature) + res_norm)
        keep_old = curvature - lowest
        take_new = -jnp.sqrt(res_norm)
        scaler = jnp.sqrt(keep_old * keep_old + take_new * take_new)
        vector = (keep_old * vector + take_new * direction) / scaler
        image = (keep_old * image + take_new * turned) / scaler
        lowest_list.append(lowest)
    return (vector, jnp.stack(lowest_list).astype(jnp.float32))
```

```python
import jax
import jax.numpy as jnp
from jax import lax
from jax.experimental import pallas as pl
from jax.experimental.pallas import tpu as pltpu
from jax.sharding import Mesh, PartitionSpec as P

EPS = 1e-06
SECTORS = 16
BLOCK = 128
PAIRS = 16
OWN = 4
WINDOW = 8
PLANE = 32
CHUNK = 32
EXTRA = 8
ENTRIES = float(SECTORS * BLOCK * BLOCK)
PLANE_AXES = ("y", "z")
CROSS_AXES = ("c", "wf")
OP_AXES = ("y", "z", "c")

f32 = jnp.float32
bf16 = jnp.bfloat16


def dot(first, second, first_dim=1, second_dim=0):
    return lax.dot_general(
        first, second, (((first_dim,), (second_dim,)), ((), ())), preferred_element_type=f32
    )


def total(values):
    return jnp.sum(values, axis=(0, 1), keepdims=True)


def ratio(top, bottom):
    return jnp.where(bottom > 0, top / jnp.where(bottom > 0, bottom, 1.0), 0.0)


def sector_at(wf, position):
    base = OWN * wf - 2
    return base + ((position - base) & 7)


def live(left_dims, right_dims, sector, first_row, rows):
    held = jnp.clip(sector, 0, SECTORS - 1)
    inside = (sector >= 0) & (sector < SECTORS)
    height = jnp.where(inside, left_dims[held], 0)
    width = right_dims[SECTORS - 1 - held]
    row = lax.broadcasted_iota(jnp.int32, (rows, BLOCK), 0) + first_row
    column = lax.broadcasted_iota(jnp.int32, (rows, BLOCK), 1)
    return (row < height) & (column < width)


def pack(values):
    lane = lax.broadcasted_iota(jnp.int32, (EXTRA, BLOCK), 1)
    packed = jnp.zeros((EXTRA, BLOCK), f32)
    for place, value in enumerate(values):
        packed = jnp.where(lane == place, value, packed)
    return packed


def lanes(rows, count):
    return [rows[:, place : place + 1] for place in range(count)]


def norm_kernel(ids, left_dims, right_dims, guess, out):
    wf, chunk = ids[0], ids[1]
    sums = jnp.zeros((1, 1), f32)
    for i in range(OWN):
        mask = live(left_dims, right_dims, OWN * wf + i, 0, BLOCK)
        block = jnp.where(mask, guess[i], 0.0)
        sums = sums + total(block * block)
    out[0:EXTRA] = jnp.broadcast_to(sums, (EXTRA, BLOCK))
    block, first_row = (chunk // 4) & 3, pl.multiple_of((chunk & 3) * CHUNK, CHUNK)
    mask = live(left_dims, right_dims, OWN * wf + block, first_row, CHUNK)
    out[EXTRA:] = jnp.where(mask, guess[block, pl.ds(first_row, CHUNK)], 0.0)


def half_step(ids, shift, mask, left, right, vec_half, back, sector, index):
    for k in range(PAIRS):
        position = (sector + shift[k]) & 7
        weight = mask[k * OWN + index].astype(f32)
        value = dot(left[k, 0].T, vec_half[position])
        back[:, k * BLOCK : (k + 1) * BLOCK] = (value * weight).astype(bf16)
    return dot(back[...], right[:, 0].reshape(PAIRS * BLOCK, BLOCK))


def full_step(ids, shift, mask, left, right, vec_half, back, out):
    index = pl.program_id(0)
    sector = OWN * ids[0] + index
    middle = dot(left[:, 0].reshape(PAIRS * BLOCK, BLOCK), vec_half[sector & 7])
    for k in range(PAIRS):
        position = (sector + shift[k]) & 7
        weight = mask[k * OWN + index].astype(f32)
        term = (middle[k * BLOCK : (k + 1) * BLOCK] * weight).astype(bf16)
        out[position] += dot(term, right[k, 0], 1, 1)
    out[sector & 7] += half_step(ids, shift, mask, left, right, vec_half, back, sector, index)


def first_kernel(
    ids, left_dims, right_dims, shift, mask, guess, side_one, side_three, own, one, two, three,
    left, right, out, vector, pieces, vec_half, back,
):
    wf, chunk = ids[0], ids[1]

    @pl.when(pl.program_id(0) == 0)
    def _():
        sums = (own[0:1, 0:1] + one[0:1, 0:1]) + (two[0:1, 0:1] + three[0:1, 0:1])
        scale = 1.0 / jnp.sqrt(sums / ENTRIES + EPS)

        def put(position, block):
            alive = live(left_dims, right_dims, sector_at(wf, position), 0, BLOCK)
            value = jnp.where(alive, block, 0.0) * scale
            vector[position] = value
            vec_half[position] = value.astype(bf16)

        odd = wf & 1
        for i in range(OWN):
            put(4 * odd + i, guess[i])
        for i in range(2):
            put(4 - 2 * odd + i, side_one[i])
            put(6 - 6 * odd + i, side_three[i])
        held = [own[EXTRA:], one[EXTRA:], two[EXTRA:], three[EXTRA:]]
        for place in range(2):
            source = (chunk // 16 + 2 * place) ^ wf
            value = held[0]
            for other in range(1, 4):
                value = jnp.where(source == other, held[other], value)
            pieces[place] = value * scale
        out[...] = jnp.zeros_like(out)

    full_step(ids, shift, mask, left, right, vec_half, back, out)


def spread_kernel(parts, out):
    summed = jnp.sum(parts[...], axis=0)
    for target in range(out.shape[0]):
        out[target] = summed


def combined(ids, left_dims, right_dims, parts):
    chunk = ids[1]
    position, first_row = chunk // 4, (chunk & 3) * CHUNK
    values = []
    for place in range(2):
        sector = position + 8 * place
        value = jnp.zeros((CHUNK, BLOCK), f32)
        for wf in range(4):
            here = sector_at(wf, position) == sector
            value = value + jnp.where(here, parts[wf] + parts[4 + wf], 0.0)
        values.append(jnp.where(live(left_dims, right_dims, sector, first_row, CHUNK), value, 0.0))
    return values


def send(ids, values, sums, out):
    position = ids[1] // 4
    sector = sector_at(ids[0], position)
    chosen = jnp.where(sector == position, values[0], 0.0)
    chosen = jnp.where(sector == position + 8, values[1], chosen)
    packed = pack(sums)
    for target in range(PLANE):
        out[target, 0:CHUNK] = chosen
        out[target, CHUNK:] = packed


def image_kernel(ids, left_dims, right_dims, parts, pieces, out, image_pieces):
    image = combined(ids, left_dims, right_dims, parts)
    vec = [pieces[0], pieces[1]]

    def inner(first, second):
        return total(first[0] * second[0] + first[1] * second[1])

    vec_vec, vec_image = inner(vec, vec), inner(vec, image)
    part = ratio(vec_image, vec_vec)
    rest = [image[i] - part * vec[i] for i in range(2)]
    for i in range(2):
        image_pieces[i] = image[i]
    send(ids, image, [vec_image, vec_vec, part, inner(rest, rest)], out)


def second_kernel(
    ids, shift, mask, gathered, vector, left, right, out, direction, image, scalars, vec_half, back
):
    @pl.when(pl.program_id(0) == 0)
    def _():
        vec_image, vec_vec, part, rest = lanes(gathered[:, CHUNK, :], 4)
        ritz = total(vec_image) / ENTRIES
        apart = ritz - part
        norm = total(rest + apart * apart * vec_vec) / ENTRIES
        scale = 1.0 / jnp.sqrt(norm + EPS)
        scalars[...] = pack([ritz, norm])
        for position in range(WINDOW):
            held = gathered[4 * position : 4 * position + 4, 0:CHUNK, :].reshape(BLOCK, BLOCK)
            value = (held - ritz * vector[position]) * scale
            image[position] = held
            direction[position] = value
            vec_half[position] = value.astype(bf16)
        out[...] = jnp.zeros_like(out)

    full_step(ids, shift, mask, left, right, vec_half, back, out)


def turned_kernel(ids, left_dims, right_dims, parts, pieces, image_pieces, scalars, out):
    turned = combined(ids, left_dims, right_dims, parts)
    ritz, norm = scalars[0:1, 0:1], scalars[0:1, 1:2]
    scale = 1.0 / jnp.sqrt(norm + EPS)
    vec = [pieces[i] for i in range(2)]
    image = [image_pieces[i] for i in range(2)]
    turn = [(image[i] - ritz * vec[i]) * scale for i in range(2)]

    def inner(first, second):
        return total(first[0] * second[0] + first[1] * second[1])

    vec_vec, vec_turned = inner(vec, vec), inner(vec, turned)
    along = ratio(inner(vec, turn), vec_vec)
    new = [turn[i] - along * vec[i] for i in range(2)]
    on_vec = ratio(vec_turned, vec_vec)
    rest = [turned[i] - on_vec * vec[i] for i in range(2)]
    new_new = inner(new, new)
    on_new = ratio(inner(new, rest), new_new)
    rest = [rest[i] - on_new * new[i] for i in range(2)]
    sums = [
        vec_turned, inner(turn, image), inner(turn, turned),
        vec_vec, along, on_vec, new_new, on_new, inner(rest, rest),
    ]
    send(ids, turned, sums, out)


def mixing(ritz, curvature, norm):
    gap = ritz - curvature
    lowest = 0.5 * (ritz + curvature) - jnp.sqrt(0.25 * gap * gap + norm)
    keep = curvature - lowest
    take = -jnp.sqrt(norm)
    scale = jnp.sqrt(keep * keep + take * take)
    return lowest, keep / scale, take / scale


def third_kernel(
    ids, shift, mask, gathered, vector, direction, image, scalars, left, right,
    out, new_vector, new_direction, new_scalars, vec_half, own, back, sums,
):
    index = pl.program_id(0)
    wf = ids[0]

    @pl.when(index == 0)
    def _():
        (
            vec_turned, turn_image, turn_turned, vec_vec, along, on_vec, new_new, on_new, rest,
        ) = lanes(gathered[:, CHUNK, :], 9)
        ritz, norm = scalars[0:1, 0:1], scalars[0:1, 1:2]
        curvature = total(turn_turned) / ENTRIES
        lowest, keep, take = mixing(ritz, curvature, norm)
        mixed = (total(vec_turned) + total(turn_image)) / ENTRIES
        next_ritz = keep * keep * ritz + keep * take * mixed + take * take * curvature
        first = keep * (ritz - next_ritz)
        second = keep * jnp.sqrt(norm + EPS) - take * next_ritz
        on_first = first + second * along + take * on_vec
        on_second = second + take * on_new
        squares = on_first * on_first * vec_vec + on_second * on_second * new_new
        next_norm = total(squares + take * take * rest) / ENTRIES
        scale = 1.0 / jnp.sqrt(next_norm + EPS)
        new_scalars[...] = pack([next_ritz, next_norm, lowest])
        for position in range(WINDOW):
            turned = gathered[4 * position : 4 * position + 4, 0:CHUNK, :].reshape(BLOCK, BLOCK)
            mixed_vec = keep * vector[position] + take * direction[position]
            mixed_image = keep * image[position] + take * turned
            value = (mixed_image - next_ritz * mixed_vec) * scale
            vec_half[position] = value.astype(bf16)
            own[position] = value
            new_vector_here = mixed_vec

            @pl.when((position // 4) == (wf & 1))
            def _():
                new_vector[position % 4] = new_vector_here
                new_direction[position % 4] = value

        sums[...] = jnp.zeros_like(sums)

    sector = OWN * wf + index
    image_half = half_step(ids, shift, mask, left, right, vec_half, back, sector, index)
    sums[...] += image_half * own[sector & 7]

    @pl.when(index == OWN - 1)
    def _():
        value = jnp.broadcast_to(2.0 * total(sums[...]), (EXTRA, BLOCK))
        for target in range(out.shape[0]):
            out[target] = value


def last_kernel(parts, vector, direction, scalars, out, energies):
    curvature = total(jnp.sum(parts[...], axis=0)[0:1, 0:1]) / ENTRIES
    ritz, norm, first_lowest = lanes(scalars[0:1], 3)
    lowest, keep, take = mixing(ritz, curvature, norm)
    for i in range(OWN):
        out[i] = keep * vector[i] + take * direction[i]
    energies[...] = pack([first_lowest, lowest])


SCALAR = pl.BlockSpec(memory_space=pltpu.SMEM)


def whole(*shape):
    return pl.BlockSpec(shape, lambda *_: (0,) * len(shape))


def struct(*shape):
    return jax.ShapeDtypeStruct(shape, f32)


def small(kernel, name, outs, scalars, *arrays):
    return pl.pallas_call(
        kernel,
        name=name,
        in_specs=[SCALAR] * len(scalars) + [pl.BlockSpec(memory_space=pltpu.VMEM)] * len(arrays),
        out_specs=[pl.BlockSpec(memory_space=pltpu.VMEM)] * len(outs),
        out_shape=outs,
    )(*scalars, *arrays)


def step(kernel, name, outs, scratch, scalars, arrays, operators):
    operator_spec = pl.BlockSpec((PAIRS, 1, BLOCK, BLOCK), lambda i: (0, i, 0, 0))
    return pl.pallas_call(
        kernel,
        name=name,
        grid=(OWN,),
        in_specs=[SCALAR] * len(scalars)
        + [whole(*array.shape) for array in arrays]
        + [operator_spec] * 2,
        out_specs=[whole(*out.shape) for out in outs],
        out_shape=outs,
        scratch_shapes=[pltpu.VMEM((WINDOW, BLOCK, BLOCK), bf16)]
        + scratch[:1]
        + [pltpu.VMEM((BLOCK, PAIRS * BLOCK), bf16)]
        + scratch[1:],
        compiler_params=pltpu.CompilerParams(
            dimension_semantics=("arbitrary",), vmem_limit_bytes=32 << 20
        ),
    )(*scalars, *arrays, *operators)


def exchange(value, axes):
    return lax.all_to_all(value, axes, 0, 0, tiled=True)


def shards(guess, left_ops, right_ops, op_shift, op_mask, left_dims, right_dims):
    wf = lax.axis_index("wf")
    chunk = lax.axis_index("y") * lax.axis_size("z") + lax.axis_index("z")
    ids = jnp.stack([wf, chunk]).astype(jnp.int32)
    mask = op_mask.reshape(-1)
    operators = (left_ops, right_ops)
    dims = (left_dims, right_dims)
    blocks = struct(WINDOW, BLOCK, BLOCK)

    def partner(distance):
        return [(i, i ^ distance) for i in range(4)]

    odd = wf & 1
    side_one = lax.dynamic_slice_in_dim(guess, 2 - 2 * odd, 2, 0)
    side_three = lax.dynamic_slice_in_dim(guess, 2 * odd, 2, 0)
    side_one = lax.ppermute(side_one, "wf", partner(1))
    side_three = lax.ppermute(side_three, "wf", partner(3))
    (own,) = small(norm_kernel, "norm", [struct(EXTRA + CHUNK, BLOCK)], (ids, *dims), guess)
    others = [lax.ppermute(own, "wf", partner(distance)) for distance in (1, 2, 3)]

    def reduced(partial):
        parts = exchange(partial.reshape(PLANE, CHUNK, BLOCK), PLANE_AXES)
        (tiled,) = small(spread_kernel, "spread", [struct(8, CHUNK, BLOCK)], (), parts)
        return exchange(tiled, CROSS_AXES)

    partial, vector, pieces = step(
        first_kernel, "first", [blocks, blocks, struct(2, CHUNK, BLOCK)], [],
        (ids, *dims, op_shift, mask),
        (guess, side_one, side_three, own, *others), operators,
    )
    packet = struct(PLANE, CHUNK + EXTRA, BLOCK)
    packets, image_pieces = small(
        image_kernel, "image", [packet, struct(2, CHUNK, BLOCK)], (ids, *dims),
        reduced(partial), pieces,
    )
    gathered = exchange(packets, PLANE_AXES)
    partial, direction, image, scalars = step(
        second_kernel, "second", [blocks, blocks, blocks, struct(EXTRA, BLOCK)], [],
        (ids, op_shift, mask), (gathered, vector), operators,
    )
    (packets,) = small(
        turned_kernel, "turned", [packet], (ids, *dims),
        reduced(partial), pieces, image_pieces, scalars,
    )
    gathered = exchange(packets, PLANE_AXES)
    own_blocks = struct(OWN, BLOCK, BLOCK)
    sums, vector, direction, scalars = step(
        third_kernel, "third",
        [struct(8, EXTRA, BLOCK), own_blocks, own_blocks, struct(EXTRA, BLOCK)],
        [pltpu.VMEM((WINDOW, BLOCK, BLOCK), f32), pltpu.VMEM((BLOCK, BLOCK), f32)],
        (ids, op_shift, mask), (gathered, vector, direction, image, scalars), operators,
    )
    sums = exchange(sums, CROSS_AXES)
    (sums,) = small(spread_kernel, "sums", [struct(PLANE, EXTRA, BLOCK)], (), sums)
    sums = exchange(sums, PLANE_AXES)
    result, energies = small(
        last_kernel, "last", [own_blocks, struct(EXTRA, BLOCK)], (),
        sums, vector, direction, scalars,
    )
    return result, energies[0, 0:2]


def solution(mesh):
    split = Mesh(mesh.devices.reshape(4, 8, 2, 4), (*OP_AXES, "wf"))
    in_specs = (
        P("wf", None, None),
        P(OP_AXES, "wf", None, None),
        P(OP_AXES, "wf", None, None),
        P(OP_AXES),
        P(OP_AXES, "wf"),
        P(),
        P(),
    )
    out_specs = (P("wf", None, None), P())
    return jax.shard_map(
        shards, mesh=split, in_specs=in_specs, out_specs=out_specs, check_vma=False
    )
```

```python
import jax
import jax.numpy as jnp
from jax import lax
from jax.experimental import pallas as pl
from jax.experimental.pallas import tpu as pltpu
from jax.sharding import Mesh, PartitionSpec as P

EPS = 1e-06
SECTORS = 16
BLOCK = 128
PAIRS = 16
OWN = 4
WINDOW = 8
PLANE = 32
CHUNK = 32
EXTRA = 8
ENTRIES = float(SECTORS * BLOCK * BLOCK)
PLANE_AXES = ("y", "z")
CROSS_AXES = ("c", "wf")
OP_AXES = ("y", "z", "c")

f32 = jnp.float32
bf16 = jnp.bfloat16


def dot(first, second, first_dim=1, second_dim=0):
    return lax.dot_general(
        first, second, (((first_dim,), (second_dim,)), ((), ())), preferred_element_type=f32
    )


def total(values):
    return jnp.sum(values, axis=(0, 1), keepdims=True)


def ratio(top, bottom):
    return jnp.where(bottom > 0, top / jnp.where(bottom > 0, bottom, 1.0), 0.0)


def place_here():
    return lax.axis_index("wf"), lax.axis_index("y") * lax.axis_size("z") + lax.axis_index("z")


def sector_at(wf, position):
    base = OWN * wf - 2
    return base + ((position - base) & 7)


def live(left_dims, right_dims, sector, first_row, rows):
    held = jnp.clip(sector, 0, SECTORS - 1)
    inside = (sector >= 0) & (sector < SECTORS)
    height = jnp.where(inside, left_dims[held], 0)
    width = right_dims[SECTORS - 1 - held]
    row = lax.broadcasted_iota(jnp.int32, (rows, BLOCK), 0) + first_row
    column = lax.broadcasted_iota(jnp.int32, (rows, BLOCK), 1)
    return (row < height) & (column < width)


def pack(values):
    lane = lax.broadcasted_iota(jnp.int32, (EXTRA, BLOCK), 1)
    packed = jnp.zeros((EXTRA, BLOCK), f32)
    for place, value in enumerate(values):
        packed = jnp.where(lane == place, value, packed)
    return packed


def lanes(rows, count):
    return [rows[:, place : place + 1] for place in range(count)]


def fetch(pairs, sems):
    copies = [
        pltpu.make_async_copy(source, target, sems.at[place])
        for place, (source, target) in enumerate(pairs)
    ]
    for copy in copies:
        copy.start()
    return copies


def norm_kernel(left_dims_hbm, right_dims_hbm, guess, out, side_one, side_three, *scratch):
    left_dims, right_dims, sems = scratch
    wf, chunk = place_here()
    copies = fetch([(left_dims_hbm, left_dims), (right_dims_hbm, right_dims)], sems)
    odd = wf & 1
    for i in range(2):
        side_one[i] = guess[2 - 2 * odd + i]
        side_three[i] = guess[2 * odd + i]
    for copy in copies:
        copy.wait()
    sums = jnp.zeros((1, 1), f32)
    for i in range(OWN):
        mask = live(left_dims, right_dims, OWN * wf + i, 0, BLOCK)
        block = jnp.where(mask, guess[i], 0.0)
        sums = sums + total(block * block)
    block, first_row = (chunk // 4) & 3, pl.multiple_of((chunk & 3) * CHUNK, CHUNK)
    mask = live(left_dims, right_dims, OWN * wf + block, first_row, CHUNK)
    out[0:EXTRA] = jnp.broadcast_to(sums, (EXTRA, BLOCK))
    out[EXTRA:] = jnp.where(mask, guess[block, pl.ds(first_row, CHUNK)], 0.0)


def half_step(shift, mask, left, right, vec_half, back, sector, index):
    for k in range(PAIRS):
        position = (sector + shift[k]) & 7
        weight = mask[k, index].astype(f32)
        value = dot(left[index, k].T, vec_half[position])
        back[:, k * BLOCK : (k + 1) * BLOCK] = (value * weight).astype(bf16)
    return dot(back[...], right[index].reshape(PAIRS * BLOCK, BLOCK))


def full_step(shift, mask, left, right, vec_half, back, out, sector, index):
    middle = dot(left[index].reshape(PAIRS * BLOCK, BLOCK), vec_half[sector & 7])
    for k in range(PAIRS):
        position = (sector + shift[k]) & 7
        weight = mask[k, index].astype(f32)
        term = (middle[k * BLOCK : (k + 1) * BLOCK] * weight).astype(bf16)
        out[position] += dot(term, right[index, k], 1, 1)
    out[sector & 7] += half_step(shift, mask, left, right, vec_half, back, sector, index)


def start_operators(hbm, held, sems, ints):
    pairs = [(source, target) for source, target in ints]
    for i in range(OWN):
        for source, target in zip(hbm, held):
            pairs.append((source.at[:, i], target.at[i]))
    copies = fetch(pairs, sems)
    return copies[: len(ints)], copies[len(ints) :]


def sweep(copies, body):
    for i in range(OWN):
        for copy in copies[2 * i : 2 * i + 2]:
            copy.wait()
        body(i)


def first_kernel(
    left_hbm, right_hbm, shift_hbm, mask_hbm, left_dims_hbm, right_dims_hbm,
    guess, side_one, side_three, own, one, two, three, out, vector, pieces,
    left, right, shift, mask, sems, vec_half, back, left_dims, right_dims,
):
    ints = [
        (left_dims_hbm, left_dims), (right_dims_hbm, right_dims),
        (shift_hbm, shift), (mask_hbm, mask),
    ]
    waits, copies = start_operators((left_hbm, right_hbm), (left, right), sems, ints)
    wf, chunk = place_here()
    sums = (own[0:1, 0:1] + one[0:1, 0:1]) + (two[0:1, 0:1] + three[0:1, 0:1])
    scale = 1.0 / jnp.sqrt(sums / ENTRIES + EPS)
    for copy in waits:
        copy.wait()

    def put(position, block):
        alive = live(left_dims, right_dims, sector_at(wf, position), 0, BLOCK)
        value = jnp.where(alive, block, 0.0) * scale
        vector[position] = value
        vec_half[position] = value.astype(bf16)

    odd = wf & 1
    for i in range(OWN):
        put(4 * odd + i, guess[i])
    for i in range(2):
        put(4 - 2 * odd + i, side_one[i])
        put(6 - 6 * odd + i, side_three[i])
    held = [own[EXTRA:], one[EXTRA:], two[EXTRA:], three[EXTRA:]]
    for place in range(2):
        source = (chunk // 16 + 2 * place) ^ wf
        value = held[0]
        for other in range(1, 4):
            value = jnp.where(source == other, held[other], value)
        pieces[place] = value * scale
    out[...] = jnp.zeros_like(out)

    def body(i):
        full_step(shift, mask, left, right, vec_half, back, out, OWN * wf + i, i)

    sweep(copies, body)


def spread_kernel(parts, out):
    summed = jnp.sum(parts[...], axis=0)
    for target in range(out.shape[0]):
        out[target] = summed


def combined(left_dims, right_dims, parts):
    _, chunk = place_here()
    position, first_row = chunk // 4, (chunk & 3) * CHUNK
    values = []
    for place in range(2):
        sector = position + 8 * place
        value = jnp.zeros((CHUNK, BLOCK), f32)
        for other in range(4):
            here = sector_at(other, position) == sector
            value = value + jnp.where(here, parts[other] + parts[4 + other], 0.0)
        values.append(jnp.where(live(left_dims, right_dims, sector, first_row, CHUNK), value, 0.0))
    return values


def send(values, sums, out):
    wf, chunk = place_here()
    position = chunk // 4
    sector = sector_at(wf, position)
    chosen = jnp.where(sector == position, values[0], 0.0)
    chosen = jnp.where(sector == position + 8, values[1], chosen)
    packed = pack(sums)
    for target in range(PLANE):
        out[target, 0:CHUNK] = chosen
        out[target, CHUNK:] = packed


def image_kernel(
    left_dims_hbm, right_dims_hbm, parts, pieces, out, image_pieces, left_dims, right_dims, sems
):
    for copy in fetch([(left_dims_hbm, left_dims), (right_dims_hbm, right_dims)], sems):
        copy.wait()
    image = combined(left_dims, right_dims, parts)
    vec = [pieces[0], pieces[1]]

    def inner(first, second):
        return total(first[0] * second[0] + first[1] * second[1])

    vec_vec, vec_image = inner(vec, vec), inner(vec, image)
    part = ratio(vec_image, vec_vec)
    rest = [image[i] - part * vec[i] for i in range(2)]
    for i in range(2):
        image_pieces[i] = image[i]
    send(image, [vec_image, vec_vec, part, inner(rest, rest)], out)


def second_kernel(
    left_hbm, right_hbm, shift_hbm, mask_hbm, gathered, vector,
    out, direction, image, scalars, left, right, shift, mask, sems, vec_half, back,
):
    ints = [(shift_hbm, shift), (mask_hbm, mask)]
    waits, copies = start_operators((left_hbm, right_hbm), (left, right), sems, ints)
    wf, _ = place_here()
    vec_image, vec_vec, part, rest = lanes(gathered[:, CHUNK, :], 4)
    ritz = total(vec_image) / ENTRIES
    apart = ritz - part
    norm = total(rest + apart * apart * vec_vec) / ENTRIES
    scale = 1.0 / jnp.sqrt(norm + EPS)
    scalars[...] = pack([ritz, norm])
    for position in range(WINDOW):
        held = gathered[4 * position : 4 * position + 4, 0:CHUNK, :].reshape(BLOCK, BLOCK)
        value = (held - ritz * vector[position]) * scale
        image[position] = held
        direction[position] = value
        vec_half[position] = value.astype(bf16)
    out[...] = jnp.zeros_like(out)
    for copy in waits:
        copy.wait()

    def body(i):
        full_step(shift, mask, left, right, vec_half, back, out, OWN * wf + i, i)

    sweep(copies, body)


def turned_kernel(
    left_dims_hbm, right_dims_hbm, parts, pieces, image_pieces, scalars, out,
    left_dims, right_dims, sems,
):
    for copy in fetch([(left_dims_hbm, left_dims), (right_dims_hbm, right_dims)], sems):
        copy.wait()
    turned = combined(left_dims, right_dims, parts)
    ritz, norm = scalars[0:1, 0:1], scalars[0:1, 1:2]
    scale = 1.0 / jnp.sqrt(norm + EPS)
    vec = [pieces[i] for i in range(2)]
    image = [image_pieces[i] for i in range(2)]
    turn = [(image[i] - ritz * vec[i]) * scale for i in range(2)]

    def inner(first, second):
        return total(first[0] * second[0] + first[1] * second[1])

    vec_vec, vec_turned = inner(vec, vec), inner(vec, turned)
    along = ratio(inner(vec, turn), vec_vec)
    new = [turn[i] - along * vec[i] for i in range(2)]
    on_vec = ratio(vec_turned, vec_vec)
    rest = [turned[i] - on_vec * vec[i] for i in range(2)]
    new_new = inner(new, new)
    on_new = ratio(inner(new, rest), new_new)
    rest = [rest[i] - on_new * new[i] for i in range(2)]
    sums = [
        vec_turned, inner(turn, image), inner(turn, turned),
        vec_vec, along, on_vec, new_new, on_new, inner(rest, rest),
    ]
    send(turned, sums, out)


def mixing(ritz, curvature, norm):
    gap = ritz - curvature
    lowest = 0.5 * (ritz + curvature) - jnp.sqrt(0.25 * gap * gap + norm)
    keep = curvature - lowest
    take = -jnp.sqrt(norm)
    scale = jnp.sqrt(keep * keep + take * take)
    return lowest, keep / scale, take / scale


def third_kernel(
    left_hbm, right_hbm, shift_hbm, mask_hbm, gathered, vector, direction, image, scalars,
    out, new_vector, new_direction, new_scalars, left, right, shift, mask, sems, vec_half, back,
):
    ints = [(shift_hbm, shift), (mask_hbm, mask)]
    waits, copies = start_operators((left_hbm, right_hbm), (left, right), sems, ints)
    wf, _ = place_here()
    (
        vec_turned, turn_image, turn_turned, vec_vec, along, on_vec, new_new, on_new, rest,
    ) = lanes(gathered[:, CHUNK, :], 9)
    ritz, norm = scalars[0:1, 0:1], scalars[0:1, 1:2]
    curvature = total(turn_turned) / ENTRIES
    lowest, keep, take = mixing(ritz, curvature, norm)
    mixed = (total(vec_turned) + total(turn_image)) / ENTRIES
    next_ritz = keep * keep * ritz + keep * take * mixed + take * take * curvature
    first = keep * (ritz - next_ritz)
    second = keep * jnp.sqrt(norm + EPS) - take * next_ritz
    on_first = first + second * along + take * on_vec
    on_second = second + take * on_new
    squares = on_first * on_first * vec_vec + on_second * on_second * new_new
    next_norm = total(squares + take * take * rest) / ENTRIES
    scale = 1.0 / jnp.sqrt(next_norm + EPS)
    new_scalars[...] = pack([next_ritz, next_norm, lowest])
    for position in range(WINDOW):
        turned = gathered[4 * position : 4 * position + 4, 0:CHUNK, :].reshape(BLOCK, BLOCK)
        mixed_vec = keep * vector[position] + take * direction[position]
        mixed_image = keep * image[position] + take * turned
        value = (mixed_image - next_ritz * mixed_vec) * scale
        vec_half[position] = value.astype(bf16)

        @pl.when((position // 4) == (wf & 1))
        def _():
            new_vector[position % 4] = mixed_vec
            new_direction[position % 4] = value

    for copy in waits:
        copy.wait()
    sums = []

    def body(i):
        half = half_step(shift, mask, left, right, vec_half, back, OWN * wf + i, i)
        sums.append(total(half * new_direction[i]))

    sweep(copies, body)
    value = jnp.broadcast_to(2.0 * (sums[0] + sums[1] + sums[2] + sums[3]), out.shape)
    out[...] = value


def last_kernel(parts, vector, direction, scalars, out, energies):
    curvature = total(parts[...])[0:1] / (BLOCK * ENTRIES)
    ritz, norm, first_lowest = lanes(scalars[0:1], 3)
    lowest, keep, take = mixing(ritz, curvature, norm)
    for i in range(OWN):
        out[i] = keep * vector[i] + take * direction[i]
    energies[0] = first_lowest[0, 0]
    energies[1] = lowest[0, 0]


def sums_kernel(parts, out):
    out[...] = jnp.broadcast_to(jnp.sum(parts[...], axis=0, keepdims=True), out.shape)


HBM = pl.BlockSpec(memory_space=pltpu.HBM)
VMEM = pl.BlockSpec(memory_space=pltpu.VMEM)
SMEM = pl.BlockSpec(memory_space=pltpu.SMEM)


def struct(*shape):
    return jax.ShapeDtypeStruct(shape, f32)


def small(kernel, name, outs, dims, *arrays, out_specs=None):
    scratch = [pltpu.SMEM((SECTORS,), jnp.int32)] * 2 + [pltpu.SemaphoreType.DMA((2,))]
    return pl.pallas_call(
        kernel,
        name=name,
        in_specs=[HBM] * len(dims) + [VMEM] * len(arrays),
        out_specs=out_specs or [VMEM] * len(outs),
        out_shape=outs,
        scratch_shapes=scratch if dims else [],
        compiler_params=pltpu.CompilerParams(vmem_limit_bytes=6 << 20),
    )(*dims, *arrays)


def step(kernel, name, outs, ints, arrays, operators, extra=()):
    held = pltpu.VMEM((OWN, PAIRS, BLOCK, BLOCK), bf16)
    return pl.pallas_call(
        kernel,
        name=name,
        in_specs=[HBM] * (2 + len(ints)) + [VMEM] * len(arrays),
        out_specs=[VMEM] * len(outs),
        out_shape=outs,
        scratch_shapes=[
            held,
            held,
            pltpu.SMEM((PAIRS,), jnp.int32),
            pltpu.SMEM((PAIRS, OWN), jnp.int32),
            pltpu.SemaphoreType.DMA((len(ints) + 2 * OWN,)),
            pltpu.VMEM((WINDOW, BLOCK, BLOCK), bf16),
            pltpu.VMEM((BLOCK, PAIRS * BLOCK), bf16),
            *extra,
        ],
        compiler_params=pltpu.CompilerParams(vmem_limit_bytes=20 << 20),
    )(*operators, *ints, *arrays)


def exchange(value, axes):
    return lax.all_to_all(value, axes, 0, 0, tiled=True)


def shards(guess, left_ops, right_ops, op_shift, op_mask, left_dims, right_dims):
    operators = (left_ops, right_ops)
    dims = (left_dims, right_dims)
    ints = (op_shift, op_mask)
    blocks = struct(WINDOW, BLOCK, BLOCK)
    pair = struct(2, BLOCK, BLOCK)

    def partner(value, distance):
        return lax.ppermute(value, "wf", [(i, i ^ distance) for i in range(4)])

    own, side_one, side_three = small(
        norm_kernel, "norm", [struct(EXTRA + CHUNK, BLOCK), pair, pair], dims, guess
    )
    side_one, side_three = partner(side_one, 1), partner(side_three, 3)
    others = [partner(own, distance) for distance in (1, 2, 3)]

    def reduced(partial):
        parts = exchange(partial.reshape(PLANE, CHUNK, BLOCK), PLANE_AXES)
        (tiled,) = small(spread_kernel, "spread", [struct(8, CHUNK, BLOCK)], (), parts)
        return exchange(tiled, CROSS_AXES)

    partial, vector, pieces = step(
        first_kernel, "first", [blocks, blocks, struct(2, CHUNK, BLOCK)], (*ints, *dims),
        (guess, side_one, side_three, own, *others), operators,
        [pltpu.SMEM((SECTORS,), jnp.int32)] * 2,
    )
    packet = struct(PLANE, CHUNK + EXTRA, BLOCK)
    packets, image_pieces = small(
        image_kernel, "image", [packet, struct(2, CHUNK, BLOCK)], dims, reduced(partial), pieces
    )
    gathered = exchange(packets, PLANE_AXES)
    partial, direction, image, scalars = step(
        second_kernel, "second", [blocks, blocks, blocks, struct(EXTRA, BLOCK)], ints,
        (gathered, vector), operators,
    )
    (packets,) = small(
        turned_kernel, "turned", [packet], dims, reduced(partial), pieces, image_pieces, scalars
    )
    gathered = exchange(packets, PLANE_AXES)
    own_blocks = struct(OWN, BLOCK, BLOCK)
    sums, vector, direction, scalars = step(
        third_kernel, "third",
        [struct(8, BLOCK), own_blocks, own_blocks, struct(EXTRA, BLOCK)], ints,
        (gathered, vector, direction, image, scalars), operators,
    )
    sums = exchange(sums, CROSS_AXES)
    (sums,) = small(sums_kernel, "sums", [struct(PLANE, BLOCK)], (), sums)
    sums = exchange(sums, PLANE_AXES)
    result, energies = small(
        last_kernel, "last", [own_blocks, struct(2)], (), sums, vector, direction, scalars,
        out_specs=[VMEM, SMEM],
    )
    return result, energies


def solution(mesh):
    split = Mesh(mesh.devices.reshape(4, 8, 2, 4), (*OP_AXES, "wf"))
    in_specs = (
        P("wf", None, None),
        P(OP_AXES, "wf", None, None),
        P(OP_AXES, "wf", None, None),
        P(OP_AXES),
        P(OP_AXES, "wf"),
        P(),
        P(),
    )
    out_specs = (P("wf", None, None), P())
    return jax.shard_map(
        shards, mesh=split, in_specs=in_specs, out_specs=out_specs, check_vma=False
    )
```

```python
import jax
import jax.numpy as jnp
from jax import lax
from jax.experimental import pallas as pl
from jax.experimental.pallas import tpu as pltpu
from jax.sharding import Mesh, PartitionSpec as P

EPS = 1e-06
SECTORS = 16
BLOCK = 128
PAIRS = 16
OWN = 4
WINDOW = 8
PLANE = 32
HALF = 4
CHUNK = 16
SIDE = 2 * BLOCK
EXTRA = 8
ENTRIES = float(SECTORS * BLOCK * BLOCK)
PLANE_AXES = ("y", "z")
CROSS_AXES = ("c", "wf")
OP_AXES = ("y", "z", "c")

f32 = jnp.float32
bf16 = jnp.bfloat16


def dot(first, second, first_dim=1, second_dim=0):
    return lax.dot_general(
        first, second, (((first_dim,), (second_dim,)), ((), ())), preferred_element_type=f32
    )


def total(values):
    return jnp.sum(values, axis=(0, 1), keepdims=True)


def ratio(top, bottom):
    return jnp.where(bottom > 0, top / jnp.where(bottom > 0, bottom, 1.0), 0.0)


def place_here():
    chunk = lax.axis_index("y") * lax.axis_size("z") + lax.axis_index("z")
    first_row = pl.multiple_of((chunk & 7) * CHUNK, CHUNK)
    return lax.axis_index("wf"), HALF * lax.axis_index("c") + chunk // 8, first_row


def sector_at(wf, position):
    base = OWN * wf - 2
    return base + ((position - base) & 7)


def live(left_dims, right_dims, sector, first_row, rows):
    held = jnp.clip(sector, 0, SECTORS - 1)
    inside = (sector >= 0) & (sector < SECTORS)
    height = jnp.where(inside, left_dims[held], 0)
    width = right_dims[SECTORS - 1 - held]
    row = lax.broadcasted_iota(jnp.int32, (rows, BLOCK), 0) + first_row
    column = lax.broadcasted_iota(jnp.int32, (rows, BLOCK), 1)
    return (row < height) & (column < width)


def pack(values):
    lane = lax.broadcasted_iota(jnp.int32, (EXTRA, BLOCK), 1)
    packed = jnp.zeros((EXTRA, BLOCK), f32)
    for place, value in enumerate(values):
        packed = jnp.where(lane == place, value, packed)
    return packed


def lanes(rows, count):
    return [rows[:, place : place + 1] for place in range(count)]


def load_kernel(left_hbm, right_hbm, left, right, sems):
    copies = []
    for i in range(OWN):
        for source, target in ((left_hbm, left), (right_hbm, right)):
            copies.append(
                pltpu.make_async_copy(source.at[:, i], target.at[i], sems.at[len(copies)])
            )
    for copy in copies:
        copy.start()
    for copy in copies:
        copy.wait()


def norm_kernel(left_dims, right_dims, guess, start, masks, one, two, three):
    wf, position, first_row = place_here()
    sums = jnp.zeros((1, 1), f32)
    for i in range(OWN):
        mask = live(left_dims, right_dims, OWN * wf + i, 0, BLOCK)
        block = jnp.where(mask, guess[i], 0.0)
        start[i] = block
        sums = sums + total(block * block)
    odd = wf & 1
    for i in range(2):
        one[i * BLOCK : (i + 1) * BLOCK] = start[2 - 2 * odd + i]
        three[i * BLOCK : (i + 1) * BLOCK] = start[2 * odd + i]
    for out, first in ((one, SIDE), (two, 0), (three, SIDE)):
        out[first : first + EXTRA] = jnp.broadcast_to(sums, (EXTRA, BLOCK))
        out[first + EXTRA :] = start[position & 3, pl.ds(first_row, CHUNK)]
    for i in range(2):
        mask = live(left_dims, right_dims, position + 8 * i, first_row, CHUNK)
        masks[i] = jnp.where(mask, 1.0, 0.0)


def half_step(table, left, right, vec_half, back, sector, index):
    for k in range(PAIRS):
        entry = table[k * OWN + index]
        position = (sector + (entry >> 1)) & 7
        weight = (entry & 1).astype(f32)
        value = dot(left[index, k].T, vec_half[position])
        back[:, k * BLOCK : (k + 1) * BLOCK] = (value * weight).astype(bf16)
    return dot(back[...], right[index].reshape(PAIRS * BLOCK, BLOCK))


def full_step(table, left, right, vec_half, back, sums, sector, index):
    middle = dot(left[index].reshape(PAIRS * BLOCK, BLOCK), vec_half[sector & 7])
    for k in range(PAIRS):
        entry = table[k * OWN + index]
        position = (sector + (entry >> 1)) & 7
        weight = (entry & 1).astype(f32)
        term = (middle[k * BLOCK : (k + 1) * BLOCK] * weight).astype(bf16)
        sums[position] += dot(term, right[index, k], 1, 1)
    sums[sector & 7] += half_step(table, left, right, vec_half, back, sector, index)


def full_sweep(table, left, right, vec_half, back, sums, keep, give):
    sums[...] = jnp.zeros_like(sums)
    first_sector = OWN * lax.axis_index("wf")
    for i in range(OWN):
        full_step(table, left, right, vec_half, back, sums, first_sector + i, i)
    core = lax.axis_index("c")
    for i in range(HALF):
        keep[i] = sums[HALF * core + i]
        give[i] = sums[HALF - HALF * core + i]


def first_kernel(
    table, left, right, start, own, one, two, three, keep, give, vector, pieces,
    vec_half, back, sums,
):
    wf = lax.axis_index("wf")
    squares = (own[0:1, 0:1] + one[SIDE : SIDE + 1, 0:1]) + (
        two[0:1, 0:1] + three[SIDE : SIDE + 1, 0:1]
    )
    scale = 1.0 / jnp.sqrt(squares / ENTRIES + EPS)

    def put(position, block):
        sector = sector_at(wf, position)
        inside = (sector >= 0) & (sector < SECTORS)
        value = jnp.where(inside, block * scale, 0.0)
        vector[position] = value
        vec_half[position] = value.astype(bf16)

    odd = wf & 1
    for i in range(OWN):
        put(4 * odd + i, start[i])
    for i in range(2):
        rows = slice(i * BLOCK, (i + 1) * BLOCK)
        put(4 - 2 * odd + i, one[rows])
        put(6 - 6 * odd + i, three[rows])
    held = [own[EXTRA:], one[SIDE + EXTRA :], two[EXTRA:], three[SIDE + EXTRA :]]
    for place in range(2):
        source = (lax.axis_index("c") + 2 * place) ^ wf
        value = held[0]
        for other in range(1, 4):
            value = jnp.where(source == other, held[other], value)
        pieces[place] = value * scale
    full_sweep(table, left, right, vec_half, back, sums, keep, give)


def join_kernel(first, second, out):
    out[...] = first[...] + second[...]


def spread_kernel(parts, out):
    summed = jnp.sum(parts[...], axis=0)
    for target in range(out.shape[0]):
        out[target] = summed


def combined(masks, parts):
    _, position, _ = place_here()
    values = []
    for place in range(2):
        value = jnp.zeros((CHUNK, BLOCK), f32)
        for other in range(4):
            here = sector_at(other, position) == position + 8 * place
            value = value + jnp.where(here, parts[other], 0.0)
        values.append(value * masks[place])
    return values


def send(values, sums, out):
    wf, position, _ = place_here()
    sector = sector_at(wf, position)
    chosen = jnp.where(sector == position, values[0], 0.0)
    chosen = jnp.where(sector == position + 8, values[1], chosen)
    packed = pack(sums)
    for target in range(PLANE):
        out[target, 0:CHUNK] = chosen
        out[target, CHUNK:] = packed


def image_kernel(parts, masks, pieces, out, image_pieces):
    image = combined(masks, parts)
    vec = [pieces[0], pieces[1]]

    def inner(first, second):
        return total(first[0] * second[0] + first[1] * second[1])

    vec_vec, vec_image = inner(vec, vec), inner(vec, image)
    part = ratio(vec_image, vec_vec)
    rest = [image[i] - part * vec[i] for i in range(2)]
    for i in range(2):
        image_pieces[i] = image[i]
    send(image, [vec_image, vec_vec, part, inner(rest, rest)], out)


def both(cores, count):
    return zip(*[lanes(held[:, CHUNK, :], count) for held in cores])


def add(values):
    return total(values[0]) + total(values[1])


def held_block(cores, position):
    rows = slice(8 * (position % HALF), 8 * (position % HALF) + 8)
    own, other = (held[rows, 0:CHUNK, :].reshape(BLOCK, BLOCK) for held in cores)
    return jnp.where(lax.axis_index("c") == position // HALF, own, other)


def second_kernel(
    table, left, right, own, other, vector, keep, give, direction, image, scalars,
    vec_half, back, sums,
):
    cores = (own, other)
    vec_image, vec_vec, part, rest = both(cores, 4)
    ritz = add(vec_image) / ENTRIES
    norm = add([rest[i] + (ritz - part[i]) * (ritz - part[i]) * vec_vec[i] for i in range(2)])
    norm = norm / ENTRIES
    scale = 1.0 / jnp.sqrt(norm + EPS)
    scalars[...] = pack([ritz, norm])
    for position in range(WINDOW):
        held = held_block(cores, position)
        value = (held - ritz * vector[position]) * scale
        image[position] = held
        direction[position] = value
        vec_half[position] = value.astype(bf16)
    full_sweep(table, left, right, vec_half, back, sums, keep, give)


def turned_kernel(parts, masks, pieces, image_pieces, scalars, out):
    turned = combined(masks, parts)
    ritz, norm = scalars[0:1, 0:1], scalars[0:1, 1:2]
    scale = 1.0 / jnp.sqrt(norm + EPS)
    vec = [pieces[i] for i in range(2)]
    image = [image_pieces[i] for i in range(2)]
    turn = [(image[i] - ritz * vec[i]) * scale for i in range(2)]

    def inner(first, second):
        return total(first[0] * second[0] + first[1] * second[1])

    vec_vec, vec_turned = inner(vec, vec), inner(vec, turned)
    along = ratio(inner(vec, turn), vec_vec)
    new = [turn[i] - along * vec[i] for i in range(2)]
    on_vec = ratio(vec_turned, vec_vec)
    rest = [turned[i] - on_vec * vec[i] for i in range(2)]
    new_new = inner(new, new)
    on_new = ratio(inner(new, rest), new_new)
    rest = [rest[i] - on_new * new[i] for i in range(2)]
    sums = [
        vec_turned, inner(turn, image), inner(turn, turned),
        vec_vec, along, on_vec, new_new, on_new, inner(rest, rest),
    ]
    send(turned, sums, out)


def mixing(ritz, curvature, norm):
    gap = ritz - curvature
    lowest = 0.5 * (ritz + curvature) - jnp.sqrt(0.25 * gap * gap + norm)
    keep = curvature - lowest
    take = -jnp.sqrt(norm)
    scale = jnp.sqrt(keep * keep + take * take)
    return lowest, keep / scale, take / scale


def third_kernel(
    table, left, right, gathered, swapped, vector, direction, image, scalars,
    out, new_vector, new_direction, new_scalars, vec_half, back,
):
    cores = (gathered, swapped)
    wf = lax.axis_index("wf")
    (
        vec_turned, turn_image, turn_turned, vec_vec, along, on_vec, new_new, on_new, rest,
    ) = both(cores, 9)
    ritz, norm = scalars[0:1, 0:1], scalars[0:1, 1:2]
    curvature = add(turn_turned) / ENTRIES
    lowest, keep, take = mixing(ritz, curvature, norm)
    mixed = (add(vec_turned) + add(turn_image)) / ENTRIES
    next_ritz = keep * keep * ritz + keep * take * mixed + take * take * curvature
    first = keep * (ritz - next_ritz)
    second = keep * jnp.sqrt(norm + EPS) - take * next_ritz
    squares = []
    for i in range(2):
        on_first = first + second * along[i] + take * on_vec[i]
        on_second = second + take * on_new[i]
        square = on_first * on_first * vec_vec[i] + on_second * on_second * new_new[i]
        squares.append(square + take * take * rest[i])
    next_norm = add(squares) / ENTRIES
    scale = 1.0 / jnp.sqrt(next_norm + EPS)
    new_scalars[...] = pack([next_ritz, next_norm, lowest])
    for position in range(WINDOW):
        turned = held_block(cores, position)
        mixed_vec = keep * vector[position] + take * direction[position]
        mixed_image = keep * image[position] + take * turned
        value = (mixed_image - next_ritz * mixed_vec) * scale
        vec_half[position] = value.astype(bf16)

        @pl.when((position // 4) == (wf & 1))
        def _():
            new_vector[position % 4] = mixed_vec
            new_direction[position % 4] = value

    value = jnp.zeros((1, 1), f32)
    for i in range(OWN):
        half = half_step(table, left, right, vec_half, back, OWN * wf + i, i)
        value = value + total(half * new_direction[i])
    out[...] = jnp.broadcast_to(2.0 * value, out.shape)


def last_kernel(parts, vector, direction, scalars, out, energies):
    curvature = total(parts[...])[0:1] / (BLOCK * ENTRIES)
    ritz, norm, first_lowest = lanes(scalars[0:1], 3)
    lowest, keep, take = mixing(ritz, curvature, norm)
    for i in range(OWN):
        out[i] = keep * vector[i] + take * direction[i]
    energies[0] = first_lowest[0, 0]
    energies[1] = lowest[0, 0]


def sums_kernel(parts, out):
    out[...] = jnp.broadcast_to(jnp.sum(parts[...], axis=0, keepdims=True), out.shape)


HBM = pl.BlockSpec(memory_space=pltpu.HBM)
VMEM = pl.BlockSpec(memory_space=pltpu.VMEM)
SMEM = pl.BlockSpec(memory_space=pltpu.SMEM)
MIB = 1 << 20


def struct(*shape, dtype=f32):
    return jax.ShapeDtypeStruct(shape, dtype)


def call(kernel, name, outs, in_specs, args, out_specs=None, scratch=(), limit=6):
    return pl.pallas_call(
        kernel,
        name=name,
        in_specs=in_specs,
        out_specs=out_specs or [VMEM] * len(outs),
        out_shape=outs,
        scratch_shapes=scratch,
        compiler_params=pltpu.CompilerParams(vmem_limit_bytes=limit * MIB),
    )(*args)


def small(kernel, name, outs, *arrays, out_specs=None):
    return call(kernel, name, outs, [VMEM] * len(arrays), arrays, out_specs)


def step(kernel, name, outs, operators, arrays, sums=True):
    scratch = [
        pltpu.VMEM((WINDOW, BLOCK, BLOCK), bf16),
        pltpu.VMEM((BLOCK, PAIRS * BLOCK), bf16),
    ]
    if sums:
        scratch.append(pltpu.VMEM((WINDOW, BLOCK, BLOCK), f32))
    args = (*operators, *arrays)
    in_specs = [SMEM] + [VMEM] * (len(args) - 1)
    return call(kernel, name, outs, in_specs, args, scratch=scratch, limit=16)


def exchange(value, axes):
    return lax.all_to_all(value, axes, 0, 0, tiled=True)


def shards(guess, left_ops, right_ops, op_shift, op_mask, left_dims, right_dims):
    blocks = struct(WINDOW, BLOCK, BLOCK)
    half = struct(HALF, BLOCK, BLOCK)
    own_blocks = struct(OWN, BLOCK, BLOCK)
    pair = struct(2, CHUNK, BLOCK)
    scalar_row = struct(EXTRA, BLOCK)
    packet = struct(PLANE, CHUNK + EXTRA, BLOCK)

    def partner(value, distance):
        return lax.ppermute(value, "wf", [(i, i ^ distance) for i in range(4)])

    def swapped(value):
        return lax.ppermute(value, "c", [(0, 1), (1, 0)])

    table = (2 * op_shift[:, None] + op_mask).reshape(-1)
    tail = EXTRA + CHUNK
    start, masks, one, own, three = call(
        norm_kernel, "norm",
        [own_blocks, pair, struct(SIDE + tail, BLOCK), struct(tail, BLOCK),
         struct(SIDE + tail, BLOCK)],
        [SMEM, SMEM, VMEM], (left_dims, right_dims, guess), limit=60,
    )
    one, two, three = partner(one, 1), partner(own, 2), partner(three, 3)
    held = struct(OWN, PAIRS, BLOCK, BLOCK, dtype=bf16)
    left, right = call(
        load_kernel, "load", [held, held], [HBM, HBM], (left_ops, right_ops),
        scratch=[pltpu.SemaphoreType.DMA((2 * OWN,))], limit=58,
    )
    operators = (table, left, right)

    def reduced(keep, give):
        (summed,) = small(join_kernel, "join", [half], keep, swapped(give))
        parts = exchange(summed.reshape(PLANE, CHUNK, BLOCK), PLANE_AXES)
        (tiled,) = small(spread_kernel, "spread", [struct(4, CHUNK, BLOCK)], parts)
        return exchange(tiled, "wf")

    def gathered(packets):
        packets = exchange(packets, PLANE_AXES)
        return packets, swapped(packets)

    keep, give, vector, pieces = step(
        first_kernel, "first", [half, half, blocks, pair], operators,
        (start, own, one, two, three),
    )
    packets, image_pieces = small(
        image_kernel, "image", [packet, pair], reduced(keep, give), masks, pieces
    )
    keep, give, direction, image, scalars = step(
        second_kernel, "second", [half, half, blocks, blocks, scalar_row], operators,
        (*gathered(packets), vector),
    )
    (packets,) = small(
        turned_kernel, "turned", [packet], reduced(keep, give), masks, pieces, image_pieces, scalars
    )
    sums, vector, direction, scalars = step(
        third_kernel, "third", [struct(8, BLOCK), own_blocks, own_blocks, scalar_row], operators,
        (*gathered(packets), vector, direction, image, scalars), sums=False,
    )
    sums = exchange(sums, CROSS_AXES)
    (sums,) = small(sums_kernel, "sums", [struct(PLANE, BLOCK)], sums)
    sums = exchange(sums, PLANE_AXES)
    result, energies = small(
        last_kernel, "last", [own_blocks, struct(2)], sums, vector, direction, scalars,
        out_specs=[VMEM, SMEM],
    )
    return result, energies


def solution(mesh):
    split = Mesh(mesh.devices.reshape(4, 8, 2, 4), (*OP_AXES, "wf"))
    in_specs = (
        P("wf", None, None),
        P(OP_AXES, "wf", None, None),
        P(OP_AXES, "wf", None, None),
        P(OP_AXES),
        P(OP_AXES, "wf"),
        P(),
        P(),
    )
    out_specs = (P("wf", None, None), P())
    return jax.shard_map(
        shards, mesh=split, in_specs=in_specs, out_specs=out_specs, check_vma=False
    )
```

```python
import jax
import jax.numpy as jnp
from jax import lax
from jax.experimental import pallas as pl
from jax.experimental.pallas import tpu as pltpu
from jax.sharding import Mesh, PartitionSpec as P

EPS = 1e-06
SECTORS = 16
BLOCK = 128
PAIRS = 16
OWN = 4
WINDOW = 8
LINE = 8
CROSS = 16
HALF = 4
ROWS = 16
CHUNK = HALF * ROWS
SIDE = 2 * BLOCK
EXTRA = 8
ENTRIES = float(SECTORS * BLOCK * BLOCK)
CROSS_AXES = ("y", "wf")
OP_AXES = ("y", "z", "c")

f32 = jnp.float32
bf16 = jnp.bfloat16


def dot(first, second, first_dim=1, second_dim=0):
    return lax.dot_general(
        first, second, (((first_dim,), (second_dim,)), ((), ())), preferred_element_type=f32
    )


def total(values):
    return jnp.sum(values, axis=(0, 1), keepdims=True)


def ratio(top, bottom):
    return jnp.where(bottom > 0, top / jnp.where(bottom > 0, bottom, 1.0), 0.0)


def place_here():
    first_row = pl.multiple_of(lax.axis_index("z") * ROWS, ROWS)
    return lax.axis_index("wf"), HALF * lax.axis_index("c"), first_row


def sector_at(wf, position):
    base = OWN * wf - 2
    return base + ((position - base) & 7)


def live(left_dims, right_dims, sector, first_row, rows):
    held = jnp.clip(sector, 0, SECTORS - 1)
    inside = (sector >= 0) & (sector < SECTORS)
    height = jnp.where(inside, left_dims[held], 0)
    width = right_dims[SECTORS - 1 - held]
    row = lax.broadcasted_iota(jnp.int32, (rows, BLOCK), 0) + first_row
    column = lax.broadcasted_iota(jnp.int32, (rows, BLOCK), 1)
    return (row < height) & (column < width)


def pack(values):
    lane = lax.broadcasted_iota(jnp.int32, (EXTRA, BLOCK), 1)
    packed = jnp.zeros((EXTRA, BLOCK), f32)
    for place, value in enumerate(values):
        packed = jnp.where(lane == place, value, packed)
    return packed


def lanes(rows, count):
    return [rows[:, place : place + 1] for place in range(count)]


def load_kernel(left_hbm, right_hbm, left, right, sems):
    copies = []
    for i in range(OWN):
        for source, target in ((left_hbm, left), (right_hbm, right)):
            copies.append(
                pltpu.make_async_copy(source.at[:, i], target.at[i], sems.at[len(copies)])
            )
    for copy in copies:
        copy.start()
    for copy in copies:
        copy.wait()


def norm_kernel(left_dims, right_dims, guess, start, masks, one, two, three):
    wf, base, first_row = place_here()
    sums = jnp.zeros((1, 1), f32)
    for i in range(OWN):
        mask = live(left_dims, right_dims, OWN * wf + i, 0, BLOCK)
        block = jnp.where(mask, guess[i], 0.0)
        start[i] = block
        sums = sums + total(block * block)
    odd = wf & 1
    for i in range(2):
        one[i * BLOCK : (i + 1) * BLOCK] = start[2 - 2 * odd + i]
        three[i * BLOCK : (i + 1) * BLOCK] = start[2 * odd + i]
    for out, first in ((one, SIDE), (two, 0), (three, SIDE)):
        out[first : first + EXTRA] = jnp.broadcast_to(sums, (EXTRA, BLOCK))
        out[first + EXTRA :] = start[:, pl.ds(first_row, ROWS)].reshape(CHUNK, BLOCK)
    for i in range(2):
        for k in range(HALF):
            mask = live(left_dims, right_dims, base + k + 8 * i, first_row, ROWS)
            masks[i, k * ROWS : (k + 1) * ROWS] = jnp.where(mask, 1.0, 0.0)


def half_step(table, left, right, vec_half, back, sector, index):
    for k in range(PAIRS):
        entry = table[k * OWN + index]
        position = (sector + (entry >> 1)) & 7
        weight = (entry & 1).astype(f32)
        value = dot(left[index, k].T, vec_half[position])
        back[:, k * BLOCK : (k + 1) * BLOCK] = (value * weight).astype(bf16)
    return dot(back[...], right[index].reshape(PAIRS * BLOCK, BLOCK))


def full_step(table, left, right, vec_half, back, sums, sector, index):
    middle = dot(left[index].reshape(PAIRS * BLOCK, BLOCK), vec_half[sector & 7])
    for k in range(PAIRS):
        entry = table[k * OWN + index]
        position = (sector + (entry >> 1)) & 7
        weight = (entry & 1).astype(f32)
        term = (middle[k * BLOCK : (k + 1) * BLOCK] * weight).astype(bf16)
        sums[position] += dot(term, right[index, k], 1, 1)
    sums[sector & 7] += half_step(table, left, right, vec_half, back, sector, index)


def full_sweep(table, left, right, vec_half, back, sums, keep, give):
    sums[...] = jnp.zeros_like(sums)
    first_sector = OWN * lax.axis_index("wf")
    for i in range(OWN):
        full_step(table, left, right, vec_half, back, sums, first_sector + i, i)
    core = lax.axis_index("c")
    for out, first in ((keep, HALF * core), (give, HALF - HALF * core)):
        for i in range(HALF):
            out[:, i * ROWS : (i + 1) * ROWS] = sums[first + i].reshape(LINE, ROWS, BLOCK)


def first_kernel(
    table, left, right, start, own, one, two, three, keep, give, vector, pieces,
    vec_half, back, sums,
):
    wf = lax.axis_index("wf")
    squares = (own[0:1, 0:1] + one[SIDE : SIDE + 1, 0:1]) + (
        two[0:1, 0:1] + three[SIDE : SIDE + 1, 0:1]
    )
    scale = 1.0 / jnp.sqrt(squares / ENTRIES + EPS)

    def put(position, block):
        sector = sector_at(wf, position)
        inside = (sector >= 0) & (sector < SECTORS)
        value = jnp.where(inside, block * scale, 0.0)
        vector[position] = value
        vec_half[position] = value.astype(bf16)

    odd = wf & 1
    for i in range(OWN):
        put(4 * odd + i, start[i])
    for i in range(2):
        rows = slice(i * BLOCK, (i + 1) * BLOCK)
        put(4 - 2 * odd + i, one[rows])
        put(6 - 6 * odd + i, three[rows])
    held = [own[EXTRA:], one[SIDE + EXTRA :], two[EXTRA:], three[SIDE + EXTRA :]]
    for place in range(2):
        source = (lax.axis_index("c") + 2 * place) ^ wf
        value = held[0]
        for other in range(1, 4):
            value = jnp.where(source == other, held[other], value)
        pieces[place] = value * scale
    full_sweep(table, left, right, vec_half, back, sums, keep, give)


def join_kernel(first, second, out):
    out[...] = first[...] + second[...]


def spread_kernel(parts, out):
    summed = jnp.sum(parts[...], axis=0)
    for target in range(out.shape[0]):
        out[target] = summed


def combined(masks, parts):
    base = HALF * lax.axis_index("c")
    sums = []
    for other in range(4):
        rows = parts[other] + parts[4 + other] + (parts[8 + other] + parts[12 + other])
        sums.append(rows.reshape(HALF, ROWS, BLOCK))
    values = []
    for place in range(2):
        blocks = []
        for k in range(HALF):
            value = jnp.zeros((ROWS, BLOCK), f32)
            for other in range(4):
                here = sector_at(other, base + k) == base + k + 8 * place
                value = value + jnp.where(here, sums[other][k], 0.0)
            blocks.append(value)
        values.append(jnp.concatenate(blocks, axis=0) * masks[place])
    return values


def send(values, sums, out):
    wf, base, _ = place_here()
    chosen = []
    for k in range(HALF):
        sector = sector_at(wf, base + k)
        rows = slice(k * ROWS, (k + 1) * ROWS)
        block = jnp.where(sector == base + k, values[0][rows], 0.0)
        chosen.append(jnp.where(sector == base + k + 8, values[1][rows], block))
    chosen = jnp.concatenate(chosen, axis=0)
    packed = pack(sums)
    for target in range(LINE):
        out[target, 0:CHUNK] = chosen
        out[target, CHUNK:] = packed


def image_kernel(parts, masks, pieces, out, image_pieces):
    image = combined(masks, parts)
    vec = [pieces[0], pieces[1]]

    def inner(first, second):
        return total(first[0] * second[0] + first[1] * second[1])

    vec_vec, vec_image = inner(vec, vec), inner(vec, image)
    part = ratio(vec_image, vec_vec)
    rest = [image[i] - part * vec[i] for i in range(2)]
    for i in range(2):
        image_pieces[i] = image[i]
    send(image, [vec_image, vec_vec, part, inner(rest, rest)], out)


def both(cores, count):
    return zip(*[lanes(held[:, CHUNK, :], count) for held in cores])


def add(values):
    return total(values[0]) + total(values[1])


def held_block(cores, position):
    rows = slice(ROWS * (position % HALF), ROWS * (position % HALF) + ROWS)
    own, other = (held[:, rows, :].reshape(BLOCK, BLOCK) for held in cores)
    return jnp.where(lax.axis_index("c") == position // HALF, own, other)


def second_kernel(
    table, left, right, own, other, vector, keep, give, direction, image, scalars,
    vec_half, back, sums,
):
    cores = (own, other)
    vec_image, vec_vec, part, rest = both(cores, 4)
    ritz = add(vec_image) / ENTRIES
    norm = add([rest[i] + (ritz - part[i]) * (ritz - part[i]) * vec_vec[i] for i in range(2)])
    norm = norm / ENTRIES
    scale = 1.0 / jnp.sqrt(norm + EPS)
    scalars[...] = pack([ritz, norm])
    for position in range(WINDOW):
        held = held_block(cores, position)
        value = (held - ritz * vector[position]) * scale
        image[position] = held
        direction[position] = value
        vec_half[position] = value.astype(bf16)
    full_sweep(table, left, right, vec_half, back, sums, keep, give)


def turned_kernel(parts, masks, pieces, image_pieces, scalars, out):
    turned = combined(masks, parts)
    ritz, norm = scalars[0:1, 0:1], scalars[0:1, 1:2]
    scale = 1.0 / jnp.sqrt(norm + EPS)
    vec = [pieces[i] for i in range(2)]
    image = [image_pieces[i] for i in range(2)]
    turn = [(image[i] - ritz * vec[i]) * scale for i in range(2)]

    def inner(first, second):
        return total(first[0] * second[0] + first[1] * second[1])

    vec_vec, vec_turned = inner(vec, vec), inner(vec, turned)
    along = ratio(inner(vec, turn), vec_vec)
    new = [turn[i] - along * vec[i] for i in range(2)]
    on_vec = ratio(vec_turned, vec_vec)
    rest = [turned[i] - on_vec * vec[i] for i in range(2)]
    new_new = inner(new, new)
    on_new = ratio(inner(new, rest), new_new)
    rest = [rest[i] - on_new * new[i] for i in range(2)]
    sums = [
        vec_turned, inner(turn, image), inner(turn, turned),
        vec_vec, along, on_vec, new_new, on_new, inner(rest, rest),
    ]
    send(turned, sums, out)


def mixing(ritz, curvature, norm):
    gap = ritz - curvature
    lowest = 0.5 * (ritz + curvature) - jnp.sqrt(0.25 * gap * gap + norm)
    keep = curvature - lowest
    take = -jnp.sqrt(norm)
    scale = jnp.sqrt(keep * keep + take * take)
    return lowest, keep / scale, take / scale


def third_kernel(
    table, left, right, gathered, swapped, vector, direction, image, scalars,
    out, new_vector, new_direction, new_scalars, vec_half, back,
):
    cores = (gathered, swapped)
    wf = lax.axis_index("wf")
    (
        vec_turned, turn_image, turn_turned, vec_vec, along, on_vec, new_new, on_new, rest,
    ) = both(cores, 9)
    ritz, norm = scalars[0:1, 0:1], scalars[0:1, 1:2]
    curvature = add(turn_turned) / ENTRIES
    lowest, keep, take = mixing(ritz, curvature, norm)
    mixed = (add(vec_turned) + add(turn_image)) / ENTRIES
    next_ritz = keep * keep * ritz + keep * take * mixed + take * take * curvature
    first = keep * (ritz - next_ritz)
    second = keep * jnp.sqrt(norm + EPS) - take * next_ritz
    squares = []
    for i in range(2):
        on_first = first + second * along[i] + take * on_vec[i]
        on_second = second + take * on_new[i]
        square = on_first * on_first * vec_vec[i] + on_second * on_second * new_new[i]
        squares.append(square + take * take * rest[i])
    next_norm = add(squares) / ENTRIES
    scale = 1.0 / jnp.sqrt(next_norm + EPS)
    new_scalars[...] = pack([next_ritz, next_norm, lowest])
    for position in range(WINDOW):
        turned = held_block(cores, position)
        mixed_vec = keep * vector[position] + take * direction[position]
        mixed_image = keep * image[position] + take * turned
        value = (mixed_image - next_ritz * mixed_vec) * scale
        vec_half[position] = value.astype(bf16)

        @pl.when((position // 4) == (wf & 1))
        def _():
            new_vector[position % 4] = mixed_vec
            new_direction[position % 4] = value

    value = jnp.zeros((1, 1), f32)
    for i in range(OWN):
        half = half_step(table, left, right, vec_half, back, OWN * wf + i, i)
        value = value + total(half * new_direction[i])
    out[...] = jnp.broadcast_to(2.0 * value, out.shape)


def last_kernel(parts, vector, direction, scalars, out, energies):
    curvature = total(parts[:, 0:1]) / ENTRIES
    ritz, norm, first_lowest = lanes(scalars[0:1], 3)
    lowest, keep, take = mixing(ritz, curvature, norm)
    for i in range(OWN):
        out[i] = keep * vector[i] + take * direction[i]
    energies[0] = first_lowest[0, 0]
    energies[1] = lowest[0, 0]


HBM = pl.BlockSpec(memory_space=pltpu.HBM)
VMEM = pl.BlockSpec(memory_space=pltpu.VMEM)
SMEM = pl.BlockSpec(memory_space=pltpu.SMEM)
MIB = 1 << 20


def struct(*shape, dtype=f32):
    return jax.ShapeDtypeStruct(shape, dtype)


def call(kernel, name, outs, in_specs, args, out_specs=None, scratch=(), limit=6):
    return pl.pallas_call(
        kernel,
        name=name,
        in_specs=in_specs,
        out_specs=out_specs or [VMEM] * len(outs),
        out_shape=outs,
        scratch_shapes=scratch,
        compiler_params=pltpu.CompilerParams(vmem_limit_bytes=int(limit * MIB)),
    )(*args)


def small(kernel, name, outs, *arrays, out_specs=None):
    return call(kernel, name, outs, [VMEM] * len(arrays), arrays, out_specs)


def step(kernel, name, outs, operators, arrays, sums=True):
    scratch = [
        pltpu.VMEM((WINDOW, BLOCK, BLOCK), bf16),
        pltpu.VMEM((BLOCK, PAIRS * BLOCK), bf16),
    ]
    if sums:
        scratch.append(pltpu.VMEM((WINDOW, BLOCK, BLOCK), f32))
    args = (*operators, *arrays)
    in_specs = [SMEM] + [VMEM] * (len(args) - 1)
    return call(kernel, name, outs, in_specs, args, scratch=scratch, limit=16)


def exchange(value, axes):
    return lax.all_to_all(value, axes, 0, 0, tiled=True)


def shards(guess, left_ops, right_ops, op_shift, op_mask, left_dims, right_dims):
    blocks = struct(WINDOW, BLOCK, BLOCK)
    half = struct(LINE, CHUNK, BLOCK)
    own_blocks = struct(OWN, BLOCK, BLOCK)
    pair = struct(2, CHUNK, BLOCK)
    scalar_row = struct(EXTRA, BLOCK)
    packet = struct(LINE, CHUNK + EXTRA, BLOCK)

    def partner(value, distance):
        return lax.ppermute(value, "wf", [(i, i ^ distance) for i in range(4)])

    def swapped(value):
        return lax.ppermute(value, "c", [(0, 1), (1, 0)])

    table = (2 * op_shift[:, None] + op_mask).reshape(-1)
    tail = EXTRA + CHUNK
    start, masks, one, own, three = call(
        norm_kernel, "norm",
        [own_blocks, pair, struct(SIDE + tail, BLOCK), struct(tail, BLOCK),
         struct(SIDE + tail, BLOCK)],
        [SMEM, SMEM, VMEM], (left_dims, right_dims, guess), limit=60,
    )
    one, two, three = partner(one, 1), partner(own, 2), partner(three, 3)
    held = struct(OWN, PAIRS, BLOCK, BLOCK, dtype=bf16)
    left, right = call(
        load_kernel, "load", [held, held], [HBM, HBM], (left_ops, right_ops),
        scratch=[pltpu.SemaphoreType.DMA((2 * OWN,))], limit=55.5,
    )
    operators = (table, left, right)

    def reduced(keep, give):
        (summed,) = small(join_kernel, "join", [half], keep, swapped(give))
        parts = exchange(summed, "z")
        (tiled,) = small(spread_kernel, "spread", [struct(CROSS, CHUNK, BLOCK)], parts)
        return exchange(tiled, CROSS_AXES)

    def gathered(packets):
        packets = exchange(packets, "z")
        return packets, swapped(packets)

    keep, give, vector, pieces = step(
        first_kernel, "first", [half, half, blocks, pair], operators,
        (start, own, one, two, three),
    )
    packets, image_pieces = small(
        image_kernel, "image", [packet, pair], reduced(keep, give), masks, pieces
    )
    keep, give, direction, image, scalars = step(
        second_kernel, "second", [half, half, blocks, blocks, scalar_row], operators,
        (*gathered(packets), vector),
    )
    (packets,) = small(
        turned_kernel, "turned", [packet], reduced(keep, give), masks, pieces, image_pieces, scalars
    )
    sums, vector, direction, scalars = step(
        third_kernel, "third", [struct(256, BLOCK), own_blocks, own_blocks, scalar_row], operators,
        (*gathered(packets), vector, direction, image, scalars), sums=False,
    )
    sums = exchange(sums, (*OP_AXES, "wf"))
    result, energies = small(
        last_kernel, "last", [own_blocks, struct(2)], sums, vector, direction, scalars,
        out_specs=[VMEM, SMEM],
    )
    return result, energies


def solution(mesh):
    split = Mesh(mesh.devices.reshape(4, 8, 2, 4), (*OP_AXES, "wf"))
    in_specs = (
        P("wf", None, None),
        P(OP_AXES, "wf", None, None),
        P(OP_AXES, "wf", None, None),
        P(OP_AXES),
        P(OP_AXES, "wf"),
        P(),
        P(),
    )
    out_specs = (P("wf", None, None), P())
    return jax.shard_map(
        shards, mesh=split, in_specs=in_specs, out_specs=out_specs, check_vma=False
    )
```

```python
import jax
import jax.numpy as jnp
from jax import lax
from jax.experimental import pallas as pl
from jax.experimental.pallas import tpu as pltpu
from jax.sharding import Mesh, PartitionSpec as P

EPS = 1e-06
SECTORS = 16
BLOCK = 128
PAIRS = 16
OWN = 4
WINDOW = 8
LINE = 16
CROSS = 8
HALF = 4
ROWS = 8
CHUNK = HALF * ROWS
SIDE = 2 * BLOCK
EXTRA = 8
ENTRIES = float(SECTORS * BLOCK * BLOCK)
LINE_AXES = ("y_far", "z")
CROSS_AXES = ("y_near", "wf")
OP_AXES = ("y_far", "y_near", "z", "c")

f32 = jnp.float32
bf16 = jnp.bfloat16


def dot(first, second, first_dim=1, second_dim=0):
    return lax.dot_general(
        first, second, (((first_dim,), (second_dim,)), ((), ())), preferred_element_type=f32
    )


def total(values):
    return jnp.sum(values, axis=(0, 1), keepdims=True)


def ratio(top, bottom):
    return jnp.where(bottom > 0, top / jnp.where(bottom > 0, bottom, 1.0), 0.0)


def place_here():
    chunk = lax.axis_index("y_far") * lax.axis_size("z") + lax.axis_index("z")
    first_row = pl.multiple_of(chunk * ROWS, ROWS)
    return lax.axis_index("wf"), HALF * lax.axis_index("c"), first_row


def sector_at(wf, position):
    base = OWN * wf - 2
    return base + ((position - base) & 7)


def live(left_dims, right_dims, sector, first_row, rows):
    held = jnp.clip(sector, 0, SECTORS - 1)
    inside = (sector >= 0) & (sector < SECTORS)
    height = jnp.where(inside, left_dims[held], 0)
    width = right_dims[SECTORS - 1 - held]
    row = lax.broadcasted_iota(jnp.int32, (rows, BLOCK), 0) + first_row
    column = lax.broadcasted_iota(jnp.int32, (rows, BLOCK), 1)
    return (row < height) & (column < width)


def pack(values):
    lane = lax.broadcasted_iota(jnp.int32, (EXTRA, BLOCK), 1)
    packed = jnp.zeros((EXTRA, BLOCK), f32)
    for place, value in enumerate(values):
        packed = jnp.where(lane == place, value, packed)
    return packed


def lanes(rows, count):
    return [rows[:, place : place + 1] for place in range(count)]


def load_kernel(left_hbm, right_hbm, left, right, sems):
    copies = []
    for i in range(OWN):
        for source, target in ((left_hbm, left), (right_hbm, right)):
            copies.append(
                pltpu.make_async_copy(source.at[:, i], target.at[i], sems.at[len(copies)])
            )
    for copy in copies:
        copy.start()
    for copy in copies:
        copy.wait()


def norm_kernel(left_dims, right_dims, guess, start, masks, one, two, three):
    wf, base, first_row = place_here()
    sums = jnp.zeros((1, 1), f32)
    for i in range(OWN):
        mask = live(left_dims, right_dims, OWN * wf + i, 0, BLOCK)
        block = jnp.where(mask, guess[i], 0.0)
        start[i] = block
        sums = sums + total(block * block)
    odd = wf & 1
    for i in range(2):
        one[i * BLOCK : (i + 1) * BLOCK] = start[2 - 2 * odd + i]
        three[i * BLOCK : (i + 1) * BLOCK] = start[2 * odd + i]
    for out, first in ((one, SIDE), (two, 0), (three, SIDE)):
        out[first : first + EXTRA] = jnp.broadcast_to(sums, (EXTRA, BLOCK))
        out[first + EXTRA :] = start[:, pl.ds(first_row, ROWS)].reshape(CHUNK, BLOCK)
    for i in range(2):
        for k in range(HALF):
            mask = live(left_dims, right_dims, base + k + 8 * i, first_row, ROWS)
            masks[i, k * ROWS : (k + 1) * ROWS] = jnp.where(mask, 1.0, 0.0)


def half_step(table, left, right, vec_half, back, sector, index):
    for k in range(PAIRS):
        entry = table[k * OWN + index]
        position = (sector + (entry >> 1)) & 7
        weight = (entry & 1).astype(f32)
        value = dot(left[index, k].T, vec_half[position])
        back[:, k * BLOCK : (k + 1) * BLOCK] = (value * weight).astype(bf16)
    return dot(back[...], right[index].reshape(PAIRS * BLOCK, BLOCK))


def full_step(table, left, right, vec_half, back, sums, sector, index):
    middle = dot(left[index].reshape(PAIRS * BLOCK, BLOCK), vec_half[sector & 7])
    for k in range(PAIRS):
        entry = table[k * OWN + index]
        position = (sector + (entry >> 1)) & 7
        weight = (entry & 1).astype(f32)
        term = (middle[k * BLOCK : (k + 1) * BLOCK] * weight).astype(bf16)
        sums[position] += dot(term, right[index, k], 1, 1)
    sums[sector & 7] += half_step(table, left, right, vec_half, back, sector, index)


def full_sweep(table, left, right, vec_half, back, sums, keep, give):
    sums[...] = jnp.zeros_like(sums)
    first_sector = OWN * lax.axis_index("wf")
    for i in range(OWN):
        full_step(table, left, right, vec_half, back, sums, first_sector + i, i)
    core = lax.axis_index("c")
    for out, first in ((keep, HALF * core), (give, HALF - HALF * core)):
        for i in range(HALF):
            out[:, i * ROWS : (i + 1) * ROWS] = sums[first + i].reshape(LINE, ROWS, BLOCK)


def first_kernel(
    table, left, right, start, own, one, two, three, keep, give, vector, pieces,
    vec_half, back, sums,
):
    wf = lax.axis_index("wf")
    squares = (own[0:1, 0:1] + one[SIDE : SIDE + 1, 0:1]) + (
        two[0:1, 0:1] + three[SIDE : SIDE + 1, 0:1]
    )
    scale = 1.0 / jnp.sqrt(squares / ENTRIES + EPS)

    def put(position, block):
        sector = sector_at(wf, position)
        inside = (sector >= 0) & (sector < SECTORS)
        value = jnp.where(inside, block * scale, 0.0)
        vector[position] = value
        vec_half[position] = value.astype(bf16)

    odd = wf & 1
    for i in range(OWN):
        put(4 * odd + i, start[i])
    for i in range(2):
        rows = slice(i * BLOCK, (i + 1) * BLOCK)
        put(4 - 2 * odd + i, one[rows])
        put(6 - 6 * odd + i, three[rows])
    held = [own[EXTRA:], one[SIDE + EXTRA :], two[EXTRA:], three[SIDE + EXTRA :]]
    for place in range(2):
        source = (lax.axis_index("c") + 2 * place) ^ wf
        value = held[0]
        for other in range(1, 4):
            value = jnp.where(source == other, held[other], value)
        pieces[place] = value * scale
    full_sweep(table, left, right, vec_half, back, sums, keep, give)


def join_kernel(first, second, out):
    out[...] = first[...] + second[...]


def spread_kernel(parts, out):
    summed = jnp.sum(parts[...], axis=0)
    for target in range(out.shape[0]):
        out[target] = summed


def combined(masks, parts):
    base = HALF * lax.axis_index("c")
    sums = []
    for other in range(4):
        sums.append((parts[other] + parts[4 + other]).reshape(HALF, ROWS, BLOCK))
    values = []
    for place in range(2):
        blocks = []
        for k in range(HALF):
            value = jnp.zeros((ROWS, BLOCK), f32)
            for other in range(4):
                here = sector_at(other, base + k) == base + k + 8 * place
                value = value + jnp.where(here, sums[other][k], 0.0)
            blocks.append(value)
        values.append(jnp.concatenate(blocks, axis=0) * masks[place])
    return values


def send(values, sums, out):
    wf, base, _ = place_here()
    chosen = []
    for k in range(HALF):
        sector = sector_at(wf, base + k)
        rows = slice(k * ROWS, (k + 1) * ROWS)
        block = jnp.where(sector == base + k, values[0][rows], 0.0)
        chosen.append(jnp.where(sector == base + k + 8, values[1][rows], block))
    chosen = jnp.concatenate(chosen, axis=0)
    packed = pack(sums)
    for target in range(LINE):
        out[target, 0:CHUNK] = chosen
        out[target, CHUNK:] = packed


def image_kernel(parts, masks, pieces, out, image_pieces):
    image = combined(masks, parts)
    vec = [pieces[0], pieces[1]]

    def inner(first, second):
        return total(first[0] * second[0] + first[1] * second[1])

    vec_vec, vec_image = inner(vec, vec), inner(vec, image)
    part = ratio(vec_image, vec_vec)
    rest = [image[i] - part * vec[i] for i in range(2)]
    for i in range(2):
        image_pieces[i] = image[i]
    send(image, [vec_image, vec_vec, part, inner(rest, rest)], out)


def both(cores, count):
    return zip(*[lanes(held[:, CHUNK, :], count) for held in cores])


def add(values):
    return total(values[0]) + total(values[1])


def held_block(cores, position):
    rows = slice(ROWS * (position % HALF), ROWS * (position % HALF) + ROWS)
    own, other = (held[:, rows, :].reshape(BLOCK, BLOCK) for held in cores)
    return jnp.where(lax.axis_index("c") == position // HALF, own, other)


def second_kernel(
    table, left, right, own, other, vector, keep, give, direction, image, scalars,
    vec_half, back, sums,
):
    cores = (own, other)
    vec_image, vec_vec, part, rest = both(cores, 4)
    ritz = add(vec_image) / ENTRIES
    norm = add([rest[i] + (ritz - part[i]) * (ritz - part[i]) * vec_vec[i] for i in range(2)])
    norm = norm / ENTRIES
    scale = 1.0 / jnp.sqrt(norm + EPS)
    scalars[...] = pack([ritz, norm])
    for position in range(WINDOW):
        held = held_block(cores, position)
        value = (held - ritz * vector[position]) * scale
        image[position] = held
        direction[position] = value
        vec_half[position] = value.astype(bf16)
    full_sweep(table, left, right, vec_half, back, sums, keep, give)


def turned_kernel(parts, masks, pieces, image_pieces, scalars, out):
    turned = combined(masks, parts)
    ritz, norm = scalars[0:1, 0:1], scalars[0:1, 1:2]
    scale = 1.0 / jnp.sqrt(norm + EPS)
    vec = [pieces[i] for i in range(2)]
    image = [image_pieces[i] for i in range(2)]
    turn = [(image[i] - ritz * vec[i]) * scale for i in range(2)]

    def inner(first, second):
        return total(first[0] * second[0] + first[1] * second[1])

    vec_vec, vec_turned = inner(vec, vec), inner(vec, turned)
    along = ratio(inner(vec, turn), vec_vec)
    new = [turn[i] - along * vec[i] for i in range(2)]
    on_vec = ratio(vec_turned, vec_vec)
    rest = [turned[i] - on_vec * vec[i] for i in range(2)]
    new_new = inner(new, new)
    on_new = ratio(inner(new, rest), new_new)
    rest = [rest[i] - on_new * new[i] for i in range(2)]
    sums = [
        vec_turned, inner(turn, image), inner(turn, turned),
        vec_vec, along, on_vec, new_new, on_new, inner(rest, rest),
    ]
    send(turned, sums, out)


def mixing(ritz, curvature, norm):
    gap = ritz - curvature
    lowest = 0.5 * (ritz + curvature) - jnp.sqrt(0.25 * gap * gap + norm)
    keep = curvature - lowest
    take = -jnp.sqrt(norm)
    scale = jnp.sqrt(keep * keep + take * take)
    return lowest, keep / scale, take / scale


def third_kernel(
    table, left, right, gathered, swapped, vector, direction, image, scalars,
    out, new_vector, new_direction, new_scalars, vec_half, back,
):
    cores = (gathered, swapped)
    wf = lax.axis_index("wf")
    (
        vec_turned, turn_image, turn_turned, vec_vec, along, on_vec, new_new, on_new, rest,
    ) = both(cores, 9)
    ritz, norm = scalars[0:1, 0:1], scalars[0:1, 1:2]
    curvature = add(turn_turned) / ENTRIES
    lowest, keep, take = mixing(ritz, curvature, norm)
    mixed = (add(vec_turned) + add(turn_image)) / ENTRIES
    next_ritz = keep * keep * ritz + keep * take * mixed + take * take * curvature
    first = keep * (ritz - next_ritz)
    second = keep * jnp.sqrt(norm + EPS) - take * next_ritz
    squares = []
    for i in range(2):
        on_first = first + second * along[i] + take * on_vec[i]
        on_second = second + take * on_new[i]
        square = on_first * on_first * vec_vec[i] + on_second * on_second * new_new[i]
        squares.append(square + take * take * rest[i])
    next_norm = add(squares) / ENTRIES
    scale = 1.0 / jnp.sqrt(next_norm + EPS)
    new_scalars[...] = pack([next_ritz, next_norm, lowest])
    for position in range(WINDOW):
        turned = held_block(cores, position)
        mixed_vec = keep * vector[position] + take * direction[position]
        mixed_image = keep * image[position] + take * turned
        value = (mixed_image - next_ritz * mixed_vec) * scale
        vec_half[position] = value.astype(bf16)

        @pl.when((position // 4) == (wf & 1))
        def _():
            new_vector[position % 4] = mixed_vec
            new_direction[position % 4] = value

    value = jnp.zeros((1, 1), f32)
    for i in range(OWN):
        half = half_step(table, left, right, vec_half, back, OWN * wf + i, i)
        value = value + total(half * new_direction[i])
    out[...] = jnp.broadcast_to(2.0 * value, out.shape)


def last_kernel(parts, vector, direction, scalars, out, energies):
    curvature = total(parts[:, 0:1]) / ENTRIES
    ritz, norm, first_lowest = lanes(scalars[0:1], 3)
    lowest, keep, take = mixing(ritz, curvature, norm)
    for i in range(OWN):
        out[i] = keep * vector[i] + take * direction[i]
    energies[0] = first_lowest[0, 0]
    energies[1] = lowest[0, 0]


HBM = pl.BlockSpec(memory_space=pltpu.HBM)
VMEM = pl.BlockSpec(memory_space=pltpu.VMEM)
SMEM = pl.BlockSpec(memory_space=pltpu.SMEM)
MIB = 1 << 20


def struct(*shape, dtype=f32):
    return jax.ShapeDtypeStruct(shape, dtype)


def call(kernel, name, outs, in_specs, args, out_specs=None, scratch=(), limit=6):
    return pl.pallas_call(
        kernel,
        name=name,
        in_specs=in_specs,
        out_specs=out_specs or [VMEM] * len(outs),
        out_shape=outs,
        scratch_shapes=scratch,
        compiler_params=pltpu.CompilerParams(vmem_limit_bytes=int(limit * MIB)),
    )(*args)


def small(kernel, name, outs, *arrays, out_specs=None):
    return call(kernel, name, outs, [VMEM] * len(arrays), arrays, out_specs)


def step(kernel, name, outs, operators, arrays, sums=True):
    scratch = [
        pltpu.VMEM((WINDOW, BLOCK, BLOCK), bf16),
        pltpu.VMEM((BLOCK, PAIRS * BLOCK), bf16),
    ]
    if sums:
        scratch.append(pltpu.VMEM((WINDOW, BLOCK, BLOCK), f32))
    args = (*operators, *arrays)
    in_specs = [SMEM] + [VMEM] * (len(args) - 1)
    return call(kernel, name, outs, in_specs, args, scratch=scratch, limit=16)


def exchange(value, axes):
    return lax.all_to_all(value, axes, 0, 0, tiled=True)


def shards(guess, left_ops, right_ops, op_shift, op_mask, left_dims, right_dims):
    blocks = struct(WINDOW, BLOCK, BLOCK)
    half = struct(LINE, CHUNK, BLOCK)
    own_blocks = struct(OWN, BLOCK, BLOCK)
    pair = struct(2, CHUNK, BLOCK)
    scalar_row = struct(EXTRA, BLOCK)
    packet = struct(LINE, CHUNK + EXTRA, BLOCK)

    def partner(value, distance):
        return lax.ppermute(value, "wf", [(i, i ^ distance) for i in range(4)])

    def swapped(value):
        return lax.ppermute(value, "c", [(0, 1), (1, 0)])

    table = (2 * op_shift[:, None] + op_mask).reshape(-1)
    tail = EXTRA + CHUNK
    start, masks, one, own, three = call(
        norm_kernel, "norm",
        [own_blocks, pair, struct(SIDE + tail, BLOCK), struct(tail, BLOCK),
         struct(SIDE + tail, BLOCK)],
        [SMEM, SMEM, VMEM], (left_dims, right_dims, guess), limit=60,
    )
    one, two, three = partner(one, 1), partner(own, 2), partner(three, 3)
    held = struct(OWN, PAIRS, BLOCK, BLOCK, dtype=bf16)
    left, right = call(
        load_kernel, "load", [held, held], [HBM, HBM], (left_ops, right_ops),
        scratch=[pltpu.SemaphoreType.DMA((2 * OWN,))], limit=49,
    )
    operators = (table, left, right)

    def reduced(keep, give):
        (summed,) = small(join_kernel, "join", [half], keep, swapped(give))
        parts = exchange(summed, LINE_AXES)
        (tiled,) = small(spread_kernel, "spread", [struct(CROSS, CHUNK, BLOCK)], parts)
        return exchange(tiled, CROSS_AXES)

    def gathered(packets):
        packets = exchange(packets, LINE_AXES)
        return packets, swapped(packets)

    keep, give, vector, pieces = step(
        first_kernel, "first", [half, half, blocks, pair], operators,
        (start, own, one, two, three),
    )
    packets, image_pieces = small(
        image_kernel, "image", [packet, pair], reduced(keep, give), masks, pieces
    )
    keep, give, direction, image, scalars = step(
        second_kernel, "second", [half, half, blocks, blocks, scalar_row], operators,
        (*gathered(packets), vector),
    )
    (packets,) = small(
        turned_kernel, "turned", [packet], reduced(keep, give), masks, pieces, image_pieces, scalars
    )
    sums, vector, direction, scalars = step(
        third_kernel, "third", [struct(256, BLOCK), own_blocks, own_blocks, scalar_row], operators,
        (*gathered(packets), vector, direction, image, scalars), sums=False,
    )
    sums = exchange(sums, (*OP_AXES, "wf"))
    result, energies = small(
        last_kernel, "last", [own_blocks, struct(2)], sums, vector, direction, scalars,
        out_specs=[VMEM, SMEM],
    )
    return result, energies


def solution(mesh):
    split = Mesh(mesh.devices.reshape(2, 2, 8, 2, 4), (*OP_AXES, "wf"))
    in_specs = (
        P("wf", None, None),
        P(OP_AXES, "wf", None, None),
        P(OP_AXES, "wf", None, None),
        P(OP_AXES),
        P(OP_AXES, "wf"),
        P(),
        P(),
    )
    out_specs = (P("wf", None, None), P())
    return jax.shard_map(
        shards, mesh=split, in_specs=in_specs, out_specs=out_specs, check_vma=False
    )
```

```python
import jax
import jax.numpy as jnp
from jax import lax
from jax.experimental import pallas as pl
from jax.experimental.pallas import tpu as pltpu
from jax.sharding import Mesh, PartitionSpec as P

EPS = 1e-06
SECTORS = 16
BLOCK = 128
PAIRS = 16
OWN = 4
WINDOW = 8
LINE = 16
CROSS = 8
HALF = 4
ROWS = 8
CHUNK = HALF * ROWS
SIDE = 2 * BLOCK
EXTRA = 8
ENTRIES = float(SECTORS * BLOCK * BLOCK)
LINE_AXES = ("y_far", "z")
CROSS_AXES = ("y_near", "wf")
OP_AXES = ("y_far", "y_near", "z", "c")

f32 = jnp.float32
bf16 = jnp.bfloat16


def dot(first, second, first_dim=1, second_dim=0):
    return lax.dot_general(
        first, second, (((first_dim,), (second_dim,)), ((), ())), preferred_element_type=f32
    )


def total(values):
    return jnp.sum(values, axis=(0, 1), keepdims=True)


def ratio(top, bottom):
    return jnp.where(bottom > 0, top / jnp.where(bottom > 0, bottom, 1.0), 0.0)


def place_here():
    chunk = lax.axis_index("y_far") * lax.axis_size("z") + lax.axis_index("z")
    first_row = pl.multiple_of(chunk * ROWS, ROWS)
    return lax.axis_index("wf"), HALF * lax.axis_index("c"), first_row


def sector_at(wf, position):
    base = OWN * wf - 2
    return base + ((position - base) & 7)


def live(left_dims, right_dims, sector, first_row, rows):
    held = jnp.clip(sector, 0, SECTORS - 1)
    inside = (sector >= 0) & (sector < SECTORS)
    height = jnp.where(inside, left_dims[held], 0)
    width = right_dims[SECTORS - 1 - held]
    row = lax.broadcasted_iota(jnp.int32, (rows, BLOCK), 0) + first_row
    column = lax.broadcasted_iota(jnp.int32, (rows, BLOCK), 1)
    return (row < height) & (column < width)


def pack(values):
    lane = lax.broadcasted_iota(jnp.int32, (EXTRA, BLOCK), 1)
    packed = jnp.zeros((EXTRA, BLOCK), f32)
    for place, value in enumerate(values):
        packed = jnp.where(lane == place, value, packed)
    return packed


def lanes(rows, count):
    return [rows[:, place : place + 1] for place in range(count)]


def load_kernel(left_hbm, right_hbm, left, right, sems):
    copies = []
    for i in range(OWN):
        for source, target in ((left_hbm, left), (right_hbm, right)):
            copies.append(
                pltpu.make_async_copy(source.at[:, i], target.at[i], sems.at[len(copies)])
            )
    for copy in copies:
        copy.start()
    for copy in copies:
        copy.wait()


def norm_kernel(left_dims, right_dims, guess, start, masks, one, two, three):
    wf, base, first_row = place_here()
    sums = jnp.zeros((1, 1), f32)
    for i in range(OWN):
        mask = live(left_dims, right_dims, OWN * wf + i, 0, BLOCK)
        block = jnp.where(mask, guess[i], 0.0)
        start[i] = block
        sums = sums + total(block * block)
    odd = wf & 1
    for i in range(2):
        one[i * BLOCK : (i + 1) * BLOCK] = start[2 - 2 * odd + i]
        three[i * BLOCK : (i + 1) * BLOCK] = start[2 * odd + i]
    for out, first in ((one, SIDE), (two, 0), (three, SIDE)):
        out[first : first + EXTRA] = jnp.broadcast_to(sums, (EXTRA, BLOCK))
        out[first + EXTRA :] = start[:, pl.ds(first_row, ROWS)].reshape(CHUNK, BLOCK)
    for i in range(2):
        for k in range(HALF):
            mask = live(left_dims, right_dims, base + k + 8 * i, first_row, ROWS)
            masks[i, k * ROWS : (k + 1) * ROWS] = jnp.where(mask, 1.0, 0.0)


def half_step(table, left, right, vec_half, back, sector, index):
    for k in range(PAIRS):
        entry = table[index * PAIRS + k]
        position = (sector + (entry >> 1)) & 7
        weight = (entry & 1).astype(f32)
        value = dot(left[index, k].T, vec_half[position])
        back[:, k * BLOCK : (k + 1) * BLOCK] = (value * weight).astype(bf16)
    return dot(back[...], right[index].reshape(PAIRS * BLOCK, BLOCK))


def full_step(table, left, right, vec_half, back, sums, sector, index):
    middle = dot(left[index].reshape(PAIRS * BLOCK, BLOCK), vec_half[sector & 7])
    for k in range(PAIRS):
        entry = table[index * PAIRS + k]
        position = (sector + (entry >> 1)) & 7
        weight = (entry & 1).astype(f32)
        term = (middle[k * BLOCK : (k + 1) * BLOCK] * weight).astype(bf16)
        sums[position] += dot(term, right[index, k], 1, 1)
    sums[sector & 7] += half_step(table, left, right, vec_half, back, sector, index)


def full_sweep(table, left, right, vec_half, back, sums, keep, give):
    sums[...] = jnp.zeros_like(sums)
    first_sector = OWN * lax.axis_index("wf")
    for i in range(OWN):
        full_step(table, left, right, vec_half, back, sums, first_sector + i, i)
    core = lax.axis_index("c")
    for out, first in ((keep, HALF * core), (give, HALF - HALF * core)):
        for i in range(HALF):
            out[:, i * ROWS : (i + 1) * ROWS] = sums[first + i].reshape(LINE, ROWS, BLOCK)


def first_kernel(
    table, left, right, start, own, one, two, three, keep, give, vector, pieces,
    vec_half, back, sums,
):
    wf = lax.axis_index("wf")
    squares = (own[0:1, 0:1] + one[SIDE : SIDE + 1, 0:1]) + (
        two[0:1, 0:1] + three[SIDE : SIDE + 1, 0:1]
    )
    scale = 1.0 / jnp.sqrt(squares / ENTRIES + EPS)

    def put(position, block):
        sector = sector_at(wf, position)
        inside = (sector >= 0) & (sector < SECTORS)
        value = jnp.where(inside, block * scale, 0.0)
        vector[position] = value
        vec_half[position] = value.astype(bf16)

    odd = wf & 1
    for i in range(OWN):
        put(4 * odd + i, start[i])
    for i in range(2):
        rows = slice(i * BLOCK, (i + 1) * BLOCK)
        put(4 - 2 * odd + i, one[rows])
        put(6 - 6 * odd + i, three[rows])
    held = [own[EXTRA:], one[SIDE + EXTRA :], two[EXTRA:], three[SIDE + EXTRA :]]
    for place in range(2):
        source = (lax.axis_index("c") + 2 * place) ^ wf
        value = held[0]
        for other in range(1, 4):
            value = jnp.where(source == other, held[other], value)
        pieces[place] = value * scale
    full_sweep(table, left, right, vec_half, back, sums, keep, give)


def join_kernel(first, second, out):
    out[...] = (first[...] + second[...]).astype(out.dtype)


def spread_kernel(parts, out):
    summed = jnp.sum(parts[...].astype(f32), axis=0)
    for target in range(out.shape[0]):
        out[target] = summed


def combined(masks, parts):
    base = HALF * lax.axis_index("c")
    sums = []
    for other in range(4):
        sums.append((parts[other] + parts[4 + other]).reshape(HALF, ROWS, BLOCK))
    values = []
    for place in range(2):
        blocks = []
        for k in range(HALF):
            value = jnp.zeros((ROWS, BLOCK), f32)
            for other in range(4):
                here = sector_at(other, base + k) == base + k + 8 * place
                value = value + jnp.where(here, sums[other][k], 0.0)
            blocks.append(value)
        values.append(jnp.concatenate(blocks, axis=0) * masks[place])
    return values


def send(values, sums, out):
    wf, base, _ = place_here()
    chosen = []
    for k in range(HALF):
        sector = sector_at(wf, base + k)
        rows = slice(k * ROWS, (k + 1) * ROWS)
        block = jnp.where(sector == base + k, values[0][rows], 0.0)
        chosen.append(jnp.where(sector == base + k + 8, values[1][rows], block))
    chosen = jnp.concatenate(chosen, axis=0)
    packed = pack(sums)
    for target in range(LINE):
        out[target, 0:CHUNK] = chosen
        out[target, CHUNK:] = packed


def image_kernel(parts, masks, pieces, out, image_pieces):
    image = combined(masks, parts)
    vec = [pieces[0], pieces[1]]

    def inner(first, second):
        return total(first[0] * second[0] + first[1] * second[1])

    vec_vec, vec_image = inner(vec, vec), inner(vec, image)
    part = ratio(vec_image, vec_vec)
    rest = [image[i] - part * vec[i] for i in range(2)]
    for i in range(2):
        image_pieces[i] = image[i]
    send(image, [vec_image, vec_vec, part, inner(rest, rest)], out)


def both(cores, count):
    return zip(*[lanes(held[:, CHUNK, :], count) for held in cores])


def add(values):
    return total(values[0]) + total(values[1])


def held_block(cores, position):
    rows = slice(ROWS * (position % HALF), ROWS * (position % HALF) + ROWS)
    own, other = (held[:, rows, :].reshape(BLOCK, BLOCK) for held in cores)
    return jnp.where(lax.axis_index("c") == position // HALF, own, other)


def second_kernel(
    table, left, right, own, other, vector, keep, give, direction, image, scalars,
    vec_half, back, sums,
):
    cores = (own, other)
    vec_image, vec_vec, part, rest = both(cores, 4)
    ritz = add(vec_image) / ENTRIES
    norm = add([rest[i] + (ritz - part[i]) * (ritz - part[i]) * vec_vec[i] for i in range(2)])
    norm = norm / ENTRIES
    scale = 1.0 / jnp.sqrt(norm + EPS)
    scalars[...] = pack([ritz, norm])
    for position in range(WINDOW):
        held = held_block(cores, position)
        value = (held - ritz * vector[position]) * scale
        image[position] = held
        direction[position] = value
        vec_half[position] = value.astype(bf16)
    full_sweep(table, left, right, vec_half, back, sums, keep, give)


def turned_kernel(parts, masks, pieces, image_pieces, scalars, out):
    turned = combined(masks, parts)
    ritz, norm = scalars[0:1, 0:1], scalars[0:1, 1:2]
    scale = 1.0 / jnp.sqrt(norm + EPS)
    vec = [pieces[i] for i in range(2)]
    image = [image_pieces[i] for i in range(2)]
    turn = [(image[i] - ritz * vec[i]) * scale for i in range(2)]

    def inner(first, second):
        return total(first[0] * second[0] + first[1] * second[1])

    vec_vec, vec_turned = inner(vec, vec), inner(vec, turned)
    along = ratio(inner(vec, turn), vec_vec)
    new = [turn[i] - along * vec[i] for i in range(2)]
    on_vec = ratio(vec_turned, vec_vec)
    rest = [turned[i] - on_vec * vec[i] for i in range(2)]
    new_new = inner(new, new)
    on_new = ratio(inner(new, rest), new_new)
    rest = [rest[i] - on_new * new[i] for i in range(2)]
    sums = [
        vec_turned, inner(turn, image), inner(turn, turned),
        vec_vec, along, on_vec, new_new, on_new, inner(rest, rest),
    ]
    send(turned, sums, out)


def mixing(ritz, curvature, norm):
    gap = ritz - curvature
    lowest = 0.5 * (ritz + curvature) - jnp.sqrt(0.25 * gap * gap + norm)
    keep = curvature - lowest
    take = -jnp.sqrt(norm)
    scale = jnp.sqrt(keep * keep + take * take)
    return lowest, keep / scale, take / scale


def third_kernel(
    table, left, right, gathered, swapped, vector, direction, image, scalars,
    out, new_vector, new_direction, new_scalars, vec_half, back,
):
    cores = (gathered, swapped)
    wf = lax.axis_index("wf")
    (
        vec_turned, turn_image, turn_turned, vec_vec, along, on_vec, new_new, on_new, rest,
    ) = both(cores, 9)
    ritz, norm = scalars[0:1, 0:1], scalars[0:1, 1:2]
    curvature = add(turn_turned) / ENTRIES
    lowest, keep, take = mixing(ritz, curvature, norm)
    mixed = (add(vec_turned) + add(turn_image)) / ENTRIES
    next_ritz = keep * keep * ritz + keep * take * mixed + take * take * curvature
    first = keep * (ritz - next_ritz)
    second = keep * jnp.sqrt(norm + EPS) - take * next_ritz
    squares = []
    for i in range(2):
        on_first = first + second * along[i] + take * on_vec[i]
        on_second = second + take * on_new[i]
        square = on_first * on_first * vec_vec[i] + on_second * on_second * new_new[i]
        squares.append(square + take * take * rest[i])
    next_norm = add(squares) / ENTRIES
    scale = 1.0 / jnp.sqrt(next_norm + EPS)
    new_scalars[...] = pack([next_ritz, next_norm, lowest])
    for position in range(WINDOW):
        turned = held_block(cores, position)
        mixed_vec = keep * vector[position] + take * direction[position]
        mixed_image = keep * image[position] + take * turned
        value = (mixed_image - next_ritz * mixed_vec) * scale
        vec_half[position] = value.astype(bf16)

        @pl.when((position // 4) == (wf & 1))
        def _():
            new_vector[position % 4] = mixed_vec
            new_direction[position % 4] = value

    value = jnp.zeros((1, 1), f32)
    for i in range(OWN):
        half = half_step(table, left, right, vec_half, back, OWN * wf + i, i)
        value = value + total(half * new_direction[i])
    out[...] = jnp.broadcast_to(2.0 * value, out.shape)


def last_kernel(parts, vector, direction, scalars, out, energies):
    curvature = total(parts[:, 0:1]) / ENTRIES
    ritz, norm, first_lowest = lanes(scalars[0:1], 3)
    lowest, keep, take = mixing(ritz, curvature, norm)
    for i in range(OWN):
        out[i] = keep * vector[i] + take * direction[i]
    energies[0] = first_lowest[0, 0]
    energies[1] = lowest[0, 0]


HBM = pl.BlockSpec(memory_space=pltpu.HBM)
VMEM = pl.BlockSpec(memory_space=pltpu.VMEM)
SMEM = pl.BlockSpec(memory_space=pltpu.SMEM)
MIB = 1 << 20


def struct(*shape, dtype=f32):
    return jax.ShapeDtypeStruct(shape, dtype)


def call(kernel, name, outs, in_specs, args, out_specs=None, scratch=(), limit=6):
    return pl.pallas_call(
        kernel,
        name=name,
        in_specs=in_specs,
        out_specs=out_specs or [VMEM] * len(outs),
        out_shape=outs,
        scratch_shapes=scratch,
        compiler_params=pltpu.CompilerParams(vmem_limit_bytes=int(limit * MIB)),
    )(*args)


def small(kernel, name, outs, *arrays, out_specs=None):
    return call(kernel, name, outs, [VMEM] * len(arrays), arrays, out_specs)


def step(kernel, name, outs, operators, arrays, sums=True):
    scratch = [
        pltpu.VMEM((WINDOW, BLOCK, BLOCK), bf16),
        pltpu.VMEM((BLOCK, PAIRS * BLOCK), bf16),
    ]
    if sums:
        scratch.append(pltpu.VMEM((WINDOW, BLOCK, BLOCK), f32))
    args = (*operators, *arrays)
    in_specs = [SMEM] + [VMEM] * (len(args) - 1)
    return call(kernel, name, outs, in_specs, args, scratch=scratch, limit=16)


def exchange(value, axes):
    return lax.all_to_all(value, axes, 0, 0, tiled=True)


def shards(guess, left_ops, right_ops, op_shift, op_mask, left_dims, right_dims):
    blocks = struct(WINDOW, BLOCK, BLOCK)
    half = struct(LINE, CHUNK, BLOCK)
    sent = struct(LINE, CHUNK, BLOCK, dtype=bf16)
    own_blocks = struct(OWN, BLOCK, BLOCK)
    pair = struct(2, CHUNK, BLOCK)
    scalar_row = struct(EXTRA, BLOCK)
    packet = struct(LINE, CHUNK + EXTRA, BLOCK)

    def partner(value, distance):
        return lax.ppermute(value, "wf", [(i, i ^ distance) for i in range(4)])

    def swapped(value):
        return lax.ppermute(value, "c", [(0, 1), (1, 0)])

    table = (2 * op_shift[None, :] + op_mask.T).reshape(-1)
    tail = EXTRA + CHUNK
    start, masks, one, own, three = call(
        norm_kernel, "norm",
        [own_blocks, pair, struct(SIDE + tail, BLOCK), struct(tail, BLOCK),
         struct(SIDE + tail, BLOCK)],
        [SMEM, SMEM, VMEM], (left_dims, right_dims, guess), limit=60,
    )
    one, two, three = partner(one, 1), partner(own, 2), partner(three, 3)
    held = struct(OWN, PAIRS, BLOCK, BLOCK, dtype=bf16)
    left, right = call(
        load_kernel, "load", [held, held], [HBM, HBM], (left_ops, right_ops),
        scratch=[pltpu.SemaphoreType.DMA((2 * OWN,))], limit=49,
    )
    operators = (table, left, right)

    def reduced(keep, give):
        (summed,) = small(join_kernel, "join", [sent], keep, swapped(give))
        parts = exchange(summed, LINE_AXES)
        (tiled,) = small(spread_kernel, "spread", [struct(CROSS, CHUNK, BLOCK)], parts)
        return exchange(tiled, CROSS_AXES)

    def gathered(packets):
        packets = exchange(packets, LINE_AXES)
        return packets, swapped(packets)

    keep, give, vector, pieces = step(
        first_kernel, "first", [half, half, blocks, pair], operators,
        (start, own, one, two, three),
    )
    packets, image_pieces = small(
        image_kernel, "image", [packet, pair], reduced(keep, give), masks, pieces
    )
    keep, give, direction, image, scalars = step(
        second_kernel, "second", [half, half, blocks, blocks, scalar_row], operators,
        (*gathered(packets), vector),
    )
    (packets,) = small(
        turned_kernel, "turned", [packet], reduced(keep, give), masks, pieces, image_pieces, scalars
    )
    sums, vector, direction, scalars = step(
        third_kernel, "third", [struct(256, BLOCK), own_blocks, own_blocks, scalar_row], operators,
        (*gathered(packets), vector, direction, image, scalars), sums=False,
    )
    sums = exchange(sums, (*OP_AXES, "wf"))
    result, energies = small(
        last_kernel, "last", [own_blocks, struct(2)], sums, vector, direction, scalars,
        out_specs=[VMEM, SMEM],
    )
    return result, energies


def solution(mesh):
    split = Mesh(mesh.devices.reshape(2, 2, 8, 2, 4), (*OP_AXES, "wf"))
    in_specs = (
        P("wf", None, None),
        P(OP_AXES, "wf", None, None),
        P(OP_AXES, "wf", None, None),
        P(OP_AXES),
        P(OP_AXES, "wf"),
        P(),
        P(),
    )
    out_specs = (P("wf", None, None), P())
    return jax.shard_map(
        shards, mesh=split, in_specs=in_specs, out_specs=out_specs, check_vma=False
    )
```

```python
import jax
import jax.numpy as jnp
from jax import lax
from jax.experimental import pallas as pl
from jax.experimental.pallas import tpu as pltpu
from jax.sharding import Mesh, PartitionSpec as P

EPS = 1e-06
SECTORS = 16
BLOCK = 128
PAIRS = 16
OWN = 4
WINDOW = 8
LINE = 16
CROSS = 8
HALF = 4
ROWS = 8
CHUNK = HALF * ROWS
PACKET = CHUNK + 1
SIDE = 2 * BLOCK
EXTRA = 8
ENTRIES = float(SECTORS * BLOCK * BLOCK)
LINE_AXES = ("y_far", "z")
CROSS_AXES = ("y_near", "wf")
OP_AXES = ("y_far", "y_near", "z", "c")

f32 = jnp.float32
bf16 = jnp.bfloat16


def dot(first, second, first_dim=1, second_dim=0):
    return lax.dot_general(
        first, second, (((first_dim,), (second_dim,)), ((), ())), preferred_element_type=f32
    )


def total(values):
    return jnp.sum(values, axis=(0, 1), keepdims=True)


def ratio(top, bottom):
    return jnp.where(bottom > 0, top / jnp.where(bottom > 0, bottom, 1.0), 0.0)


def place_here():
    chunk = lax.axis_index("y_far") * lax.axis_size("z") + lax.axis_index("z")
    first_row = pl.multiple_of(chunk * ROWS, ROWS)
    return lax.axis_index("wf"), HALF * lax.axis_index("c"), first_row


def sector_at(wf, position):
    base = OWN * wf - 2
    return base + ((position - base) & 7)


def live(left_dims, right_dims, sector, first_row, rows):
    held = jnp.clip(sector, 0, SECTORS - 1)
    inside = (sector >= 0) & (sector < SECTORS)
    height = jnp.where(inside, left_dims[held], 0)
    width = right_dims[SECTORS - 1 - held]
    row = lax.broadcasted_iota(jnp.int32, (rows, BLOCK), 0) + first_row
    column = lax.broadcasted_iota(jnp.int32, (rows, BLOCK), 1)
    return (row < height) & (column < width)


def pack(values, rows=EXTRA):
    lane = lax.broadcasted_iota(jnp.int32, (rows, BLOCK), 1)
    packed = jnp.zeros((rows, BLOCK), f32)
    for place, value in enumerate(values):
        packed = jnp.where(lane == place, value, packed)
    return packed


def lanes(rows, count):
    return [rows[:, place : place + 1] for place in range(count)]


def load_kernel(left_hbm, right_hbm, left, right, sems):
    copies = []
    for i in range(OWN):
        for source, target in ((left_hbm, left), (right_hbm, right)):
            copies.append(
                pltpu.make_async_copy(source.at[:, i], target.at[i], sems.at[len(copies)])
            )
    for copy in copies:
        copy.start()
    for copy in copies:
        copy.wait()


def norm_kernel(left_dims, right_dims, guess, start, masks, one, two, three):
    wf, base, first_row = place_here()
    sums = jnp.zeros((1, 1), f32)
    for i in range(OWN):
        mask = live(left_dims, right_dims, OWN * wf + i, 0, BLOCK)
        block = jnp.where(mask, guess[i], 0.0)
        start[i] = block
        sums = sums + total(block * block)
    odd = wf & 1
    for i in range(2):
        one[i * BLOCK : (i + 1) * BLOCK] = start[2 - 2 * odd + i]
        three[i * BLOCK : (i + 1) * BLOCK] = start[2 * odd + i]
    for out, first in ((one, SIDE), (two, 0), (three, SIDE)):
        out[first : first + EXTRA] = jnp.broadcast_to(sums, (EXTRA, BLOCK))
        out[first + EXTRA :] = start[:, pl.ds(first_row, ROWS)].reshape(CHUNK, BLOCK)
    for i in range(2):
        for k in range(HALF):
            mask = live(left_dims, right_dims, base + k + 8 * i, first_row, ROWS)
            masks[i, k * ROWS : (k + 1) * ROWS] = jnp.where(mask, 1.0, 0.0)


def half_step(table, left, right, vec_half, back, sector, index):
    for k in range(PAIRS):
        entry = table[index * PAIRS + k]
        position = (sector + (entry >> 1)) & 7
        weight = (entry & 1).astype(f32)
        value = dot(left[index, k].T, vec_half[position])
        back[:, k * BLOCK : (k + 1) * BLOCK] = (value * weight).astype(bf16)
    return dot(back[...], right[index].reshape(PAIRS * BLOCK, BLOCK))


def full_step(table, left, right, vec_half, back, sums, sector, index):
    middle = dot(left[index].reshape(PAIRS * BLOCK, BLOCK), vec_half[sector & 7])
    for k in range(PAIRS):
        entry = table[index * PAIRS + k]
        position = (sector + (entry >> 1)) & 7
        weight = (entry & 1).astype(f32)
        term = (middle[k * BLOCK : (k + 1) * BLOCK] * weight).astype(bf16)
        sums[position] += dot(term, right[index, k], 1, 1)
    sums[sector & 7] += half_step(table, left, right, vec_half, back, sector, index)


def full_sweep(table, left, right, vec_half, back, sums, keep, give):
    sums[...] = jnp.zeros_like(sums)
    first_sector = OWN * lax.axis_index("wf")
    for i in range(OWN):
        full_step(table, left, right, vec_half, back, sums, first_sector + i, i)
    core = lax.axis_index("c")
    for out, first in ((keep, HALF * core), (give, HALF - HALF * core)):
        for i in range(HALF):
            out[:, i * ROWS : (i + 1) * ROWS] = sums[first + i].reshape(LINE, ROWS, BLOCK)


def first_kernel(
    table, left, right, start, own, one, two, three, keep, give, vector, pieces,
    vec_half, back, sums,
):
    wf = lax.axis_index("wf")
    squares = (own[0:1, 0:1] + one[SIDE : SIDE + 1, 0:1]) + (
        two[0:1, 0:1] + three[SIDE : SIDE + 1, 0:1]
    )
    scale = 1.0 / jnp.sqrt(squares / ENTRIES + EPS)

    def put(position, block):
        sector = sector_at(wf, position)
        inside = (sector >= 0) & (sector < SECTORS)
        value = jnp.where(inside, block * scale, 0.0)
        vector[position] = value
        vec_half[position] = value.astype(bf16)

    odd = wf & 1
    for i in range(OWN):
        put(4 * odd + i, start[i])
    for i in range(2):
        rows = slice(i * BLOCK, (i + 1) * BLOCK)
        put(4 - 2 * odd + i, one[rows])
        put(6 - 6 * odd + i, three[rows])
    held = [own[EXTRA:], one[SIDE + EXTRA :], two[EXTRA:], three[SIDE + EXTRA :]]
    for place in range(2):
        source = (lax.axis_index("c") + 2 * place) ^ wf
        value = held[0]
        for other in range(1, 4):
            value = jnp.where(source == other, held[other], value)
        pieces[place] = value * scale
    full_sweep(table, left, right, vec_half, back, sums, keep, give)


def join_kernel(first, second, out):
    out[...] = (first[...] + second[...]).astype(out.dtype)


def spread_kernel(parts, out):
    summed = jnp.sum(parts[...].astype(f32), axis=0)
    for target in range(out.shape[0]):
        out[target] = summed


def combined(masks, parts):
    base = HALF * lax.axis_index("c")
    sums = []
    for other in range(4):
        sums.append((parts[other] + parts[4 + other]).reshape(HALF, ROWS, BLOCK))
    values = []
    for place in range(2):
        blocks = []
        for k in range(HALF):
            value = jnp.zeros((ROWS, BLOCK), f32)
            for other in range(4):
                here = sector_at(other, base + k) == base + k + 8 * place
                value = value + jnp.where(here, sums[other][k], 0.0)
            blocks.append(value)
        values.append(jnp.concatenate(blocks, axis=0) * masks[place])
    return values


def send(values, sums, out):
    wf, base, _ = place_here()
    chosen = []
    for k in range(HALF):
        sector = sector_at(wf, base + k)
        rows = slice(k * ROWS, (k + 1) * ROWS)
        block = jnp.where(sector == base + k, values[0][rows], 0.0)
        chosen.append(jnp.where(sector == base + k + 8, values[1][rows], block))
    chosen = jnp.concatenate(chosen, axis=0)
    packet = jnp.concatenate([chosen, pack(sums, 1)], axis=0)
    for target in range(LINE):
        out[target * PACKET : (target + 1) * PACKET] = packet


def image_kernel(parts, masks, pieces, out, image_pieces):
    image = combined(masks, parts)
    vec = [pieces[0], pieces[1]]

    def inner(first, second):
        return total(first[0] * second[0] + first[1] * second[1])

    vec_vec, vec_image = inner(vec, vec), inner(vec, image)
    part = ratio(vec_image, vec_vec)
    rest = [image[i] - part * vec[i] for i in range(2)]
    for i in range(2):
        image_pieces[i] = image[i]
    send(image, [vec_image, vec_vec, part, inner(rest, rest)], out)


def both(cores, count):
    ends = range(CHUNK, LINE * PACKET, PACKET)
    rows = [jnp.concatenate([held[end : end + 1] for end in ends], axis=0) for held in cores]
    return zip(*[lanes(held, count) for held in rows])


def add(values):
    return total(values[0]) + total(values[1])


def held_block(cores, position):
    firsts = range(ROWS * (position % HALF), LINE * PACKET, PACKET)
    own, other = (
        jnp.concatenate([held[first : first + ROWS] for first in firsts], axis=0) for held in cores
    )
    return jnp.where(lax.axis_index("c") == position // HALF, own, other)


def second_kernel(
    table, left, right, own, other, vector, keep, give, direction, image, scalars,
    vec_half, back, sums,
):
    cores = (own, other)
    vec_image, vec_vec, part, rest = both(cores, 4)
    ritz = add(vec_image) / ENTRIES
    norm = add([rest[i] + (ritz - part[i]) * (ritz - part[i]) * vec_vec[i] for i in range(2)])
    norm = norm / ENTRIES
    scale = 1.0 / jnp.sqrt(norm + EPS)
    scalars[...] = pack([ritz, norm])
    for position in range(WINDOW):
        held = held_block(cores, position)
        value = (held - ritz * vector[position]) * scale
        image[position] = held
        direction[position] = value
        vec_half[position] = value.astype(bf16)
    full_sweep(table, left, right, vec_half, back, sums, keep, give)


def turned_kernel(parts, masks, pieces, image_pieces, scalars, out):
    turned = combined(masks, parts)
    ritz, norm = scalars[0:1, 0:1], scalars[0:1, 1:2]
    scale = 1.0 / jnp.sqrt(norm + EPS)
    vec = [pieces[i] for i in range(2)]
    image = [image_pieces[i] for i in range(2)]
    turn = [(image[i] - ritz * vec[i]) * scale for i in range(2)]

    def inner(first, second):
        return total(first[0] * second[0] + first[1] * second[1])

    vec_vec, vec_turned = inner(vec, vec), inner(vec, turned)
    along = ratio(inner(vec, turn), vec_vec)
    new = [turn[i] - along * vec[i] for i in range(2)]
    on_vec = ratio(vec_turned, vec_vec)
    rest = [turned[i] - on_vec * vec[i] for i in range(2)]
    new_new = inner(new, new)
    on_new = ratio(inner(new, rest), new_new)
    rest = [rest[i] - on_new * new[i] for i in range(2)]
    sums = [
        vec_turned, inner(turn, image), inner(turn, turned),
        vec_vec, along, on_vec, new_new, on_new, inner(rest, rest),
    ]
    send(turned, sums, out)


def mixing(ritz, curvature, norm):
    gap = ritz - curvature
    lowest = 0.5 * (ritz + curvature) - jnp.sqrt(0.25 * gap * gap + norm)
    keep = curvature - lowest
    take = -jnp.sqrt(norm)
    scale = jnp.sqrt(keep * keep + take * take)
    return lowest, keep / scale, take / scale


def third_kernel(
    table, left, right, gathered, swapped, vector, direction, image, scalars,
    out, new_vector, new_direction, new_scalars, vec_half, back,
):
    cores = (gathered, swapped)
    wf = lax.axis_index("wf")
    (
        vec_turned, turn_image, turn_turned, vec_vec, along, on_vec, new_new, on_new, rest,
    ) = both(cores, 9)
    ritz, norm = scalars[0:1, 0:1], scalars[0:1, 1:2]
    curvature = add(turn_turned) / ENTRIES
    lowest, keep, take = mixing(ritz, curvature, norm)
    mixed = (add(vec_turned) + add(turn_image)) / ENTRIES
    next_ritz = keep * keep * ritz + keep * take * mixed + take * take * curvature
    first = keep * (ritz - next_ritz)
    second = keep * jnp.sqrt(norm + EPS) - take * next_ritz
    squares = []
    for i in range(2):
        on_first = first + second * along[i] + take * on_vec[i]
        on_second = second + take * on_new[i]
        square = on_first * on_first * vec_vec[i] + on_second * on_second * new_new[i]
        squares.append(square + take * take * rest[i])
    next_norm = add(squares) / ENTRIES
    scale = 1.0 / jnp.sqrt(next_norm + EPS)
    new_scalars[...] = pack([next_ritz, next_norm, lowest])
    for position in range(WINDOW):
        turned = held_block(cores, position)
        mixed_vec = keep * vector[position] + take * direction[position]
        mixed_image = keep * image[position] + take * turned
        value = (mixed_image - next_ritz * mixed_vec) * scale
        vec_half[position] = value.astype(bf16)

        @pl.when((position // 4) == (wf & 1))
        def _():
            new_vector[position % 4] = mixed_vec
            new_direction[position % 4] = value

    value = jnp.zeros((1, 1), f32)
    for i in range(OWN):
        half = half_step(table, left, right, vec_half, back, OWN * wf + i, i)
        value = value + total(half * new_direction[i])
    out[...] = jnp.broadcast_to(2.0 * value, out.shape)


def last_kernel(parts, vector, direction, scalars, out, energies):
    curvature = total(parts[:, 0:1]) / ENTRIES
    ritz, norm, first_lowest = lanes(scalars[0:1], 3)
    lowest, keep, take = mixing(ritz, curvature, norm)
    for i in range(OWN):
        out[i] = keep * vector[i] + take * direction[i]
    energies[0] = first_lowest[0, 0]
    energies[1] = lowest[0, 0]


HBM = pl.BlockSpec(memory_space=pltpu.HBM)
VMEM = pl.BlockSpec(memory_space=pltpu.VMEM)
SMEM = pl.BlockSpec(memory_space=pltpu.SMEM)
MIB = 1 << 20


def struct(*shape, dtype=f32):
    return jax.ShapeDtypeStruct(shape, dtype)


def call(kernel, name, outs, in_specs, args, out_specs=None, scratch=(), limit=6):
    return pl.pallas_call(
        kernel,
        name=name,
        in_specs=in_specs,
        out_specs=out_specs or [VMEM] * len(outs),
        out_shape=outs,
        scratch_shapes=scratch,
        compiler_params=pltpu.CompilerParams(vmem_limit_bytes=int(limit * MIB)),
    )(*args)


def small(kernel, name, outs, *arrays, out_specs=None):
    return call(kernel, name, outs, [VMEM] * len(arrays), arrays, out_specs)


def step(kernel, name, outs, operators, arrays, sums=True):
    scratch = [
        pltpu.VMEM((WINDOW, BLOCK, BLOCK), bf16),
        pltpu.VMEM((BLOCK, PAIRS * BLOCK), bf16),
    ]
    if sums:
        scratch.append(pltpu.VMEM((WINDOW, BLOCK, BLOCK), f32))
    args = (*operators, *arrays)
    in_specs = [SMEM] + [VMEM] * (len(args) - 1)
    return call(kernel, name, outs, in_specs, args, scratch=scratch, limit=16)


def exchange(value, axes):
    return lax.all_to_all(value, axes, 0, 0, tiled=True)


def shards(guess, left_ops, right_ops, op_shift, op_mask, left_dims, right_dims):
    blocks = struct(WINDOW, BLOCK, BLOCK)
    half = struct(LINE, CHUNK, BLOCK)
    sent = struct(LINE, CHUNK, BLOCK, dtype=bf16)
    own_blocks = struct(OWN, BLOCK, BLOCK)
    pair = struct(2, CHUNK, BLOCK)
    scalar_row = struct(EXTRA, BLOCK)
    packet = struct(LINE * PACKET, BLOCK)

    def partner(value, distance):
        return lax.ppermute(value, "wf", [(i, i ^ distance) for i in range(4)])

    def swapped(value):
        return lax.ppermute(value, "c", [(0, 1), (1, 0)])

    table = (2 * op_shift[None, :] + op_mask.T).reshape(-1)
    tail = EXTRA + CHUNK
    start, masks, one, own, three = call(
        norm_kernel, "norm",
        [own_blocks, pair, struct(SIDE + tail, BLOCK), struct(tail, BLOCK),
         struct(SIDE + tail, BLOCK)],
        [SMEM, SMEM, VMEM], (left_dims, right_dims, guess), limit=60,
    )
    one, two, three = partner(one, 1), partner(own, 2), partner(three, 3)
    held = struct(OWN, PAIRS, BLOCK, BLOCK, dtype=bf16)
    left, right = call(
        load_kernel, "load", [held, held], [HBM, HBM], (left_ops, right_ops),
        scratch=[pltpu.SemaphoreType.DMA((2 * OWN,))], limit=49,
    )
    operators = (table, left, right)

    def reduced(keep, give):
        (summed,) = small(join_kernel, "join", [sent], keep, swapped(give))
        parts = exchange(summed, LINE_AXES)
        (tiled,) = small(spread_kernel, "spread", [struct(CROSS, CHUNK, BLOCK)], parts)
        return exchange(tiled, CROSS_AXES)

    def gathered(packets):
        packets = exchange(packets.reshape(-1, 1, BLOCK), LINE_AXES).reshape(-1, BLOCK)
        return packets, swapped(packets)

    keep, give, vector, pieces = step(
        first_kernel, "first", [half, half, blocks, pair], operators,
        (start, own, one, two, three),
    )
    packets, image_pieces = small(
        image_kernel, "image", [packet, pair], reduced(keep, give), masks, pieces
    )
    keep, give, direction, image, scalars = step(
        second_kernel, "second", [half, half, blocks, blocks, scalar_row], operators,
        (*gathered(packets), vector),
    )
    (packets,) = small(
        turned_kernel, "turned", [packet], reduced(keep, give), masks, pieces, image_pieces, scalars
    )
    sums, vector, direction, scalars = step(
        third_kernel, "third", [struct(256, BLOCK), own_blocks, own_blocks, scalar_row], operators,
        (*gathered(packets), vector, direction, image, scalars), sums=False,
    )
    sums = exchange(sums, (*OP_AXES, "wf"))
    result, energies = small(
        last_kernel, "last", [own_blocks, struct(2)], sums, vector, direction, scalars,
        out_specs=[VMEM, SMEM],
    )
    return result, energies


def solution(mesh):
    split = Mesh(mesh.devices.reshape(2, 2, 8, 2, 4), (*OP_AXES, "wf"))
    in_specs = (
        P("wf", None, None),
        P(OP_AXES, "wf", None, None),
        P(OP_AXES, "wf", None, None),
        P(OP_AXES),
        P(OP_AXES, "wf"),
        P(),
        P(),
    )
    out_specs = (P("wf", None, None), P())
    return jax.shard_map(
        shards, mesh=split, in_specs=in_specs, out_specs=out_specs, check_vma=False
    )
```

```python
import jax
import jax.numpy as jnp
from jax import lax
from jax.experimental import pallas as pl
from jax.experimental.pallas import tpu as pltpu
from jax.sharding import Mesh, PartitionSpec as P

EPS = 1e-06
SECTORS = 16
BLOCK = 128
PAIRS = 16
OWN = 4
WINDOW = 8
LINE = 16
CROSS = 8
HALF = 4
ROWS = 8
CHUNK = HALF * ROWS
PACKET = CHUNK + 1
SIDE = 2 * BLOCK
EXTRA = 8
ENTRIES = float(SECTORS * BLOCK * BLOCK)
LINE_AXES = ("y_far", "z")
CROSS_AXES = ("y_near", "wf")
OP_AXES = ("y_far", "y_near", "z", "c")

f32 = jnp.float32
bf16 = jnp.bfloat16


def dot(first, second, first_dim=1, second_dim=0):
    return lax.dot_general(
        first, second, (((first_dim,), (second_dim,)), ((), ())), preferred_element_type=f32
    )


def total(values):
    return jnp.sum(values, axis=(0, 1), keepdims=True)


def ratio(top, bottom):
    return jnp.where(bottom > 0, top / jnp.where(bottom > 0, bottom, 1.0), 0.0)


def place_here():
    chunk = lax.axis_index("y_far") * lax.axis_size("z") + lax.axis_index("z")
    first_row = pl.multiple_of(chunk * ROWS, ROWS)
    return lax.axis_index("wf"), HALF * lax.axis_index("c"), first_row


def sector_at(wf, position):
    base = OWN * wf - 2
    return base + ((position - base) & 7)


def live(left_dims, right_dims, sector, first_row, rows):
    held = jnp.clip(sector, 0, SECTORS - 1)
    inside = (sector >= 0) & (sector < SECTORS)
    height = jnp.where(inside, left_dims[held], 0)
    width = right_dims[SECTORS - 1 - held]
    row = lax.broadcasted_iota(jnp.int32, (rows, BLOCK), 0) + first_row
    column = lax.broadcasted_iota(jnp.int32, (rows, BLOCK), 1)
    return (row < height) & (column < width)


def pack(values, rows=EXTRA):
    lane = lax.broadcasted_iota(jnp.int32, (rows, BLOCK), 1)
    packed = jnp.zeros((rows, BLOCK), f32)
    for place, value in enumerate(values):
        packed = jnp.where(lane == place, value, packed)
    return packed


def lanes(rows, count):
    return [rows[:, place : place + 1] for place in range(count)]


def load_kernel(left_hbm, right_hbm, left, right, sems):
    copies = []
    for i in range(OWN):
        for source, target in ((left_hbm, left), (right_hbm, right)):
            copies.append(
                pltpu.make_async_copy(source.at[:, i], target.at[i], sems.at[len(copies)])
            )
    for copy in copies:
        copy.start()
    for copy in copies:
        copy.wait()


def norm_kernel(left_dims, right_dims, guess, start, masks, one, two, three):
    wf, base, first_row = place_here()
    sums = jnp.zeros((1, 1), f32)
    for i in range(OWN):
        mask = live(left_dims, right_dims, OWN * wf + i, 0, BLOCK)
        block = jnp.where(mask, guess[i], 0.0)
        start[i] = block
        sums = sums + total(block * block)
    odd = wf & 1
    for i in range(2):
        one[i * BLOCK : (i + 1) * BLOCK] = start[2 - 2 * odd + i]
        three[i * BLOCK : (i + 1) * BLOCK] = start[2 * odd + i]
    for out, first in ((one, SIDE), (two, 0), (three, SIDE)):
        out[first : first + EXTRA] = jnp.broadcast_to(sums, (EXTRA, BLOCK))
        out[first + EXTRA :] = start[:, pl.ds(first_row, ROWS)].reshape(CHUNK, BLOCK)
    for i in range(2):
        for k in range(HALF):
            mask = live(left_dims, right_dims, base + k + 8 * i, first_row, ROWS)
            masks[i, k * ROWS : (k + 1) * ROWS] = jnp.where(mask, 1.0, 0.0)


def half_step(table, left, right, vec_half, back, sector, index):
    for k in range(PAIRS):
        entry = table[index * PAIRS + k]
        position = (sector + (entry >> 1)) & 7
        weight = (entry & 1).astype(f32)
        value = dot(left[index, k].T, vec_half[position])
        back[index & 1, :, k * BLOCK : (k + 1) * BLOCK] = (value * weight).astype(bf16)
    return dot(back[index & 1], right[index].reshape(PAIRS * BLOCK, BLOCK))


def middle_pair(left, vec_half, sector, index):
    zero = jnp.zeros((BLOCK, BLOCK), bf16)
    rows = [
        jnp.concatenate([vec_half[sector & 7], zero], axis=1),
        jnp.concatenate([zero, vec_half[(sector + 1) & 7]], axis=1),
    ]
    blocks = [left[index + i].reshape(PAIRS * BLOCK, BLOCK) for i in range(2)]
    return dot(jnp.concatenate(blocks, axis=1), jnp.concatenate(rows, axis=0))


def full_sweep(table, left, right, vec_half, back, sums, keep, give):
    sums[...] = jnp.zeros_like(sums)
    first_sector = OWN * lax.axis_index("wf")
    for pair in range(0, OWN, 2):
        middle = middle_pair(left, vec_half, first_sector + pair, pair)
        for i in range(2):
            sector, index = first_sector + pair + i, pair + i
            for k in range(PAIRS):
                entry = table[index * PAIRS + k]
                position = (sector + (entry >> 1)) & 7
                weight = (entry & 1).astype(f32)
                value = middle[k * BLOCK : (k + 1) * BLOCK, i * BLOCK : (i + 1) * BLOCK]
                sums[position] += dot((value * weight).astype(bf16), right[index, k], 1, 1)
        for i in range(2):
            sector, index = first_sector + pair + i, pair + i
            sums[sector & 7] += half_step(table, left, right, vec_half, back, sector, index)
    core = lax.axis_index("c")
    for out, first in ((keep, HALF * core), (give, HALF - HALF * core)):
        for i in range(HALF):
            out[:, i * ROWS : (i + 1) * ROWS] = sums[first + i].reshape(LINE, ROWS, BLOCK)


def first_kernel(
    table, left, right, start, own, one, two, three, keep, give, vector, pieces,
    vec_half, back, sums,
):
    wf = lax.axis_index("wf")
    squares = (own[0:1, 0:1] + one[SIDE : SIDE + 1, 0:1]) + (
        two[0:1, 0:1] + three[SIDE : SIDE + 1, 0:1]
    )
    scale = 1.0 / jnp.sqrt(squares / ENTRIES + EPS)

    def put(position, block):
        sector = sector_at(wf, position)
        inside = (sector >= 0) & (sector < SECTORS)
        value = jnp.where(inside, block * scale, 0.0)
        vector[position] = value
        vec_half[position] = value.astype(bf16)

    odd = wf & 1
    for i in range(OWN):
        put(4 * odd + i, start[i])
    for i in range(2):
        rows = slice(i * BLOCK, (i + 1) * BLOCK)
        put(4 - 2 * odd + i, one[rows])
        put(6 - 6 * odd + i, three[rows])
    held = [own[EXTRA:], one[SIDE + EXTRA :], two[EXTRA:], three[SIDE + EXTRA :]]
    for place in range(2):
        source = (lax.axis_index("c") + 2 * place) ^ wf
        value = held[0]
        for other in range(1, 4):
            value = jnp.where(source == other, held[other], value)
        pieces[place] = value * scale
    full_sweep(table, left, right, vec_half, back, sums, keep, give)


def join_kernel(first, second, out):
    out[...] = (first[...] + second[...]).astype(out.dtype)


def spread_kernel(parts, out):
    summed = jnp.sum(parts[...].astype(f32), axis=0)
    for target in range(out.shape[0]):
        out[target] = summed


def combined(masks, parts):
    base = HALF * lax.axis_index("c")
    sums = []
    for other in range(4):
        sums.append((parts[other] + parts[4 + other]).reshape(HALF, ROWS, BLOCK))
    values = []
    for place in range(2):
        blocks = []
        for k in range(HALF):
            value = jnp.zeros((ROWS, BLOCK), f32)
            for other in range(4):
                here = sector_at(other, base + k) == base + k + 8 * place
                value = value + jnp.where(here, sums[other][k], 0.0)
            blocks.append(value)
        values.append(jnp.concatenate(blocks, axis=0) * masks[place])
    return values


def send(values, sums, out):
    wf, base, _ = place_here()
    chosen = []
    for k in range(HALF):
        sector = sector_at(wf, base + k)
        rows = slice(k * ROWS, (k + 1) * ROWS)
        block = jnp.where(sector == base + k, values[0][rows], 0.0)
        chosen.append(jnp.where(sector == base + k + 8, values[1][rows], block))
    chosen = jnp.concatenate(chosen, axis=0)
    packet = jnp.concatenate([chosen, pack(sums, 1)], axis=0)
    for target in range(LINE):
        out[target * PACKET : (target + 1) * PACKET] = packet


def image_kernel(parts, masks, pieces, out, image_pieces):
    image = combined(masks, parts)
    vec = [pieces[0], pieces[1]]

    def inner(first, second):
        return total(first[0] * second[0] + first[1] * second[1])

    vec_vec, vec_image = inner(vec, vec), inner(vec, image)
    part = ratio(vec_image, vec_vec)
    rest = [image[i] - part * vec[i] for i in range(2)]
    for i in range(2):
        image_pieces[i] = image[i]
    send(image, [vec_image, vec_vec, part, inner(rest, rest)], out)


def both(cores, count):
    ends = range(CHUNK, LINE * PACKET, PACKET)
    rows = [jnp.concatenate([held[end : end + 1] for end in ends], axis=0) for held in cores]
    return zip(*[lanes(held, count) for held in rows])


def add(values):
    return total(values[0]) + total(values[1])


def held_block(cores, position):
    firsts = range(ROWS * (position % HALF), LINE * PACKET, PACKET)
    own, other = (
        jnp.concatenate([held[first : first + ROWS] for first in firsts], axis=0) for held in cores
    )
    return jnp.where(lax.axis_index("c") == position // HALF, own, other)


def second_kernel(
    table, left, right, own, other, vector, keep, give, direction, image, scalars,
    vec_half, back, sums,
):
    cores = (own, other)
    vec_image, vec_vec, part, rest = both(cores, 4)
    ritz = add(vec_image) / ENTRIES
    norm = add([rest[i] + (ritz - part[i]) * (ritz - part[i]) * vec_vec[i] for i in range(2)])
    norm = norm / ENTRIES
    scale = 1.0 / jnp.sqrt(norm + EPS)
    scalars[...] = pack([ritz, norm])
    for position in range(WINDOW):
        held = held_block(cores, position)
        value = (held - ritz * vector[position]) * scale
        image[position] = held
        direction[position] = value
        vec_half[position] = value.astype(bf16)
    full_sweep(table, left, right, vec_half, back, sums, keep, give)


def turned_kernel(parts, masks, pieces, image_pieces, scalars, out):
    turned = combined(masks, parts)
    ritz, norm = scalars[0:1, 0:1], scalars[0:1, 1:2]
    scale = 1.0 / jnp.sqrt(norm + EPS)
    vec = [pieces[i] for i in range(2)]
    image = [image_pieces[i] for i in range(2)]
    turn = [(image[i] - ritz * vec[i]) * scale for i in range(2)]

    def inner(first, second):
        return total(first[0] * second[0] + first[1] * second[1])

    vec_vec, vec_turned = inner(vec, vec), inner(vec, turned)
    along = ratio(inner(vec, turn), vec_vec)
    new = [turn[i] - along * vec[i] for i in range(2)]
    on_vec = ratio(vec_turned, vec_vec)
    rest = [turned[i] - on_vec * vec[i] for i in range(2)]
    new_new = inner(new, new)
    on_new = ratio(inner(new, rest), new_new)
    rest = [rest[i] - on_new * new[i] for i in range(2)]
    sums = [
        vec_turned, inner(turn, image), inner(turn, turned),
        vec_vec, along, on_vec, new_new, on_new, inner(rest, rest),
    ]
    send(turned, sums, out)


def mixing(ritz, curvature, norm):
    gap = ritz - curvature
    lowest = 0.5 * (ritz + curvature) - jnp.sqrt(0.25 * gap * gap + norm)
    keep = curvature - lowest
    take = -jnp.sqrt(norm)
    scale = jnp.sqrt(keep * keep + take * take)
    return lowest, keep / scale, take / scale


def third_kernel(
    table, left, right, gathered, swapped, vector, direction, image, scalars,
    out, new_vector, new_direction, new_scalars, vec_half, back,
):
    cores = (gathered, swapped)
    wf = lax.axis_index("wf")
    (
        vec_turned, turn_image, turn_turned, vec_vec, along, on_vec, new_new, on_new, rest,
    ) = both(cores, 9)
    ritz, norm = scalars[0:1, 0:1], scalars[0:1, 1:2]
    curvature = add(turn_turned) / ENTRIES
    lowest, keep, take = mixing(ritz, curvature, norm)
    mixed = (add(vec_turned) + add(turn_image)) / ENTRIES
    next_ritz = keep * keep * ritz + keep * take * mixed + take * take * curvature
    first = keep * (ritz - next_ritz)
    second = keep * jnp.sqrt(norm + EPS) - take * next_ritz
    squares = []
    for i in range(2):
        on_first = first + second * along[i] + take * on_vec[i]
        on_second = second + take * on_new[i]
        square = on_first * on_first * vec_vec[i] + on_second * on_second * new_new[i]
        squares.append(square + take * take * rest[i])
    next_norm = add(squares) / ENTRIES
    scale = 1.0 / jnp.sqrt(next_norm + EPS)
    new_scalars[...] = pack([next_ritz, next_norm, lowest])
    for position in range(WINDOW):
        turned = held_block(cores, position)
        mixed_vec = keep * vector[position] + take * direction[position]
        mixed_image = keep * image[position] + take * turned
        value = (mixed_image - next_ritz * mixed_vec) * scale
        vec_half[position] = value.astype(bf16)

        @pl.when((position // 4) == (wf & 1))
        def _():
            new_vector[position % 4] = mixed_vec
            new_direction[position % 4] = value

    value = jnp.zeros((1, 1), f32)
    for i in range(OWN):
        half = half_step(table, left, right, vec_half, back, OWN * wf + i, i)
        value = value + total(half * new_direction[i])
    out[...] = jnp.broadcast_to(2.0 * value, out.shape)


def last_kernel(parts, vector, direction, scalars, out, energies):
    curvature = total(parts[:, 0:1]) / ENTRIES
    ritz, norm, first_lowest = lanes(scalars[0:1], 3)
    lowest, keep, take = mixing(ritz, curvature, norm)
    for i in range(OWN):
        out[i] = keep * vector[i] + take * direction[i]
    energies[0] = first_lowest[0, 0]
    energies[1] = lowest[0, 0]


HBM = pl.BlockSpec(memory_space=pltpu.HBM)
VMEM = pl.BlockSpec(memory_space=pltpu.VMEM)
SMEM = pl.BlockSpec(memory_space=pltpu.SMEM)
MIB = 1 << 20


def struct(*shape, dtype=f32):
    return jax.ShapeDtypeStruct(shape, dtype)


def call(kernel, name, outs, in_specs, args, out_specs=None, scratch=(), limit=6):
    return pl.pallas_call(
        kernel,
        name=name,
        in_specs=in_specs,
        out_specs=out_specs or [VMEM] * len(outs),
        out_shape=outs,
        scratch_shapes=scratch,
        compiler_params=pltpu.CompilerParams(vmem_limit_bytes=int(limit * MIB)),
    )(*args)


def small(kernel, name, outs, *arrays, out_specs=None):
    return call(kernel, name, outs, [VMEM] * len(arrays), arrays, out_specs)


def step(kernel, name, outs, operators, arrays, sums=True):
    scratch = [
        pltpu.VMEM((WINDOW, BLOCK, BLOCK), bf16),
        pltpu.VMEM((2, BLOCK, PAIRS * BLOCK), bf16),
    ]
    if sums:
        scratch.append(pltpu.VMEM((WINDOW, BLOCK, BLOCK), f32))
    args = (*operators, *arrays)
    in_specs = [SMEM] + [VMEM] * (len(args) - 1)
    return call(kernel, name, outs, in_specs, args, scratch=scratch, limit=16)


def exchange(value, axes):
    return lax.all_to_all(value, axes, 0, 0, tiled=True)


def shards(guess, left_ops, right_ops, op_shift, op_mask, left_dims, right_dims):
    blocks = struct(WINDOW, BLOCK, BLOCK)
    half = struct(LINE, CHUNK, BLOCK)
    sent = struct(LINE, CHUNK, BLOCK, dtype=bf16)
    own_blocks = struct(OWN, BLOCK, BLOCK)
    pair = struct(2, CHUNK, BLOCK)
    scalar_row = struct(EXTRA, BLOCK)
    packet = struct(LINE * PACKET, BLOCK)

    def partner(value, distance):
        return lax.ppermute(value, "wf", [(i, i ^ distance) for i in range(4)])

    def swapped(value):
        return lax.ppermute(value, "c", [(0, 1), (1, 0)])

    table = (2 * op_shift[None, :] + op_mask.T).reshape(-1)
    tail = EXTRA + CHUNK
    start, masks, one, own, three = call(
        norm_kernel, "norm",
        [own_blocks, pair, struct(SIDE + tail, BLOCK), struct(tail, BLOCK),
         struct(SIDE + tail, BLOCK)],
        [SMEM, SMEM, VMEM], (left_dims, right_dims, guess), limit=60,
    )
    one, two, three = partner(one, 1), partner(own, 2), partner(three, 3)
    held = struct(OWN, PAIRS, BLOCK, BLOCK, dtype=bf16)
    left, right = call(
        load_kernel, "load", [held, held], [HBM, HBM], (left_ops, right_ops),
        scratch=[pltpu.SemaphoreType.DMA((2 * OWN,))], limit=49,
    )
    operators = (table, left, right)

    def reduced(keep, give):
        (summed,) = small(join_kernel, "join", [sent], keep, swapped(give))
        parts = exchange(summed, LINE_AXES)
        (tiled,) = small(spread_kernel, "spread", [struct(CROSS, CHUNK, BLOCK)], parts)
        return exchange(tiled, CROSS_AXES)

    def gathered(packets):
        packets = exchange(packets.reshape(-1, 1, BLOCK), LINE_AXES).reshape(-1, BLOCK)
        return packets, swapped(packets)

    keep, give, vector, pieces = step(
        first_kernel, "first", [half, half, blocks, pair], operators,
        (start, own, one, two, three),
    )
    packets, image_pieces = small(
        image_kernel, "image", [packet, pair], reduced(keep, give), masks, pieces
    )
    keep, give, direction, image, scalars = step(
        second_kernel, "second", [half, half, blocks, blocks, scalar_row], operators,
        (*gathered(packets), vector),
    )
    (packets,) = small(
        turned_kernel, "turned", [packet], reduced(keep, give), masks, pieces, image_pieces, scalars
    )
    sums, vector, direction, scalars = step(
        third_kernel, "third", [struct(256, BLOCK), own_blocks, own_blocks, scalar_row], operators,
        (*gathered(packets), vector, direction, image, scalars), sums=False,
    )
    sums = exchange(sums, (*OP_AXES, "wf"))
    result, energies = small(
        last_kernel, "last", [own_blocks, struct(2)], sums, vector, direction, scalars,
        out_specs=[VMEM, SMEM],
    )
    return result, energies


def solution(mesh):
    split = Mesh(mesh.devices.reshape(2, 2, 8, 2, 4), (*OP_AXES, "wf"))
    in_specs = (
        P("wf", None, None),
        P(OP_AXES, "wf", None, None),
        P(OP_AXES, "wf", None, None),
        P(OP_AXES),
        P(OP_AXES, "wf"),
        P(),
        P(),
    )
    out_specs = (P("wf", None, None), P())
    return jax.shard_map(
        shards, mesh=split, in_specs=in_specs, out_specs=out_specs, check_vma=False
    )
```

```python
import jax
import jax.numpy as jnp
from jax import lax
from jax.experimental import pallas as pl
from jax.experimental.pallas import tpu as pltpu
from jax.sharding import Mesh, PartitionSpec as P

EPS = 1e-06
SECTORS = 16
BLOCK = 128
PAIRS = 16
OWN = 4
WINDOW = 8
LINE = 16
CROSS = 8
HALF = 4
ROWS = 8
CHUNK = HALF * ROWS
PACKET = CHUNK + 1
SIDE = 2 * BLOCK
EXTRA = 8
ENTRIES = float(SECTORS * BLOCK * BLOCK)
LINE_AXES = ("y_near", "z")
CROSS_AXES = ("y_far", "y_near", "wf")
CROSS_ROWS = ((0, 3), (1, 2))
OP_AXES = ("y_far", "y_near", "z", "c")

f32 = jnp.float32
bf16 = jnp.bfloat16


def dot(first, second, first_dim=1, second_dim=0):
    return lax.dot_general(
        first, second, (((first_dim,), (second_dim,)), ((), ())), preferred_element_type=f32
    )


def total(values):
    return jnp.sum(values, axis=(0, 1), keepdims=True)


def ratio(top, bottom):
    return jnp.where(bottom > 0, top / jnp.where(bottom > 0, bottom, 1.0), 0.0)


def half_of_line():
    return lax.axis_index("y_near") ^ lax.axis_index("y_far")


def place_here():
    chunk = half_of_line() * lax.axis_size("z") + lax.axis_index("z")
    first_row = pl.multiple_of(chunk * ROWS, ROWS)
    return lax.axis_index("wf"), HALF * lax.axis_index("c"), first_row


def sector_at(wf, position):
    base = OWN * wf - 2
    return base + ((position - base) & 7)


def live(left_dims, right_dims, sector, first_row, rows):
    held = jnp.clip(sector, 0, SECTORS - 1)
    inside = (sector >= 0) & (sector < SECTORS)
    height = jnp.where(inside, left_dims[held], 0)
    width = right_dims[SECTORS - 1 - held]
    row = lax.broadcasted_iota(jnp.int32, (rows, BLOCK), 0) + first_row
    column = lax.broadcasted_iota(jnp.int32, (rows, BLOCK), 1)
    return (row < height) & (column < width)


def pack(values, rows=EXTRA):
    lane = lax.broadcasted_iota(jnp.int32, (rows, BLOCK), 1)
    packed = jnp.zeros((rows, BLOCK), f32)
    for place, value in enumerate(values):
        packed = jnp.where(lane == place, value, packed)
    return packed


def lanes(rows, count):
    return [rows[:, place : place + 1] for place in range(count)]


def load_kernel(left_hbm, right_hbm, left, right, sems):
    copies = []
    for i in range(OWN):
        for source, target in ((left_hbm, left), (right_hbm, right)):
            copies.append(
                pltpu.make_async_copy(source.at[:, i], target.at[i], sems.at[len(copies)])
            )
    for copy in copies:
        copy.start()
    for copy in copies:
        copy.wait()


def norm_kernel(left_dims, right_dims, guess, start, masks, one, two, three):
    wf, base, first_row = place_here()
    sums = jnp.zeros((1, 1), f32)
    for i in range(OWN):
        mask = live(left_dims, right_dims, OWN * wf + i, 0, BLOCK)
        block = jnp.where(mask, guess[i], 0.0)
        start[i] = block
        sums = sums + total(block * block)
    odd = wf & 1
    for i in range(2):
        one[i * BLOCK : (i + 1) * BLOCK] = start[2 - 2 * odd + i]
        three[i * BLOCK : (i + 1) * BLOCK] = start[2 * odd + i]
    for out, first in ((one, SIDE), (two, 0), (three, SIDE)):
        out[first : first + EXTRA] = jnp.broadcast_to(sums, (EXTRA, BLOCK))
        out[first + EXTRA :] = start[:, pl.ds(first_row, ROWS)].reshape(CHUNK, BLOCK)
    for i in range(2):
        for k in range(HALF):
            mask = live(left_dims, right_dims, base + k + 8 * i, first_row, ROWS)
            masks[i, k * ROWS : (k + 1) * ROWS] = jnp.where(mask, 1.0, 0.0)


def half_step(table, left, right, vec_half, back, sector, index):
    for k in range(PAIRS):
        entry = table[index * PAIRS + k]
        position = (sector + (entry >> 1)) & 7
        weight = (entry & 1).astype(f32)
        value = dot(left[index, k].T, vec_half[position])
        back[index & 1, :, k * BLOCK : (k + 1) * BLOCK] = (value * weight).astype(bf16)
    return dot(back[index & 1], right[index].reshape(PAIRS * BLOCK, BLOCK))


def middle_pair(left, vec_half, sector, index):
    zero = jnp.zeros((BLOCK, BLOCK), bf16)
    rows = [
        jnp.concatenate([vec_half[sector & 7], zero], axis=1),
        jnp.concatenate([zero, vec_half[(sector + 1) & 7]], axis=1),
    ]
    blocks = [left[index + i].reshape(PAIRS * BLOCK, BLOCK) for i in range(2)]
    return dot(jnp.concatenate(blocks, axis=1), jnp.concatenate(rows, axis=0))


def full_sweep(table, left, right, vec_half, back, sums, keep, give):
    sums[...] = jnp.zeros_like(sums)
    first_sector = OWN * lax.axis_index("wf")
    for pair in range(0, OWN, 2):
        middle = middle_pair(left, vec_half, first_sector + pair, pair)
        for i in range(2):
            sector, index = first_sector + pair + i, pair + i
            for k in range(PAIRS):
                entry = table[index * PAIRS + k]
                position = (sector + (entry >> 1)) & 7
                weight = (entry & 1).astype(f32)
                value = middle[k * BLOCK : (k + 1) * BLOCK, i * BLOCK : (i + 1) * BLOCK]
                sums[position] += dot((value * weight).astype(bf16), right[index, k], 1, 1)
        for i in range(2):
            sector, index = first_sector + pair + i, pair + i
            sums[sector & 7] += half_step(table, left, right, vec_half, back, sector, index)
    core = lax.axis_index("c")
    for out, first in ((keep, HALF * core), (give, HALF - HALF * core)):
        for i in range(HALF):
            for near in range(2):
                half = pl.multiple_of((near ^ lax.axis_index("y_far")) * (BLOCK // 2), BLOCK // 2)
                rows = sums[first + i, pl.ds(half, BLOCK // 2)].reshape(LINE // 2, ROWS, BLOCK)
                peers = slice(near * LINE // 2, (near + 1) * LINE // 2)
                out[peers, i * ROWS : (i + 1) * ROWS] = rows


def first_kernel(
    table, left, right, start, own, one, two, three, keep, give, vector, pieces,
    vec_half, back, sums,
):
    wf = lax.axis_index("wf")
    squares = (own[0:1, 0:1] + one[SIDE : SIDE + 1, 0:1]) + (
        two[0:1, 0:1] + three[SIDE : SIDE + 1, 0:1]
    )
    scale = 1.0 / jnp.sqrt(squares / ENTRIES + EPS)

    def put(position, block):
        sector = sector_at(wf, position)
        inside = (sector >= 0) & (sector < SECTORS)
        value = jnp.where(inside, block * scale, 0.0)
        vector[position] = value
        vec_half[position] = value.astype(bf16)

    odd = wf & 1
    for i in range(OWN):
        put(4 * odd + i, start[i])
    for i in range(2):
        rows = slice(i * BLOCK, (i + 1) * BLOCK)
        put(4 - 2 * odd + i, one[rows])
        put(6 - 6 * odd + i, three[rows])
    held = [own[EXTRA:], one[SIDE + EXTRA :], two[EXTRA:], three[SIDE + EXTRA :]]
    for place in range(2):
        source = (lax.axis_index("c") + 2 * place) ^ wf
        value = held[0]
        for other in range(1, 4):
            value = jnp.where(source == other, held[other], value)
        pieces[place] = value * scale
    full_sweep(table, left, right, vec_half, back, sums, keep, give)


def join_kernel(first, second, out):
    out[...] = (first[...] + second[...]).astype(out.dtype)


def spread_kernel(parts, out):
    summed = jnp.sum(parts[...].astype(f32), axis=0)
    for target in range(out.shape[0]):
        out[target] = summed


def combined(masks, parts):
    base = HALF * lax.axis_index("c")
    sums = []
    for other in range(4):
        sums.append((parts[other] + parts[4 + other]).reshape(HALF, ROWS, BLOCK))
    values = []
    for place in range(2):
        blocks = []
        for k in range(HALF):
            value = jnp.zeros((ROWS, BLOCK), f32)
            for other in range(4):
                here = sector_at(other, base + k) == base + k + 8 * place
                value = value + jnp.where(here, sums[other][k], 0.0)
            blocks.append(value)
        values.append(jnp.concatenate(blocks, axis=0) * masks[place])
    return values


def send(values, sums, out):
    wf, base, _ = place_here()
    chosen = []
    for k in range(HALF):
        sector = sector_at(wf, base + k)
        rows = slice(k * ROWS, (k + 1) * ROWS)
        block = jnp.where(sector == base + k, values[0][rows], 0.0)
        chosen.append(jnp.where(sector == base + k + 8, values[1][rows], block))
    chosen = jnp.concatenate(chosen, axis=0)
    packet = jnp.concatenate([chosen, pack(sums, 1)], axis=0)
    for target in range(LINE):
        out[target * PACKET : (target + 1) * PACKET] = packet


def image_kernel(parts, masks, pieces, out, image_pieces):
    image = combined(masks, parts)
    vec = [pieces[0], pieces[1]]

    def inner(first, second):
        return total(first[0] * second[0] + first[1] * second[1])

    vec_vec, vec_image = inner(vec, vec), inner(vec, image)
    part = ratio(vec_image, vec_vec)
    rest = [image[i] - part * vec[i] for i in range(2)]
    for i in range(2):
        image_pieces[i] = image[i]
    send(image, [vec_image, vec_vec, part, inner(rest, rest)], out)


def line_rows(held, first, rows):
    places = range(first, LINE * PACKET, PACKET)
    parts = [held[place : place + rows] for place in places]
    near, far = (jnp.concatenate(parts[i : i + LINE // 2], axis=0) for i in (0, LINE // 2))
    swap = lax.axis_index("y_far") == 1
    return jnp.concatenate([jnp.where(swap, far, near), jnp.where(swap, near, far)], axis=0)


def both(cores, count):
    return zip(*[lanes(line_rows(held, CHUNK, 1), count) for held in cores])


def add(values):
    return total(values[0]) + total(values[1])


def held_block(cores, position):
    own, other = (line_rows(held, ROWS * (position % HALF), ROWS) for held in cores)
    return jnp.where(lax.axis_index("c") == position // HALF, own, other)


def second_kernel(
    table, left, right, own, other, vector, keep, give, direction, image, scalars,
    vec_half, back, sums,
):
    cores = (own, other)
    vec_image, vec_vec, part, rest = both(cores, 4)
    ritz = add(vec_image) / ENTRIES
    norm = add([rest[i] + (ritz - part[i]) * (ritz - part[i]) * vec_vec[i] for i in range(2)])
    norm = norm / ENTRIES
    scale = 1.0 / jnp.sqrt(norm + EPS)
    scalars[...] = pack([ritz, norm])
    for position in range(WINDOW):
        held = held_block(cores, position)
        value = (held - ritz * vector[position]) * scale
        image[position] = held
        direction[position] = value
        vec_half[position] = value.astype(bf16)
    full_sweep(table, left, right, vec_half, back, sums, keep, give)


def turned_kernel(parts, masks, pieces, image_pieces, scalars, out):
    turned = combined(masks, parts)
    ritz, norm = scalars[0:1, 0:1], scalars[0:1, 1:2]
    scale = 1.0 / jnp.sqrt(norm + EPS)
    vec = [pieces[i] for i in range(2)]
    image = [image_pieces[i] for i in range(2)]
    turn = [(image[i] - ritz * vec[i]) * scale for i in range(2)]

    def inner(first, second):
        return total(first[0] * second[0] + first[1] * second[1])

    vec_vec, vec_turned = inner(vec, vec), inner(vec, turned)
    along = ratio(inner(vec, turn), vec_vec)
    new = [turn[i] - along * vec[i] for i in range(2)]
    on_vec = ratio(vec_turned, vec_vec)
    rest = [turned[i] - on_vec * vec[i] for i in range(2)]
    new_new = inner(new, new)
    on_new = ratio(inner(new, rest), new_new)
    rest = [rest[i] - on_new * new[i] for i in range(2)]
    sums = [
        vec_turned, inner(turn, image), inner(turn, turned),
        vec_vec, along, on_vec, new_new, on_new, inner(rest, rest),
    ]
    send(turned, sums, out)


def mixing(ritz, curvature, norm):
    gap = ritz - curvature
    lowest = 0.5 * (ritz + curvature) - jnp.sqrt(0.25 * gap * gap + norm)
    keep = curvature - lowest
    take = -jnp.sqrt(norm)
    scale = jnp.sqrt(keep * keep + take * take)
    return lowest, keep / scale, take / scale


def third_kernel(
    table, left, right, gathered, swapped, vector, direction, image, scalars,
    out, new_vector, new_direction, new_scalars, vec_half, back,
):
    cores = (gathered, swapped)
    wf = lax.axis_index("wf")
    (
        vec_turned, turn_image, turn_turned, vec_vec, along, on_vec, new_new, on_new, rest,
    ) = both(cores, 9)
    ritz, norm = scalars[0:1, 0:1], scalars[0:1, 1:2]
    curvature = add(turn_turned) / ENTRIES
    lowest, keep, take = mixing(ritz, curvature, norm)
    mixed = (add(vec_turned) + add(turn_image)) / ENTRIES
    next_ritz = keep * keep * ritz + keep * take * mixed + take * take * curvature
    first = keep * (ritz - next_ritz)
    second = keep * jnp.sqrt(norm + EPS) - take * next_ritz
    squares = []
    for i in range(2):
        on_first = first + second * along[i] + take * on_vec[i]
        on_second = second + take * on_new[i]
        square = on_first * on_first * vec_vec[i] + on_second * on_second * new_new[i]
        squares.append(square + take * take * rest[i])
    next_norm = add(squares) / ENTRIES
    scale = 1.0 / jnp.sqrt(next_norm + EPS)
    new_scalars[...] = pack([next_ritz, next_norm, lowest])
    for position in range(WINDOW):
        turned = held_block(cores, position)
        mixed_vec = keep * vector[position] + take * direction[position]
        mixed_image = keep * image[position] + take * turned
        value = (mixed_image - next_ritz * mixed_vec) * scale
        vec_half[position] = value.astype(bf16)

        @pl.when((position // 4) == (wf & 1))
        def _():
            new_vector[position % 4] = mixed_vec
            new_direction[position % 4] = value

    value = jnp.zeros((1, 1), f32)
    for i in range(OWN):
        half = half_step(table, left, right, vec_half, back, OWN * wf + i, i)
        value = value + total(half * new_direction[i])
    out[...] = jnp.broadcast_to(2.0 * value, out.shape)


def last_kernel(parts, vector, direction, scalars, out, energies):
    curvature = total(parts[:, 0:1]) / ENTRIES
    ritz, norm, first_lowest = lanes(scalars[0:1], 3)
    lowest, keep, take = mixing(ritz, curvature, norm)
    for i in range(OWN):
        out[i] = keep * vector[i] + take * direction[i]
    energies[0] = first_lowest[0, 0]
    energies[1] = lowest[0, 0]


HBM = pl.BlockSpec(memory_space=pltpu.HBM)
VMEM = pl.BlockSpec(memory_space=pltpu.VMEM)
SMEM = pl.BlockSpec(memory_space=pltpu.SMEM)
MIB = 1 << 20


def struct(*shape, dtype=f32):
    return jax.ShapeDtypeStruct(shape, dtype)


def call(kernel, name, outs, in_specs, args, out_specs=None, scratch=(), limit=6):
    return pl.pallas_call(
        kernel,
        name=name,
        in_specs=in_specs,
        out_specs=out_specs or [VMEM] * len(outs),
        out_shape=outs,
        scratch_shapes=scratch,
        compiler_params=pltpu.CompilerParams(vmem_limit_bytes=int(limit * MIB)),
    )(*args)


def small(kernel, name, outs, *arrays, out_specs=None):
    return call(kernel, name, outs, [VMEM] * len(arrays), arrays, out_specs)


def step(kernel, name, outs, operators, arrays, sums=True):
    scratch = [
        pltpu.VMEM((WINDOW, BLOCK, BLOCK), bf16),
        pltpu.VMEM((2, BLOCK, PAIRS * BLOCK), bf16),
    ]
    if sums:
        scratch.append(pltpu.VMEM((WINDOW, BLOCK, BLOCK), f32))
    args = (*operators, *arrays)
    in_specs = [SMEM] + [VMEM] * (len(args) - 1)
    return call(kernel, name, outs, in_specs, args, scratch=scratch, limit=16)


def exchange(value, axes, groups=None):
    return lax.all_to_all(value, axes, 0, 0, axis_index_groups=groups, tiled=True)


def shards(guess, left_ops, right_ops, op_shift, op_mask, left_dims, right_dims):
    blocks = struct(WINDOW, BLOCK, BLOCK)
    half = struct(LINE, CHUNK, BLOCK)
    sent = struct(LINE, CHUNK, BLOCK, dtype=bf16)
    own_blocks = struct(OWN, BLOCK, BLOCK)
    pair = struct(2, CHUNK, BLOCK)
    scalar_row = struct(EXTRA, BLOCK)
    packet = struct(LINE * PACKET, BLOCK)

    def partner(value, distance):
        return lax.ppermute(value, "wf", [(i, i ^ distance) for i in range(4)])

    def swapped(value):
        return lax.ppermute(value, "c", [(0, 1), (1, 0)])

    table = (2 * op_shift[None, :] + op_mask.T).reshape(-1)
    tail = EXTRA + CHUNK
    start, masks, one, own, three = call(
        norm_kernel, "norm",
        [own_blocks, pair, struct(SIDE + tail, BLOCK), struct(tail, BLOCK),
         struct(SIDE + tail, BLOCK)],
        [SMEM, SMEM, VMEM], (left_dims, right_dims, guess), limit=60,
    )
    one, two, three = partner(one, 1), partner(own, 2), partner(three, 3)
    held = struct(OWN, PAIRS, BLOCK, BLOCK, dtype=bf16)
    left, right = call(
        load_kernel, "load", [held, held], [HBM, HBM], (left_ops, right_ops),
        scratch=[pltpu.SemaphoreType.DMA((2 * OWN,))], limit=49,
    )
    operators = (table, left, right)

    def reduced(keep, give):
        (summed,) = small(join_kernel, "join", [sent], keep, swapped(give))
        parts = exchange(summed, LINE_AXES)
        (tiled,) = small(spread_kernel, "spread", [struct(CROSS, CHUNK, BLOCK)], parts)
        groups = [[4 * row + wf for row in rows for wf in range(4)] for rows in CROSS_ROWS]
        return exchange(tiled, CROSS_AXES, groups)

    def gathered(packets):
        packets = exchange(packets.reshape(-1, 1, BLOCK), LINE_AXES).reshape(-1, BLOCK)
        return packets, swapped(packets)

    keep, give, vector, pieces = step(
        first_kernel, "first", [half, half, blocks, pair], operators,
        (start, own, one, two, three),
    )
    packets, image_pieces = small(
        image_kernel, "image", [packet, pair], reduced(keep, give), masks, pieces
    )
    keep, give, direction, image, scalars = step(
        second_kernel, "second", [half, half, blocks, blocks, scalar_row], operators,
        (*gathered(packets), vector),
    )
    (packets,) = small(
        turned_kernel, "turned", [packet], reduced(keep, give), masks, pieces, image_pieces, scalars
    )
    sums, vector, direction, scalars = step(
        third_kernel, "third", [struct(256, BLOCK), own_blocks, own_blocks, scalar_row], operators,
        (*gathered(packets), vector, direction, image, scalars), sums=False,
    )
    sums = exchange(sums, (*OP_AXES, "wf"))
    result, energies = small(
        last_kernel, "last", [own_blocks, struct(2)], sums, vector, direction, scalars,
        out_specs=[VMEM, SMEM],
    )
    return result, energies


def solution(mesh):
    split = Mesh(mesh.devices.reshape(2, 2, 8, 2, 4), (*OP_AXES, "wf"))
    in_specs = (
        P("wf", None, None),
        P(OP_AXES, "wf", None, None),
        P(OP_AXES, "wf", None, None),
        P(OP_AXES),
        P(OP_AXES, "wf"),
        P(),
        P(),
    )
    out_specs = (P("wf", None, None), P())
    return jax.shard_map(
        shards, mesh=split, in_specs=in_specs, out_specs=out_specs, check_vma=False
    )
```

```python
import jax
import jax.numpy as jnp
from jax import lax
from jax.experimental import pallas as pl
from jax.experimental.pallas import tpu as pltpu
from jax.sharding import Mesh, PartitionSpec as P

EPS = 1e-06
SECTORS = 16
BLOCK = 128
PAIRS = 16
OWN = 4
WINDOW = 8
LINE = 16
CROSS = 8
HALF = 4
ROWS = 8
CHUNK = HALF * ROWS
PACKET = CHUNK + 1
SIDE = 2 * BLOCK
EXTRA = 8
ENTRIES = float(SECTORS * BLOCK * BLOCK)
ALL_AXES = ("y", "z", "c", "wf")
LINE_ROWS = ((0, 1), (3, 2))
CROSS_ROWS = ((0, 3), (1, 2))
OP_AXES = ("y", "z", "c")

f32 = jnp.float32
bf16 = jnp.bfloat16


def dot(first, second, first_dim=1, second_dim=0):
    return lax.dot_general(
        first, second, (((first_dim,), (second_dim,)), ((), ())), preferred_element_type=f32
    )


def total(values):
    return jnp.sum(values, axis=(0, 1), keepdims=True)


def ratio(top, bottom):
    return jnp.where(bottom > 0, top / jnp.where(bottom > 0, bottom, 1.0), 0.0)


def line_order(core):
    return [(half, z) for half in range(2) for z in range(8)]


def place_here():
    y, z, core = (lax.axis_index(axis) for axis in OP_AXES)
    half = (y ^ (y // 2)) & 1
    chunk = half * 8 + z
    first_row = pl.multiple_of(chunk * ROWS, ROWS)
    return lax.axis_index("wf"), HALF * core, first_row


def sector_at(wf, position):
    base = OWN * wf - 2
    return base + ((position - base) & 7)


def live(left_dims, right_dims, sector, first_row, rows):
    held = jnp.clip(sector, 0, SECTORS - 1)
    inside = (sector >= 0) & (sector < SECTORS)
    height = jnp.where(inside, left_dims[held], 0)
    width = right_dims[SECTORS - 1 - held]
    row = lax.broadcasted_iota(jnp.int32, (rows, BLOCK), 0) + first_row
    column = lax.broadcasted_iota(jnp.int32, (rows, BLOCK), 1)
    return (row < height) & (column < width)


def pack(values, rows=EXTRA):
    lane = lax.broadcasted_iota(jnp.int32, (rows, BLOCK), 1)
    packed = jnp.zeros((rows, BLOCK), f32)
    for place, value in enumerate(values):
        packed = jnp.where(lane == place, value, packed)
    return packed


def lanes(rows, count):
    return [rows[:, place : place + 1] for place in range(count)]


def load_kernel(left_hbm, right_hbm, left, right, sems):
    copies = []
    for i in range(OWN):
        for source, target in ((left_hbm, left), (right_hbm, right)):
            copies.append(
                pltpu.make_async_copy(source.at[:, i], target.at[i], sems.at[len(copies)])
            )
    for copy in copies:
        copy.start()
    for copy in copies:
        copy.wait()


def norm_kernel(left_dims, right_dims, guess, start, masks, one, two, three):
    wf, base, first_row = place_here()
    sums = jnp.zeros((1, 1), f32)
    for i in range(OWN):
        mask = live(left_dims, right_dims, OWN * wf + i, 0, BLOCK)
        block = jnp.where(mask, guess[i], 0.0)
        start[i] = block
        sums = sums + total(block * block)
    odd = wf & 1
    for i in range(2):
        one[i * BLOCK : (i + 1) * BLOCK] = start[2 - 2 * odd + i]
        three[i * BLOCK : (i + 1) * BLOCK] = start[2 * odd + i]
    for out, first in ((one, SIDE), (two, 0), (three, SIDE)):
        out[first : first + EXTRA] = jnp.broadcast_to(sums, (EXTRA, BLOCK))
        out[first + EXTRA :] = start[:, pl.ds(first_row, ROWS)].reshape(CHUNK, BLOCK)
    for i in range(2):
        for k in range(HALF):
            mask = live(left_dims, right_dims, base + k + 8 * i, first_row, ROWS)
            masks[i, k * ROWS : (k + 1) * ROWS] = jnp.where(mask, 1.0, 0.0)


def half_step(shift, mask, left, right, vec_half, back, sector, index):
    for k in range(PAIRS):
        position = (sector + shift[k]) & 7
        weight = mask[index, k].astype(f32)
        value = dot(left[index, k].T, vec_half[position])
        back[index & 1, :, k * BLOCK : (k + 1) * BLOCK] = (value * weight).astype(bf16)
    return dot(back[index & 1], right[index].reshape(PAIRS * BLOCK, BLOCK))


def middle_pair(left, vec_half, sector, index):
    zero = jnp.zeros((BLOCK, BLOCK), bf16)
    rows = [
        jnp.concatenate([vec_half[sector & 7], zero], axis=1),
        jnp.concatenate([zero, vec_half[(sector + 1) & 7]], axis=1),
    ]
    blocks = [left[index + i].reshape(PAIRS * BLOCK, BLOCK) for i in range(2)]
    return dot(jnp.concatenate(blocks, axis=1), jnp.concatenate(rows, axis=0))


def full_sweep(shift, mask, left, right, vec_half, back, sums, keep, give):
    sums[...] = jnp.zeros_like(sums)
    first_sector = OWN * lax.axis_index("wf")
    for pair in range(0, OWN, 2):
        middle = middle_pair(left, vec_half, first_sector + pair, pair)
        for i in range(2):
            sector, index = first_sector + pair + i, pair + i
            for k in range(PAIRS):
                position = (sector + shift[k]) & 7
                weight = mask[index, k].astype(f32)
                value = middle[k * BLOCK : (k + 1) * BLOCK, i * BLOCK : (i + 1) * BLOCK]
                sums[position] += dot((value * weight).astype(bf16), right[index, k], 1, 1)
        for i in range(2):
            sector, index = first_sector + pair + i, pair + i
            sums[sector & 7] += half_step(shift, mask, left, right, vec_half, back, sector, index)
    core = lax.axis_index("c")
    for out, first in ((keep, HALF * core), (give, HALF - HALF * core)):
        for i in range(HALF):
            rows = sums[first + i].reshape(LINE, ROWS, BLOCK)
            out[:, i * ROWS : (i + 1) * ROWS] = rows


def first_kernel(
    shift, mask, left, right, start, own, one, two, three, keep, give, vector, pieces,
    vec_half, back, sums,
):
    wf = lax.axis_index("wf")
    squares = (own[0:1, 0:1] + one[SIDE : SIDE + 1, 0:1]) + (
        two[0:1, 0:1] + three[SIDE : SIDE + 1, 0:1]
    )
    scale = 1.0 / jnp.sqrt(squares / ENTRIES + EPS)

    def put(position, block):
        sector = sector_at(wf, position)
        inside = (sector >= 0) & (sector < SECTORS)
        value = jnp.where(inside, block * scale, 0.0)
        vector[position] = value
        vec_half[position] = value.astype(bf16)

    odd = wf & 1
    for i in range(OWN):
        put(4 * odd + i, start[i])
    for i in range(2):
        rows = slice(i * BLOCK, (i + 1) * BLOCK)
        put(4 - 2 * odd + i, one[rows])
        put(6 - 6 * odd + i, three[rows])
    held = [own[EXTRA:], one[SIDE + EXTRA :], two[EXTRA:], three[SIDE + EXTRA :]]
    for place in range(2):
        source = (lax.axis_index("c") + 2 * place) ^ wf
        value = held[0]
        for other in range(1, 4):
            value = jnp.where(source == other, held[other], value)
        pieces[place] = value * scale
    full_sweep(shift, mask, left, right, vec_half, back, sums, keep, give)


def join_kernel(first, second, out):
    out[...] = (first[...] + second[...]).astype(out.dtype)


def spread_kernel(parts, out):
    summed = jnp.sum(parts[...].astype(f32), axis=0)
    for target in range(out.shape[0]):
        out[target] = summed


def combined(masks, parts):
    base = HALF * lax.axis_index("c")
    sums = []
    for other in range(4):
        sums.append((parts[other] + parts[4 + other]).reshape(HALF, ROWS, BLOCK))
    values = []
    for place in range(2):
        blocks = []
        for k in range(HALF):
            value = jnp.zeros((ROWS, BLOCK), f32)
            for other in range(4):
                here = sector_at(other, base + k) == base + k + 8 * place
                value = value + jnp.where(here, sums[other][k], 0.0)
            blocks.append(value)
        values.append(jnp.concatenate(blocks, axis=0) * masks[place])
    return values


def send(values, sums, out):
    wf, base, _ = place_here()
    chosen = []
    for k in range(HALF):
        sector = sector_at(wf, base + k)
        rows = slice(k * ROWS, (k + 1) * ROWS)
        block = jnp.where(sector == base + k, values[0][rows], 0.0)
        chosen.append(jnp.where(sector == base + k + 8, values[1][rows], block))
    chosen = jnp.concatenate(chosen, axis=0)
    packet = jnp.concatenate([chosen, pack(sums, 1)], axis=0)
    for target in range(LINE):
        out[target * PACKET : (target + 1) * PACKET] = packet


def image_kernel(parts, masks, pieces, out, image_pieces):
    image = combined(masks, parts)
    vec = [pieces[0], pieces[1]]

    def inner(first, second):
        return total(first[0] * second[0] + first[1] * second[1])

    vec_vec, vec_image = inner(vec, vec), inner(vec, image)
    part = ratio(vec_image, vec_vec)
    rest = [image[i] - part * vec[i] for i in range(2)]
    for i in range(2):
        image_pieces[i] = image[i]
    send(image, [vec_image, vec_vec, part, inner(rest, rest)], out)


def line_rows(held, first, rows):
    places = range(first, LINE * PACKET, PACKET)
    return jnp.concatenate([held[place : place + rows] for place in places], axis=0)


def both(cores, count):
    return zip(*[lanes(line_rows(held, CHUNK, 1), count) for held in cores])


def add(values):
    return total(values[0]) + total(values[1])


def held_block(cores, position):
    own, other = (line_rows(held, ROWS * (position % HALF), ROWS) for held in cores)
    return jnp.where(lax.axis_index("c") == position // HALF, own, other)


def second_kernel(
    shift, mask, left, right, own, other, vector, keep, give, direction, image, scalars,
    vec_half, back, sums,
):
    cores = (own, other)
    vec_image, vec_vec, part, rest = both(cores, 4)
    ritz = add(vec_image) / ENTRIES
    norm = add([rest[i] + (ritz - part[i]) * (ritz - part[i]) * vec_vec[i] for i in range(2)])
    norm = norm / ENTRIES
    scale = 1.0 / jnp.sqrt(norm + EPS)
    scalars[...] = pack([ritz, norm])
    for position in range(WINDOW):
        held = held_block(cores, position)
        value = (held - ritz * vector[position]) * scale
        image[position] = held
        direction[position] = value
        vec_half[position] = value.astype(bf16)
    full_sweep(shift, mask, left, right, vec_half, back, sums, keep, give)


def turned_kernel(parts, masks, pieces, image_pieces, scalars, out):
    turned = combined(masks, parts)
    ritz, norm = scalars[0:1, 0:1], scalars[0:1, 1:2]
    scale = 1.0 / jnp.sqrt(norm + EPS)
    vec = [pieces[i] for i in range(2)]
    image = [image_pieces[i] for i in range(2)]
    turn = [(image[i] - ritz * vec[i]) * scale for i in range(2)]

    def inner(first, second):
        return total(first[0] * second[0] + first[1] * second[1])

    vec_vec, vec_turned = inner(vec, vec), inner(vec, turned)
    along = ratio(inner(vec, turn), vec_vec)
    new = [turn[i] - along * vec[i] for i in range(2)]
    on_vec = ratio(vec_turned, vec_vec)
    rest = [turned[i] - on_vec * vec[i] for i in range(2)]
    new_new = inner(new, new)
    on_new = ratio(inner(new, rest), new_new)
    rest = [rest[i] - on_new * new[i] for i in range(2)]
    sums = [
        vec_turned, inner(turn, image), inner(turn, turned),
        vec_vec, along, on_vec, new_new, on_new, inner(rest, rest),
    ]
    send(turned, sums, out)


def mixing(ritz, curvature, norm):
    gap = ritz - curvature
    lowest = 0.5 * (ritz + curvature) - jnp.sqrt(0.25 * gap * gap + norm)
    keep = curvature - lowest
    take = -jnp.sqrt(norm)
    scale = jnp.sqrt(keep * keep + take * take)
    return lowest, keep / scale, take / scale


def third_kernel(
    shift, mask, left, right, gathered, swapped, vector, direction, image, scalars,
    out, new_vector, new_direction, new_scalars, vec_half, back,
):
    cores = (gathered, swapped)
    wf = lax.axis_index("wf")
    (
        vec_turned, turn_image, turn_turned, vec_vec, along, on_vec, new_new, on_new, rest,
    ) = both(cores, 9)
    ritz, norm = scalars[0:1, 0:1], scalars[0:1, 1:2]
    curvature = add(turn_turned) / ENTRIES
    lowest, keep, take = mixing(ritz, curvature, norm)
    mixed = (add(vec_turned) + add(turn_image)) / ENTRIES
    next_ritz = keep * keep * ritz + keep * take * mixed + take * take * curvature
    first = keep * (ritz - next_ritz)
    second = keep * jnp.sqrt(norm + EPS) - take * next_ritz
    squares = []
    for i in range(2):
        on_first = first + second * along[i] + take * on_vec[i]
        on_second = second + take * on_new[i]
        square = on_first * on_first * vec_vec[i] + on_second * on_second * new_new[i]
        squares.append(square + take * take * rest[i])
    next_norm = add(squares) / ENTRIES
    scale = 1.0 / jnp.sqrt(next_norm + EPS)
    new_scalars[...] = pack([next_ritz, next_norm, lowest])
    for position in range(WINDOW):
        turned = held_block(cores, position)
        mixed_vec = keep * vector[position] + take * direction[position]
        mixed_image = keep * image[position] + take * turned
        value = (mixed_image - next_ritz * mixed_vec) * scale
        vec_half[position] = value.astype(bf16)

        @pl.when((position // 4) == (wf & 1))
        def _():
            new_vector[position % 4] = mixed_vec
            new_direction[position % 4] = value

    value = jnp.zeros((1, 1), f32)
    for i in range(OWN):
        half = half_step(shift, mask, left, right, vec_half, back, OWN * wf + i, i)
        value = value + total(half * new_direction[i])
    out[...] = jnp.broadcast_to(2.0 * value, out.shape)


def last_kernel(parts, vector, direction, scalars, out, energies):
    curvature = total(parts[:, 0:1]) / ENTRIES
    ritz, norm, first_lowest = lanes(scalars[0:1], 3)
    lowest, keep, take = mixing(ritz, curvature, norm)
    for i in range(OWN):
        out[i] = keep * vector[i] + take * direction[i]
    energies[0] = first_lowest[0, 0]
    energies[1] = lowest[0, 0]


HBM = pl.BlockSpec(memory_space=pltpu.HBM)
VMEM = pl.BlockSpec(memory_space=pltpu.VMEM)
SMEM = pl.BlockSpec(memory_space=pltpu.SMEM)
MIB = 1 << 20


def struct(*shape, dtype=f32):
    return jax.ShapeDtypeStruct(shape, dtype)


def call(kernel, name, outs, in_specs, args, out_specs=None, scratch=(), limit=6):
    return pl.pallas_call(
        kernel,
        name=name,
        in_specs=in_specs,
        out_specs=out_specs or [VMEM] * len(outs),
        out_shape=outs,
        scratch_shapes=scratch,
        compiler_params=pltpu.CompilerParams(vmem_limit_bytes=int(limit * MIB)),
    )(*args)


def small(kernel, name, outs, *arrays, out_specs=None):
    return call(kernel, name, outs, [VMEM] * len(arrays), arrays, out_specs)


def step(kernel, name, outs, operators, arrays, sums=True):
    scratch = [
        pltpu.VMEM((WINDOW, BLOCK, BLOCK), bf16),
        pltpu.VMEM((2, BLOCK, PAIRS * BLOCK), bf16),
    ]
    if sums:
        scratch.append(pltpu.VMEM((WINDOW, BLOCK, BLOCK), f32))
    args = (*operators, *arrays)
    in_specs = [SMEM] * 2 + [VMEM] * (len(args) - 2)
    return call(kernel, name, outs, in_specs, args, scratch=scratch, limit=16)


def device(y, z, core, wf):
    return ((y * 8 + z) * 2 + core) * 4 + wf


LINE_GROUPS = [
    [device(rows[half], z, core, wf) for half, z in line_order(core)]
    for rows in LINE_ROWS
    for core in range(2)
    for wf in range(4)
]
CROSS_GROUPS = [
    [device(y, z, core, wf) for y in rows for wf in range(4)]
    for rows in CROSS_ROWS
    for z in range(8)
    for core in range(2)
]


def exchange(value, groups=None):
    return lax.all_to_all(value, ALL_AXES, 0, 0, axis_index_groups=groups, tiled=True)


def shards(guess, left_ops, right_ops, op_shift, op_mask, left_dims, right_dims):
    blocks = struct(WINDOW, BLOCK, BLOCK)
    half = struct(LINE, CHUNK, BLOCK)
    sent = struct(LINE, CHUNK, BLOCK, dtype=bf16)
    own_blocks = struct(OWN, BLOCK, BLOCK)
    pair = struct(2, CHUNK, BLOCK)
    scalar_row = struct(EXTRA, BLOCK)
    packet = struct(LINE * PACKET, BLOCK)

    def partner(value, distance):
        return lax.ppermute(value, "wf", [(i, i ^ distance) for i in range(4)])

    def swapped(value):
        return lax.ppermute(value, "c", [(0, 1), (1, 0)])

    tail = EXTRA + CHUNK
    start, masks, one, own, three = call(
        norm_kernel, "norm",
        [own_blocks, pair, struct(SIDE + tail, BLOCK), struct(tail, BLOCK),
         struct(SIDE + tail, BLOCK)],
        [SMEM, SMEM, VMEM], (left_dims, right_dims, guess), limit=60,
    )
    three, one, two = partner(three, 3), partner(one, 1), partner(own, 2)
    held = struct(OWN, PAIRS, BLOCK, BLOCK, dtype=bf16)
    left, right = call(
        load_kernel, "load", [held, held], [HBM, HBM], (left_ops, right_ops),
        scratch=[pltpu.SemaphoreType.DMA((2 * OWN,))], limit=49,
    )
    operators = (op_shift, op_mask.T, left, right)

    def reduced(keep, give):
        (summed,) = small(join_kernel, "join", [sent], keep, swapped(give))
        parts = exchange(summed, LINE_GROUPS)
        (tiled,) = small(spread_kernel, "spread", [struct(CROSS, CHUNK, BLOCK)], parts)
        return exchange(tiled, CROSS_GROUPS)

    def gathered(packets):
        packets = exchange(packets.reshape(-1, 1, BLOCK), LINE_GROUPS).reshape(-1, BLOCK)
        return packets, swapped(packets)

    keep, give, vector, pieces = step(
        first_kernel, "first", [half, half, blocks, pair], operators,
        (start, own, one, two, three),
    )
    packets, image_pieces = small(
        image_kernel, "image", [packet, pair], reduced(keep, give), masks, pieces
    )
    keep, give, direction, image, scalars = step(
        second_kernel, "second", [half, half, blocks, blocks, scalar_row], operators,
        (*gathered(packets), vector),
    )
    (packets,) = small(
        turned_kernel, "turned", [packet], reduced(keep, give), masks, pieces, image_pieces, scalars
    )
    sums, vector, direction, scalars = step(
        third_kernel, "third", [struct(256, BLOCK), own_blocks, own_blocks, scalar_row], operators,
        (*gathered(packets), vector, direction, image, scalars), sums=False,
    )
    sums = exchange(sums)
    result, energies = small(
        last_kernel, "last", [own_blocks, struct(2)], sums, vector, direction, scalars,
        out_specs=[VMEM, SMEM],
    )
    return result, energies


def solution(mesh):
    split = Mesh(mesh.devices.reshape(4, 8, 2, 4), (*OP_AXES, "wf"))
    in_specs = (
        P("wf", None, None),
        P(OP_AXES, "wf", None, None),
        P(OP_AXES, "wf", None, None),
        P(OP_AXES),
        P(OP_AXES, "wf"),
        P(),
        P(),
    )
    out_specs = (P("wf", None, None), P())
    return jax.shard_map(
        shards, mesh=split, in_specs=in_specs, out_specs=out_specs, check_vma=False
    )
```

```python
import jax
import jax.numpy as jnp
from jax import lax
from jax.experimental import pallas as pl
from jax.experimental.pallas import tpu as pltpu
from jax.sharding import Mesh, PartitionSpec as P

EPS = 1e-06
SECTORS = 16
BLOCK = 128
PAIRS = 16
OWN = 4
WINDOW = 8
LINE = 16
CROSS = 8
HALF = 4
ROWS = 8
CHUNK = HALF * ROWS
PACKET = CHUNK + 1
SIDE = 2 * BLOCK
EXTRA = 8
ENTRIES = float(SECTORS * BLOCK * BLOCK)
ALL_AXES = ("y", "z", "c", "wf")
LINE_ROWS = ((0, 1), (3, 2))
CROSS_ROWS = ((0, 3), (1, 2))
OP_AXES = ("y", "z", "c")

f32 = jnp.float32
bf16 = jnp.bfloat16


def dot(first, second, first_dim=1, second_dim=0):
    return lax.dot_general(
        first, second, (((first_dim,), (second_dim,)), ((), ())), preferred_element_type=f32
    )


def total(values):
    return jnp.sum(values, axis=(0, 1), keepdims=True)


def ratio(top, bottom):
    return jnp.where(bottom > 0, top / jnp.where(bottom > 0, bottom, 1.0), 0.0)


def line_order(core):
    return [(half, z) for half in range(2) for z in range(8)]


def place_here():
    y, z, core = (lax.axis_index(axis) for axis in OP_AXES)
    half = (y ^ (y // 2)) & 1
    chunk = half * 8 + z
    first_row = pl.multiple_of(chunk * ROWS, ROWS)
    return lax.axis_index("wf"), HALF * core, first_row


def sector_at(wf, position):
    base = OWN * wf - 2
    return base + ((position - base) & 7)


def live(left_dims, right_dims, sector, first_row, rows):
    held = jnp.clip(sector, 0, SECTORS - 1)
    inside = (sector >= 0) & (sector < SECTORS)
    height = jnp.where(inside, left_dims[held], 0)
    width = right_dims[SECTORS - 1 - held]
    row = lax.broadcasted_iota(jnp.int32, (rows, BLOCK), 0) + first_row
    column = lax.broadcasted_iota(jnp.int32, (rows, BLOCK), 1)
    return (row < height) & (column < width)


def pack(values, rows=EXTRA):
    lane = lax.broadcasted_iota(jnp.int32, (rows, BLOCK), 1)
    packed = jnp.zeros((rows, BLOCK), f32)
    for place, value in enumerate(values):
        packed = jnp.where(lane == place, value, packed)
    return packed


def lanes(rows, count):
    return [rows[:, place : place + 1] for place in range(count)]


def load_kernel(left_hbm, right_hbm, left, right, sems):
    copies = []
    for i in range(OWN):
        for source, target in ((left_hbm, left), (right_hbm, right)):
            copies.append(
                pltpu.make_async_copy(source.at[:, i], target.at[i], sems.at[len(copies)])
            )
    for copy in copies:
        copy.start()
    for copy in copies:
        copy.wait()


def norm_kernel(left_dims, right_dims, guess, masks, one, two, three, start):
    wf, base, first_row = place_here()
    sums = jnp.zeros((1, 1), f32)
    for i in range(OWN):
        mask = live(left_dims, right_dims, OWN * wf + i, 0, BLOCK)
        block = jnp.where(mask, guess[i], 0.0)
        start[i] = block
        sums = sums + total(block * block)
    odd = wf & 1
    for i in range(2):
        one[i * BLOCK : (i + 1) * BLOCK] = start[2 - 2 * odd + i]
        three[i * BLOCK : (i + 1) * BLOCK] = start[2 * odd + i]
    for out, first in ((one, SIDE), (two, 0), (three, SIDE)):
        out[first : first + EXTRA] = jnp.broadcast_to(sums, (EXTRA, BLOCK))
        out[first + EXTRA :] = start[:, pl.ds(first_row, ROWS)].reshape(CHUNK, BLOCK)
    for i in range(2):
        for k in range(HALF):
            mask = live(left_dims, right_dims, base + k + 8 * i, first_row, ROWS)
            masks[i, k * ROWS : (k + 1) * ROWS] = jnp.where(mask, 1.0, 0.0)


def half_step(shift, mask, left, right, vec_half, back, sector, index):
    for k in range(PAIRS):
        position = (sector + shift[k]) & 7
        weight = mask[index, k].astype(f32)
        value = dot(left[index, k].T, vec_half[position])
        back[index & 1, :, k * BLOCK : (k + 1) * BLOCK] = (value * weight).astype(bf16)
    return dot(back[index & 1], right[index].reshape(PAIRS * BLOCK, BLOCK))


def middle_pair(left, vec_half, sector, index):
    zero = jnp.zeros((BLOCK, BLOCK), bf16)
    rows = [
        jnp.concatenate([vec_half[sector & 7], zero], axis=1),
        jnp.concatenate([zero, vec_half[(sector + 1) & 7]], axis=1),
    ]
    blocks = [left[index + i].reshape(PAIRS * BLOCK, BLOCK) for i in range(2)]
    return dot(jnp.concatenate(blocks, axis=1), jnp.concatenate(rows, axis=0))


def full_sweep(shift, mask, left, right, vec_half, back, sums, keep, give):
    sums[...] = jnp.zeros_like(sums)
    first_sector = OWN * lax.axis_index("wf")
    for pair in range(0, OWN, 2):
        middle = middle_pair(left, vec_half, first_sector + pair, pair)
        for i in range(2):
            sector, index = first_sector + pair + i, pair + i
            for k in range(PAIRS):
                position = (sector + shift[k]) & 7
                weight = mask[index, k].astype(f32)
                value = middle[k * BLOCK : (k + 1) * BLOCK, i * BLOCK : (i + 1) * BLOCK]
                sums[position] += dot((value * weight).astype(bf16), right[index, k], 1, 1)
        for i in range(2):
            sector, index = first_sector + pair + i, pair + i
            sums[sector & 7] += half_step(shift, mask, left, right, vec_half, back, sector, index)
    core = lax.axis_index("c")
    for out, first in ((keep, HALF * core), (give, HALF - HALF * core)):
        for i in range(HALF):
            rows = sums[first + i].reshape(LINE, ROWS, BLOCK)
            out[:, i * ROWS : (i + 1) * ROWS] = rows


def first_kernel(
    shift, mask, left, right, sent_one, sent_three, one, two, three,
    keep, give, vector, pieces,
    vec_half, back, sums,
):
    wf = lax.axis_index("wf")
    squares = (sent_one[SIDE : SIDE + 1, 0:1] + one[SIDE : SIDE + 1, 0:1]) + (
        two[0:1, 0:1] + three[SIDE : SIDE + 1, 0:1]
    )
    scale = 1.0 / jnp.sqrt(squares / ENTRIES + EPS)

    def put(position, block):
        sector = sector_at(wf, position)
        inside = (sector >= 0) & (sector < SECTORS)
        value = jnp.where(inside, block * scale, 0.0)
        vector[position] = value
        vec_half[position] = value.astype(bf16)

    odd = wf & 1
    for i in range(2):
        rows = slice(i * BLOCK, (i + 1) * BLOCK)
        put(6 * odd + i, sent_three[rows])
        put(2 + 2 * odd + i, sent_one[rows])
        put(4 - 2 * odd + i, one[rows])
        put(6 - 6 * odd + i, three[rows])
    held = [sent_one[SIDE + EXTRA :], one[SIDE + EXTRA :], two[EXTRA:], three[SIDE + EXTRA :]]
    for place in range(2):
        source = (lax.axis_index("c") + 2 * place) ^ wf
        value = held[0]
        for other in range(1, 4):
            value = jnp.where(source == other, held[other], value)
        pieces[place] = value * scale
    full_sweep(shift, mask, left, right, vec_half, back, sums, keep, give)


def join_kernel(first, second, out):
    out[...] = (first[...] + second[...]).astype(out.dtype)


def spread_kernel(parts, out):
    summed = jnp.sum(parts[...].astype(f32), axis=0)
    for target in range(out.shape[0]):
        out[target] = summed


def combined(masks, parts):
    base = HALF * lax.axis_index("c")
    sums = []
    for other in range(4):
        sums.append((parts[other] + parts[4 + other]).reshape(HALF, ROWS, BLOCK))
    values = []
    for place in range(2):
        blocks = []
        for k in range(HALF):
            value = jnp.zeros((ROWS, BLOCK), f32)
            for other in range(4):
                here = sector_at(other, base + k) == base + k + 8 * place
                value = value + jnp.where(here, sums[other][k], 0.0)
            blocks.append(value)
        values.append(jnp.concatenate(blocks, axis=0) * masks[place])
    return values


def send(values, sums, out):
    wf, base, _ = place_here()
    chosen = []
    for k in range(HALF):
        sector = sector_at(wf, base + k)
        rows = slice(k * ROWS, (k + 1) * ROWS)
        block = jnp.where(sector == base + k, values[0][rows], 0.0)
        chosen.append(jnp.where(sector == base + k + 8, values[1][rows], block))
    chosen = jnp.concatenate(chosen, axis=0)
    packet = jnp.concatenate([chosen, pack(sums, 1)], axis=0)
    for target in range(LINE):
        out[target * PACKET : (target + 1) * PACKET] = packet


def image_kernel(parts, masks, pieces, out, image_pieces):
    image = combined(masks, parts)
    vec = [pieces[0], pieces[1]]

    def inner(first, second):
        return total(first[0] * second[0] + first[1] * second[1])

    vec_vec, vec_image = inner(vec, vec), inner(vec, image)
    part = ratio(vec_image, vec_vec)
    rest = [image[i] - part * vec[i] for i in range(2)]
    for i in range(2):
        image_pieces[i] = image[i]
    send(image, [vec_image, vec_vec, part, inner(rest, rest)], out)


def line_rows(held, first, rows):
    places = range(first, LINE * PACKET, PACKET)
    return jnp.concatenate([held[place : place + rows] for place in places], axis=0)


def both(cores, count):
    return zip(*[lanes(line_rows(held, CHUNK, 1), count) for held in cores])


def add(values):
    return total(values[0]) + total(values[1])


def held_block(cores, position):
    own, other = (line_rows(held, ROWS * (position % HALF), ROWS) for held in cores)
    return jnp.where(lax.axis_index("c") == position // HALF, own, other)


def second_kernel(
    shift, mask, left, right, own, other, vector, keep, give, direction, image, scalars,
    vec_half, back, sums,
):
    cores = (own, other)
    vec_image, vec_vec, part, rest = both(cores, 4)
    ritz = add(vec_image) / ENTRIES
    norm = add([rest[i] + (ritz - part[i]) * (ritz - part[i]) * vec_vec[i] for i in range(2)])
    norm = norm / ENTRIES
    scale = 1.0 / jnp.sqrt(norm + EPS)
    scalars[...] = pack([ritz, norm])
    for position in range(WINDOW):
        held = held_block(cores, position)
        value = (held - ritz * vector[position]) * scale
        image[position] = held
        direction[position] = value
        vec_half[position] = value.astype(bf16)
    full_sweep(shift, mask, left, right, vec_half, back, sums, keep, give)


def turned_kernel(parts, masks, pieces, image_pieces, scalars, out):
    turned = combined(masks, parts)
    ritz, norm = scalars[0:1, 0:1], scalars[0:1, 1:2]
    scale = 1.0 / jnp.sqrt(norm + EPS)
    vec = [pieces[i] for i in range(2)]
    image = [image_pieces[i] for i in range(2)]
    turn = [(image[i] - ritz * vec[i]) * scale for i in range(2)]

    def inner(first, second):
        return total(first[0] * second[0] + first[1] * second[1])

    vec_vec, vec_turned = inner(vec, vec), inner(vec, turned)
    along = ratio(inner(vec, turn), vec_vec)
    new = [turn[i] - along * vec[i] for i in range(2)]
    on_vec = ratio(vec_turned, vec_vec)
    rest = [turned[i] - on_vec * vec[i] for i in range(2)]
    new_new = inner(new, new)
    on_new = ratio(inner(new, rest), new_new)
    rest = [rest[i] - on_new * new[i] for i in range(2)]
    sums = [
        vec_turned, inner(turn, image), inner(turn, turned),
        vec_vec, along, on_vec, new_new, on_new, inner(rest, rest),
    ]
    send(turned, sums, out)


def mixing(ritz, curvature, norm):
    gap = ritz - curvature
    lowest = 0.5 * (ritz + curvature) - jnp.sqrt(0.25 * gap * gap + norm)
    keep = curvature - lowest
    take = -jnp.sqrt(norm)
    scale = jnp.sqrt(keep * keep + take * take)
    return lowest, keep / scale, take / scale


def third_kernel(
    shift, mask, left, right, gathered, swapped, vector, direction, image, scalars,
    out, new_vector, new_direction, new_scalars, vec_half, back,
):
    cores = (gathered, swapped)
    wf = lax.axis_index("wf")
    (
        vec_turned, turn_image, turn_turned, vec_vec, along, on_vec, new_new, on_new, rest,
    ) = both(cores, 9)
    ritz, norm = scalars[0:1, 0:1], scalars[0:1, 1:2]
    curvature = add(turn_turned) / ENTRIES
    lowest, keep, take = mixing(ritz, curvature, norm)
    mixed = (add(vec_turned) + add(turn_image)) / ENTRIES
    next_ritz = keep * keep * ritz + keep * take * mixed + take * take * curvature
    first = keep * (ritz - next_ritz)
    second = keep * jnp.sqrt(norm + EPS) - take * next_ritz
    squares = []
    for i in range(2):
        on_first = first + second * along[i] + take * on_vec[i]
        on_second = second + take * on_new[i]
        square = on_first * on_first * vec_vec[i] + on_second * on_second * new_new[i]
        squares.append(square + take * take * rest[i])
    next_norm = add(squares) / ENTRIES
    scale = 1.0 / jnp.sqrt(next_norm + EPS)
    new_scalars[...] = pack([next_ritz, next_norm, lowest])
    for position in range(WINDOW):
        turned = held_block(cores, position)
        mixed_vec = keep * vector[position] + take * direction[position]
        mixed_image = keep * image[position] + take * turned
        value = (mixed_image - next_ritz * mixed_vec) * scale
        vec_half[position] = value.astype(bf16)

        @pl.when((position // 4) == (wf & 1))
        def _():
            new_vector[position % 4] = mixed_vec
            new_direction[position % 4] = value

    value = jnp.zeros((1, 1), f32)
    for i in range(OWN):
        half = half_step(shift, mask, left, right, vec_half, back, OWN * wf + i, i)
        value = value + total(half * new_direction[i])
    out[...] = jnp.broadcast_to(2.0 * value, out.shape)


def last_kernel(parts, vector, direction, scalars, out, energies):
    curvature = total(parts[:, 0:1]) / ENTRIES
    ritz, norm, first_lowest = lanes(scalars[0:1], 3)
    lowest, keep, take = mixing(ritz, curvature, norm)
    for i in range(OWN):
        out[i] = keep * vector[i] + take * direction[i]
    energies[0] = first_lowest[0, 0]
    energies[1] = lowest[0, 0]


HBM = pl.BlockSpec(memory_space=pltpu.HBM)
VMEM = pl.BlockSpec(memory_space=pltpu.VMEM)
SMEM = pl.BlockSpec(memory_space=pltpu.SMEM)
MIB = 1 << 20


def struct(*shape, dtype=f32):
    return jax.ShapeDtypeStruct(shape, dtype)


def call(kernel, name, outs, in_specs, args, out_specs=None, scratch=(), limit=6):
    return pl.pallas_call(
        kernel,
        name=name,
        in_specs=in_specs,
        out_specs=out_specs or [VMEM] * len(outs),
        out_shape=outs,
        scratch_shapes=scratch,
        compiler_params=pltpu.CompilerParams(vmem_limit_bytes=int(limit * MIB)),
    )(*args)


def small(kernel, name, outs, *arrays, out_specs=None):
    return call(kernel, name, outs, [VMEM] * len(arrays), arrays, out_specs)


def step(kernel, name, outs, operators, arrays, sums=True):
    scratch = [
        pltpu.VMEM((WINDOW, BLOCK, BLOCK), bf16),
        pltpu.VMEM((2, BLOCK, PAIRS * BLOCK), bf16),
    ]
    if sums:
        scratch.append(pltpu.VMEM((WINDOW, BLOCK, BLOCK), f32))
    args = (*operators, *arrays)
    in_specs = [SMEM] * 2 + [VMEM] * (len(args) - 2)
    return call(kernel, name, outs, in_specs, args, scratch=scratch, limit=16)


def device(y, z, core, wf):
    return ((y * 8 + z) * 2 + core) * 4 + wf


LINE_GROUPS = [
    [device(rows[half], z, core, wf) for half, z in line_order(core)]
    for rows in LINE_ROWS
    for core in range(2)
    for wf in range(4)
]
CROSS_GROUPS = [
    [device(y, z, core, wf) for y in rows for wf in range(4)]
    for rows in CROSS_ROWS
    for z in range(8)
    for core in range(2)
]


def exchange(value, groups=None):
    return lax.all_to_all(value, ALL_AXES, 0, 0, axis_index_groups=groups, tiled=True)


def shards(guess, left_ops, right_ops, op_shift, op_mask, left_dims, right_dims):
    blocks = struct(WINDOW, BLOCK, BLOCK)
    half = struct(LINE, CHUNK, BLOCK)
    sent = struct(LINE, CHUNK, BLOCK, dtype=bf16)
    own_blocks = struct(OWN, BLOCK, BLOCK)
    pair = struct(2, CHUNK, BLOCK)
    scalar_row = struct(EXTRA, BLOCK)
    packet = struct(LINE * PACKET, BLOCK)

    def partner(value, distance):
        return lax.ppermute(value, "wf", [(i, i ^ distance) for i in range(4)])

    def swapped(value):
        return lax.ppermute(value, "c", [(0, 1), (1, 0)])

    tail = EXTRA + CHUNK
    masks, sent_one, sent_two, sent_three = call(
        norm_kernel, "norm",
        [pair, struct(SIDE + tail, BLOCK), struct(tail, BLOCK), struct(SIDE + tail, BLOCK)],
        [SMEM, SMEM, VMEM], (left_dims, right_dims, guess),
        scratch=[pltpu.VMEM((OWN, BLOCK, BLOCK), f32)], limit=60,
    )
    three, one, two = partner(sent_three, 3), partner(sent_one, 1), partner(sent_two, 2)
    held = struct(OWN, PAIRS, BLOCK, BLOCK, dtype=bf16)
    left, right = call(
        load_kernel, "load", [held, held], [HBM, HBM], (left_ops, right_ops),
        scratch=[pltpu.SemaphoreType.DMA((2 * OWN,))], limit=49,
    )
    operators = (op_shift, op_mask.T, left, right)

    def reduced(keep, give):
        (summed,) = small(join_kernel, "join", [sent], keep, swapped(give))
        parts = exchange(summed, LINE_GROUPS)
        (tiled,) = small(spread_kernel, "spread", [struct(CROSS, CHUNK, BLOCK)], parts)
        return exchange(tiled, CROSS_GROUPS)

    def gathered(packets):
        packets = exchange(packets.reshape(-1, 1, BLOCK), LINE_GROUPS).reshape(-1, BLOCK)
        return packets, swapped(packets)

    keep, give, vector, pieces = step(
        first_kernel, "first", [half, half, blocks, pair], operators,
        (sent_one, sent_three, one, two, three),
    )
    packets, image_pieces = small(
        image_kernel, "image", [packet, pair], reduced(keep, give), masks, pieces
    )
    keep, give, direction, image, scalars = step(
        second_kernel, "second", [half, half, blocks, blocks, scalar_row], operators,
        (*gathered(packets), vector),
    )
    (packets,) = small(
        turned_kernel, "turned", [packet], reduced(keep, give), masks, pieces, image_pieces, scalars
    )
    sums, vector, direction, scalars = step(
        third_kernel, "third", [struct(256, BLOCK), own_blocks, own_blocks, scalar_row], operators,
        (*gathered(packets), vector, direction, image, scalars), sums=False,
    )
    sums = exchange(sums)
    result, energies = small(
        last_kernel, "last", [own_blocks, struct(2)], sums, vector, direction, scalars,
        out_specs=[VMEM, SMEM],
    )
    return result, energies


def solution(mesh):
    split = Mesh(mesh.devices.reshape(4, 8, 2, 4), (*OP_AXES, "wf"))
    in_specs = (
        P("wf", None, None),
        P(OP_AXES, "wf", None, None),
        P(OP_AXES, "wf", None, None),
        P(OP_AXES),
        P(OP_AXES, "wf"),
        P(),
        P(),
    )
    out_specs = (P("wf", None, None), P())
    return jax.shard_map(
        shards, mesh=split, in_specs=in_specs, out_specs=out_specs, check_vma=False
    )
```

```python
import jax
import jax.numpy as jnp
from jax import lax
from jax.experimental import pallas as pl
from jax.experimental.pallas import tpu as pltpu
from jax.sharding import Mesh, PartitionSpec as P

EPS = 1e-06
SECTORS = 16
BLOCK = 128
PAIRS = 16
OWN = 4
WINDOW = 8
LINE = 16
CROSS = 8
HALF = 4
ROWS = 8
CHUNK = HALF * ROWS
PACKET = CHUNK + 1
SIDE = 2 * BLOCK
EXTRA = 8
ENTRIES = float(SECTORS * BLOCK * BLOCK)
ALL_AXES = ("y", "z", "c", "wf")
LINE_ROWS = ((0, 1), (3, 2))
CROSS_ROWS = ((0, 3), (1, 2))
OP_AXES = ("y", "z", "c")

f32 = jnp.float32
bf16 = jnp.bfloat16


def dot(first, second, first_dim=1, second_dim=0):
    return lax.dot_general(
        first, second, (((first_dim,), (second_dim,)), ((), ())), preferred_element_type=f32
    )


def total(values):
    return jnp.sum(values, axis=(0, 1), keepdims=True)


def ratio(top, bottom):
    return jnp.where(bottom > 0, top / jnp.where(bottom > 0, bottom, 1.0), 0.0)


def line_order(core):
    return [(half, (1 + 2 * core) * z % 8) for half in range(2) for z in range(8)]


def place_here():
    y, z, core = (lax.axis_index(axis) for axis in OP_AXES)
    half = (y ^ (y // 2)) & 1
    chunk = half * 8 + ((z + 2 * z * core) & 7)
    first_row = pl.multiple_of(chunk * ROWS, ROWS)
    return lax.axis_index("wf"), HALF * core, first_row


def sector_at(wf, position):
    base = OWN * wf - 2
    return base + ((position - base) & 7)


def live(left_dims, right_dims, sector, first_row, rows):
    held = jnp.clip(sector, 0, SECTORS - 1)
    inside = (sector >= 0) & (sector < SECTORS)
    height = jnp.where(inside, left_dims[held], 0)
    width = right_dims[SECTORS - 1 - held]
    row = lax.broadcasted_iota(jnp.int32, (rows, BLOCK), 0) + first_row
    column = lax.broadcasted_iota(jnp.int32, (rows, BLOCK), 1)
    return (row < height) & (column < width)


def pack(values, rows=EXTRA):
    lane = lax.broadcasted_iota(jnp.int32, (rows, BLOCK), 1)
    packed = jnp.zeros((rows, BLOCK), f32)
    for place, value in enumerate(values):
        packed = jnp.where(lane == place, value, packed)
    return packed


def lanes(rows, count):
    return [rows[:, place : place + 1] for place in range(count)]


def load_kernel(left_hbm, right_hbm, left, right, sems):
    copies = []
    for i in range(OWN):
        for source, target in ((left_hbm, left), (right_hbm, right)):
            copies.append(
                pltpu.make_async_copy(source.at[:, i], target.at[i], sems.at[len(copies)])
            )
    for copy in copies:
        copy.start()
    for copy in copies:
        copy.wait()


def norm_kernel(left_dims, right_dims, guess, masks, one, two, three, start):
    wf, base, first_row = place_here()
    sums = jnp.zeros((1, 1), f32)
    for i in range(OWN):
        mask = live(left_dims, right_dims, OWN * wf + i, 0, BLOCK)
        block = jnp.where(mask, guess[i], 0.0)
        start[i] = block
        sums = sums + total(block * block)
    odd = wf & 1
    for i in range(2):
        one[i * BLOCK : (i + 1) * BLOCK] = start[2 - 2 * odd + i]
        three[i * BLOCK : (i + 1) * BLOCK] = start[2 * odd + i]
    for out, first in ((one, SIDE), (two, 0), (three, SIDE)):
        out[first : first + EXTRA] = jnp.broadcast_to(sums, (EXTRA, BLOCK))
        out[first + EXTRA :] = start[:, pl.ds(first_row, ROWS)].reshape(CHUNK, BLOCK)
    for i in range(2):
        for k in range(HALF):
            mask = live(left_dims, right_dims, base + k + 8 * i, first_row, ROWS)
            masks[i, k * ROWS : (k + 1) * ROWS] = jnp.where(mask, 1.0, 0.0)


def half_step(shift, mask, left, right, vec_half, back, sector, index):
    for k in range(PAIRS):
        position = (sector + shift[k]) & 7
        weight = mask[index, k].astype(f32)
        value = dot(left[index, k].T, vec_half[position])
        back[index & 1, :, k * BLOCK : (k + 1) * BLOCK] = (value * weight).astype(bf16)
    return dot(back[index & 1], right[index].reshape(PAIRS * BLOCK, BLOCK))


def middle_pair(left, vec_half, sector, index):
    zero = jnp.zeros((BLOCK, BLOCK), bf16)
    rows = [
        jnp.concatenate([vec_half[sector & 7], zero], axis=1),
        jnp.concatenate([zero, vec_half[(sector + 1) & 7]], axis=1),
    ]
    blocks = [left[index + i].reshape(PAIRS * BLOCK, BLOCK) for i in range(2)]
    return dot(jnp.concatenate(blocks, axis=1), jnp.concatenate(rows, axis=0))


def full_sweep(shift, mask, left, right, vec_half, back, sums, keep, give):
    sums[...] = jnp.zeros_like(sums)
    first_sector = OWN * lax.axis_index("wf")
    for pair in range(0, OWN, 2):
        middle = middle_pair(left, vec_half, first_sector + pair, pair)
        for i in range(2):
            sector, index = first_sector + pair + i, pair + i
            for k in range(PAIRS):
                position = (sector + shift[k]) & 7
                weight = mask[index, k].astype(f32)
                value = middle[k * BLOCK : (k + 1) * BLOCK, i * BLOCK : (i + 1) * BLOCK]
                sums[position] += dot((value * weight).astype(bf16), right[index, k], 1, 1)
        for i in range(2):
            sector, index = first_sector + pair + i, pair + i
            sums[sector & 7] += half_step(shift, mask, left, right, vec_half, back, sector, index)
    core = lax.axis_index("c")
    for out, first in ((keep, HALF * core), (give, HALF - HALF * core)):
        for i in range(HALF):
            rows = sums[first + i].reshape(LINE, ROWS, BLOCK)
            out[:, i * ROWS : (i + 1) * ROWS] = rows


def first_kernel(
    shift, mask, left, right, sent_one, sent_three, one, two, three,
    keep, give, vector, pieces,
    vec_half, back, sums,
):
    wf = lax.axis_index("wf")
    squares = (sent_one[SIDE : SIDE + 1, 0:1] + one[SIDE : SIDE + 1, 0:1]) + (
        two[0:1, 0:1] + three[SIDE : SIDE + 1, 0:1]
    )
    scale = 1.0 / jnp.sqrt(squares / ENTRIES + EPS)

    def put(position, block):
        sector = sector_at(wf, position)
        inside = (sector >= 0) & (sector < SECTORS)
        value = jnp.where(inside, block * scale, 0.0)
        vector[position] = value
        vec_half[position] = value.astype(bf16)

    odd = wf & 1
    for i in range(2):
        rows = slice(i * BLOCK, (i + 1) * BLOCK)
        put(6 * odd + i, sent_three[rows])
        put(2 + 2 * odd + i, sent_one[rows])
        put(4 - 2 * odd + i, one[rows])
        put(6 - 6 * odd + i, three[rows])
    held = [sent_one[SIDE + EXTRA :], one[SIDE + EXTRA :], two[EXTRA:], three[SIDE + EXTRA :]]
    for place in range(2):
        source = (lax.axis_index("c") + 2 * place) ^ wf
        value = held[0]
        for other in range(1, 4):
            value = jnp.where(source == other, held[other], value)
        pieces[place] = value * scale
    full_sweep(shift, mask, left, right, vec_half, back, sums, keep, give)


def join_kernel(first, second, out):
    out[...] = (first[...] + second[...]).astype(out.dtype)


def spread_kernel(parts, out):
    summed = jnp.sum(parts[...].astype(f32), axis=0)
    for target in range(out.shape[0]):
        out[target] = summed


def combined(masks, parts):
    base = HALF * lax.axis_index("c")
    sums = []
    for other in range(4):
        sums.append((parts[other] + parts[4 + other]).reshape(HALF, ROWS, BLOCK))
    values = []
    for place in range(2):
        blocks = []
        for k in range(HALF):
            value = jnp.zeros((ROWS, BLOCK), f32)
            for other in range(4):
                here = sector_at(other, base + k) == base + k + 8 * place
                value = value + jnp.where(here, sums[other][k], 0.0)
            blocks.append(value)
        values.append(jnp.concatenate(blocks, axis=0) * masks[place])
    return values


def send(values, sums, out):
    wf, base, _ = place_here()
    chosen = []
    for k in range(HALF):
        sector = sector_at(wf, base + k)
        rows = slice(k * ROWS, (k + 1) * ROWS)
        block = jnp.where(sector == base + k, values[0][rows], 0.0)
        chosen.append(jnp.where(sector == base + k + 8, values[1][rows], block))
    chosen = jnp.concatenate(chosen, axis=0)
    packet = jnp.concatenate([chosen, pack(sums, 1)], axis=0)
    for target in range(LINE):
        out[target * PACKET : (target + 1) * PACKET] = packet


def image_kernel(parts, masks, pieces, out, image_pieces):
    image = combined(masks, parts)
    vec = [pieces[0], pieces[1]]

    def inner(first, second):
        return total(first[0] * second[0] + first[1] * second[1])

    vec_vec, vec_image = inner(vec, vec), inner(vec, image)
    part = ratio(vec_image, vec_vec)
    rest = [image[i] - part * vec[i] for i in range(2)]
    for i in range(2):
        image_pieces[i] = image[i]
    send(image, [vec_image, vec_vec, part, inner(rest, rest)], out)


def line_rows(held, first, rows):
    places = range(first, LINE * PACKET, PACKET)
    return jnp.concatenate([held[place : place + rows] for place in places], axis=0)


def both(cores, count):
    return zip(*[lanes(line_rows(held, CHUNK, 1), count) for held in cores])


def add(values):
    return total(values[0]) + total(values[1])


def held_block(cores, position):
    own, other = (line_rows(held, ROWS * (position % HALF), ROWS) for held in cores)
    return jnp.where(lax.axis_index("c") == position // HALF, own, other)


def second_kernel(
    shift, mask, left, right, own, other, vector, keep, give, direction, image, scalars,
    vec_half, back, sums,
):
    cores = (own, other)
    vec_image, vec_vec, part, rest = both(cores, 4)
    ritz = add(vec_image) / ENTRIES
    norm = add([rest[i] + (ritz - part[i]) * (ritz - part[i]) * vec_vec[i] for i in range(2)])
    norm = norm / ENTRIES
    scale = 1.0 / jnp.sqrt(norm + EPS)
    scalars[...] = pack([ritz, norm])
    for position in range(WINDOW):
        held = held_block(cores, position)
        value = (held - ritz * vector[position]) * scale
        image[position] = held
        direction[position] = value
        vec_half[position] = value.astype(bf16)
    full_sweep(shift, mask, left, right, vec_half, back, sums, keep, give)


def turned_kernel(parts, masks, pieces, image_pieces, scalars, out):
    turned = combined(masks, parts)
    ritz, norm = scalars[0:1, 0:1], scalars[0:1, 1:2]
    scale = 1.0 / jnp.sqrt(norm + EPS)
    vec = [pieces[i] for i in range(2)]
    image = [image_pieces[i] for i in range(2)]
    turn = [(image[i] - ritz * vec[i]) * scale for i in range(2)]

    def inner(first, second):
        return total(first[0] * second[0] + first[1] * second[1])

    vec_vec, vec_turned = inner(vec, vec), inner(vec, turned)
    along = ratio(inner(vec, turn), vec_vec)
    new = [turn[i] - along * vec[i] for i in range(2)]
    on_vec = ratio(vec_turned, vec_vec)
    rest = [turned[i] - on_vec * vec[i] for i in range(2)]
    new_new = inner(new, new)
    on_new = ratio(inner(new, rest), new_new)
    rest = [rest[i] - on_new * new[i] for i in range(2)]
    sums = [
        vec_turned, inner(turn, image), inner(turn, turned),
        vec_vec, along, on_vec, new_new, on_new, inner(rest, rest),
    ]
    send(turned, sums, out)


def mixing(ritz, curvature, norm):
    gap = ritz - curvature
    lowest = 0.5 * (ritz + curvature) - jnp.sqrt(0.25 * gap * gap + norm)
    keep = curvature - lowest
    take = -jnp.sqrt(norm)
    scale = jnp.sqrt(keep * keep + take * take)
    return lowest, keep / scale, take / scale


def third_kernel(
    shift, mask, left, right, gathered, swapped, vector, direction, image, scalars,
    out, new_vector, new_direction, new_scalars, vec_half, back,
):
    cores = (gathered, swapped)
    wf = lax.axis_index("wf")
    (
        vec_turned, turn_image, turn_turned, vec_vec, along, on_vec, new_new, on_new, rest,
    ) = both(cores, 9)
    ritz, norm = scalars[0:1, 0:1], scalars[0:1, 1:2]
    curvature = add(turn_turned) / ENTRIES
    lowest, keep, take = mixing(ritz, curvature, norm)
    mixed = (add(vec_turned) + add(turn_image)) / ENTRIES
    next_ritz = keep * keep * ritz + keep * take * mixed + take * take * curvature
    first = keep * (ritz - next_ritz)
    second = keep * jnp.sqrt(norm + EPS) - take * next_ritz
    squares = []
    for i in range(2):
        on_first = first + second * along[i] + take * on_vec[i]
        on_second = second + take * on_new[i]
        square = on_first * on_first * vec_vec[i] + on_second * on_second * new_new[i]
        squares.append(square + take * take * rest[i])
    next_norm = add(squares) / ENTRIES
    scale = 1.0 / jnp.sqrt(next_norm + EPS)
    new_scalars[...] = pack([next_ritz, next_norm, lowest])
    for position in range(WINDOW):
        turned = held_block(cores, position)
        mixed_vec = keep * vector[position] + take * direction[position]
        mixed_image = keep * image[position] + take * turned
        value = (mixed_image - next_ritz * mixed_vec) * scale
        vec_half[position] = value.astype(bf16)

        @pl.when((position // 4) == (wf & 1))
        def _():
            new_vector[position % 4] = mixed_vec
            new_direction[position % 4] = value

    value = jnp.zeros((1, 1), f32)
    for i in range(OWN):
        half = half_step(shift, mask, left, right, vec_half, back, OWN * wf + i, i)
        value = value + total(half * new_direction[i])
    out[...] = jnp.broadcast_to(2.0 * value, out.shape)


def last_kernel(parts, vector, direction, scalars, out, energies):
    curvature = total(parts[:, 0:1]) / ENTRIES
    ritz, norm, first_lowest = lanes(scalars[0:1], 3)
    lowest, keep, take = mixing(ritz, curvature, norm)
    for i in range(OWN):
        out[i] = keep * vector[i] + take * direction[i]
    energies[0] = first_lowest[0, 0]
    energies[1] = lowest[0, 0]


HBM = pl.BlockSpec(memory_space=pltpu.HBM)
VMEM = pl.BlockSpec(memory_space=pltpu.VMEM)
SMEM = pl.BlockSpec(memory_space=pltpu.SMEM)
MIB = 1 << 20


def struct(*shape, dtype=f32):
    return jax.ShapeDtypeStruct(shape, dtype)


def call(kernel, name, outs, in_specs, args, out_specs=None, scratch=(), limit=6):
    return pl.pallas_call(
        kernel,
        name=name,
        in_specs=in_specs,
        out_specs=out_specs or [VMEM] * len(outs),
        out_shape=outs,
        scratch_shapes=scratch,
        compiler_params=pltpu.CompilerParams(vmem_limit_bytes=int(limit * MIB)),
    )(*args)


def small(kernel, name, outs, *arrays, out_specs=None):
    return call(kernel, name, outs, [VMEM] * len(arrays), arrays, out_specs)


def step(kernel, name, outs, operators, arrays, sums=True):
    scratch = [
        pltpu.VMEM((WINDOW, BLOCK, BLOCK), bf16),
        pltpu.VMEM((2, BLOCK, PAIRS * BLOCK), bf16),
    ]
    if sums:
        scratch.append(pltpu.VMEM((WINDOW, BLOCK, BLOCK), f32))
    args = (*operators, *arrays)
    in_specs = [SMEM] * 2 + [VMEM] * (len(args) - 2)
    return call(kernel, name, outs, in_specs, args, scratch=scratch, limit=16)


def device(y, z, core, wf):
    return ((y * 8 + z) * 2 + core) * 4 + wf


LINE_GROUPS = [
    [device(rows[half], z, core, wf) for half, z in line_order(core)]
    for rows in LINE_ROWS
    for core in range(2)
    for wf in range(4)
]
CROSS_GROUPS = [
    [device(y, z, core, wf) for y in rows for wf in range(4)]
    for rows in CROSS_ROWS
    for z in range(8)
    for core in range(2)
]


def exchange(value, groups=None):
    return lax.all_to_all(value, ALL_AXES, 0, 0, axis_index_groups=groups, tiled=True)


def shards(guess, left_ops, right_ops, op_shift, op_mask, left_dims, right_dims):
    blocks = struct(WINDOW, BLOCK, BLOCK)
    half = struct(LINE, CHUNK, BLOCK)
    sent = struct(LINE, CHUNK, BLOCK, dtype=bf16)
    own_blocks = struct(OWN, BLOCK, BLOCK)
    pair = struct(2, CHUNK, BLOCK)
    scalar_row = struct(EXTRA, BLOCK)
    packet = struct(LINE * PACKET, BLOCK)

    def partner(value, distance):
        return lax.ppermute(value, "wf", [(i, i ^ distance) for i in range(4)])

    def swapped(value):
        return lax.ppermute(value, "c", [(0, 1), (1, 0)])

    tail = EXTRA + CHUNK
    masks, sent_one, sent_two, sent_three = call(
        norm_kernel, "norm",
        [pair, struct(SIDE + tail, BLOCK), struct(tail, BLOCK), struct(SIDE + tail, BLOCK)],
        [SMEM, SMEM, VMEM], (left_dims, right_dims, guess),
        scratch=[pltpu.VMEM((OWN, BLOCK, BLOCK), f32)], limit=60,
    )
    three, one, two = partner(sent_three, 3), partner(sent_one, 1), partner(sent_two, 2)
    held = struct(OWN, PAIRS, BLOCK, BLOCK, dtype=bf16)
    left, right = call(
        load_kernel, "load", [held, held], [HBM, HBM], (left_ops, right_ops),
        scratch=[pltpu.SemaphoreType.DMA((2 * OWN,))], limit=49,
    )
    operators = (op_shift, op_mask.T, left, right)

    def reduced(keep, give):
        (summed,) = small(join_kernel, "join", [sent], keep, swapped(give))
        parts = exchange(summed, LINE_GROUPS)
        (tiled,) = small(spread_kernel, "spread", [struct(CROSS, CHUNK, BLOCK)], parts)
        return exchange(tiled, CROSS_GROUPS)

    def gathered(packets):
        packets = exchange(packets.reshape(-1, 1, BLOCK), LINE_GROUPS).reshape(-1, BLOCK)
        return packets, swapped(packets)

    keep, give, vector, pieces = step(
        first_kernel, "first", [half, half, blocks, pair], operators,
        (sent_one, sent_three, one, two, three),
    )
    packets, image_pieces = small(
        image_kernel, "image", [packet, pair], reduced(keep, give), masks, pieces
    )
    keep, give, direction, image, scalars = step(
        second_kernel, "second", [half, half, blocks, blocks, scalar_row], operators,
        (*gathered(packets), vector),
    )
    (packets,) = small(
        turned_kernel, "turned", [packet], reduced(keep, give), masks, pieces, image_pieces, scalars
    )
    sums, vector, direction, scalars = step(
        third_kernel, "third", [struct(256, BLOCK), own_blocks, own_blocks, scalar_row], operators,
        (*gathered(packets), vector, direction, image, scalars), sums=False,
    )
    sums = exchange(sums)
    result, energies = small(
        last_kernel, "last", [own_blocks, struct(2)], sums, vector, direction, scalars,
        out_specs=[VMEM, SMEM],
    )
    return result, energies


def solution(mesh):
    split = Mesh(mesh.devices.reshape(4, 8, 2, 4), (*OP_AXES, "wf"))
    in_specs = (
        P("wf", None, None),
        P(OP_AXES, "wf", None, None),
        P(OP_AXES, "wf", None, None),
        P(OP_AXES),
        P(OP_AXES, "wf"),
        P(),
        P(),
    )
    out_specs = (P("wf", None, None), P())
    return jax.shard_map(
        shards, mesh=split, in_specs=in_specs, out_specs=out_specs, check_vma=False
    )
```
